32 devices in a mesh: dp: 4 (over y, x), ctx: 4 (over z), tp: 2 (over core).
Axes of the slice: x: 2, y: 2, z: 4, core: 2. Of those that a mesh axis runs over, the one named last changes fastest.
Arguments:
- hidden_in: bfloat16 [8, 1024, 1024], P('dp', 'ctx'), may hold values from -6 to 6
- positions: int32 [8, 1024], P('dp', 'ctx'), may hold values from 0 to 1023, as said below
- gain_attn: bfloat16 [1024], P(('dp', 'ctx')), may hold values from 0.25 to 1.75
- w_qkv: bfloat16 [1024, 2, 384], P(('dp', 'ctx'), 'tp'), may hold values from -0.1875 to 0.1875
- w_attn_out: bfloat16 [512, 1024], P('tp', ('dp', 'ctx')), may hold values from -1.5 to 1.5
- w_zx: bfloat16 [1024, 2, 1536], P(('dp', 'ctx'), None, 'tp'), may hold values from -0.1875 to 0.1875
- w_bc: bfloat16 [1024, 256], P(('dp', 'ctx')), may hold values from -0.1875 to 0.1875
- w_dt: bfloat16 [1024, 24], P(('dp', 'ctx'), 'tp'), may hold values from -0.046875 to 0.046875
- conv_x: bfloat16 [4, 1536], P(None, 'tp'), may hold values from -3 to 3
- conv_bc: bfloat16 [4, 256], replicated, may hold values from -3 to 3
- a_log: float32 [24], P('tp'), may hold values from -1 to 3
- dt_bias: float32 [24], P('tp'), may hold values from -6 to -3
- d_skip: float32 [24], P('tp'), may hold values from 0.5 to 1.5
- w_mamba_out: bfloat16 [1536, 1024], P('tp', ('dp', 'ctx')), may hold values from -0.15625 to 0.15625
- gain_ffn: bfloat16 [1024], P(('dp', 'ctx')), may hold values from 0.25 to 1.75
- w_gu: bfloat16 [1024, 2, 2048], P(('dp', 'ctx'), None, 'tp'), may hold values from -0.1875 to 0.1875
- w_down: bfloat16 [2048, 1024], P('tp', ('dp', 'ctx')), may hold values from -0.125 to 0.125
- output_cotangent: bfloat16 [8, 1024, 1024], P('dp', 'ctx'), may hold values from -6 to 6
Outputs:
- block_out: bfloat16 [8, 1024, 1024], P('dp', 'ctx')
- d_hidden: bfloat16 [8, 1024, 1024], P('dp', 'ctx')
- grad_gain_attn: float32 [1024], P(('dp', 'ctx'))
- grad_w_qkv: float32 [1024, 2, 384], P(('dp', 'ctx'), 'tp')
- grad_w_attn_out: float32 [512, 1024], P('tp', ('dp', 'ctx'))
- grad_w_zx: float32 [1024, 2, 1536], P(('dp', 'ctx'), None, 'tp')
- grad_w_bc: float32 [1024, 256], P(('dp', 'ctx'))
- grad_w_dt: float32 [1024, 24], P(('dp', 'ctx'), 'tp')
- grad_conv_x: float32 [4, 1536], P(None, 'tp')
- grad_conv_bc: float32 [4, 256], replicated
- grad_a_log: float32 [24], P('tp')
- grad_dt_bias: float32 [24], P('tp')
- grad_d_skip: float32 [24], P('tp')
- grad_w_mamba_out: float32 [1536, 1024], P('tp', ('dp', 'ctx'))
- grad_gain_ffn: float32 [1024], P(('dp', 'ctx'))
- grad_w_gu: float32 [1024, 2, 2048], P(('dp', 'ctx'), None, 'tp')
- grad_w_down: float32 [2048, 1024], P('tp', ('dp', 'ctx'))
The draws below stay inside these ranges and needn't reach their ends.
Inputs may be any that keep to these rules, and one draw needn't show every extreme that they name: Each row of 1024 tokens is packed with documents: a position of 0 starts a document and positions then rise by one. Every document but the last of a row has 60 to 800 tokens. Of the 2 rows of each index of dp, one row drawn from the seed is a single document.
All inputs are finite; a program needn't handle non-finite values.
Results may differ from the reference program's by a relative error of at most 0.02.
Values may be sent and summed in bfloat16 or wider, within the bound.
No kernel may reach another device: no remote copies, remote signals or barrier semaphores. Data moves between devices by JAX's collectives and lax.ppermute only.
A program may use at most 192 MiB of HBM per device.

```python
import math
import jax
import jax.numpy as jnp
from jax import lax

D = 1024
HD = 64
QH = 8
KVH = 2
MH = 24
NS = 128
FF = 2048
KC = 4
DOC_MIN = 60
DOC_MAX = 800
LENGTH = 1024
BLK = 256
SEQS = 2
BATCH = 8
MI = 1536


def draw_positions(key, part):
    key = jax.random.fold_in(key, 11)
    first_key, second_key = jax.random.split(key)
    count = LENGTH // DOC_MIN + 1
    sizes_drawn = jax.random.randint(first_key, (BATCH, count), DOC_MIN, DOC_MAX + 1)
    ends = jnp.cumsum(sizes_drawn, axis=1)
    starts = ends - sizes_drawn
    index = jnp.arange(LENGTH)
    inside = starts[:, None, :] <= index[None, :, None]
    begin = jnp.max(jnp.where(inside, starts[:, None, :], 0), axis=2)
    packed = index[None, :] - begin
    groups = BATCH // SEQS
    whole = jax.random.randint(second_key, (groups,), 0, SEQS)
    rows = jnp.arange(BATCH)
    chosen = rows % SEQS == whole[rows // SEQS]
    return jnp.where(chosen[:, None], index[None, :], packed).astype(jnp.int32)


def steps_of(stream_key, shape, cuts, low, largest):
    loudness, own = 1.0, jax.random.fold_in(stream_key, 6)
    for dim, blocks in cuts:
        heights = jnp.exp(jax.random.uniform(jax.random.fold_in(own, dim), (blocks,), jnp.float32, low / len(cuts), largest / len(cuts)))
        loudness = loudness * jnp.repeat(heights, shape[dim] // blocks).reshape([-1 if axis == dim else 1 for axis in range(len(shape))])
    return loudness


def noise(key, extent, scale, reach, cuts=(), kind=jnp.bfloat16):
    level = steps_of(key, extent, cuts, -0.22, 0.18) if cuts else 1.0
    entries = jax.random.normal(key, extent, jnp.float32) * scale * level
    return jnp.minimum(jnp.maximum(entries, -reach), reach).astype(kind)


def setup_inputs(seed: int = 0) -> dict:
    streams_of = jax.random.split(jax.random.key(seed), 19)
    hidden_in = noise(streams_of[0], (BATCH, LENGTH, D), 1.0, 6.0, ((0, 4), (1, 4)))
    positions = draw_positions(jax.random.fold_in(streams_of[18], 71), 0)
    gain_attn = jnp.clip(1.0 + 0.15 * jax.random.normal(streams_of[2], (D,), jnp.float32), 0.25, 1.75).astype(jnp.bfloat16)
    w_qkv = noise(streams_of[3], (D, KVH, (QH // KVH + 2) * HD), D ** -0.5, 0.1875, ((0, 16), (1, 2)))
    w_attn_out = noise(streams_of[4], (QH * HD, D), (QH * HD // 32) ** -0.5, 1.5, ((0, 2), (1, 16)))
    w_zx = noise(streams_of[5], (D, 2, MI), D ** -0.5, 0.1875, ((0, 16), (2, 2)))
    w_bc = noise(streams_of[6], (D, 2 * NS), D ** -0.5, 0.1875, ((0, 16),))
    w_dt = noise(streams_of[7], (D, MH), (16 * D) ** -0.5, 0.046875, ((0, 16), (1, 2)))
    conv_x = noise(streams_of[8], (KC, MI), KC ** -0.5, 3.0, ((1, 2),))
    conv_bc = noise(streams_of[9], (KC, 2 * NS), KC ** -0.5, 3.0)
    a_log = jnp.clip(-1.0 + 4.0 * jax.random.uniform(streams_of[10], (MH,), jnp.float32) ** steps_of(streams_of[10], (MH,), ((0, 2),), -0.2, 0.2), -1.0, 3.0)
    dt_bias = jnp.clip(-6.0 + 3.0 * jax.random.uniform(streams_of[11], (MH,), jnp.float32) ** steps_of(streams_of[11], (MH,), ((0, 2),), -0.2, 0.2), -6.0, -3.0)
    d_skip = jnp.clip(0.5 + 1.0 * jax.random.uniform(streams_of[12], (MH,), jnp.float32) ** steps_of(streams_of[12], (MH,), ((0, 2),), -0.2, 0.2), 0.5, 1.5)
    w_mamba_out = noise(streams_of[13], (MI, D), MI ** -0.5, 0.15625, ((0, 2), (1, 16)))
    gain_ffn = jnp.clip(1.0 + 0.15 * jax.random.normal(streams_of[14], (D,), jnp.float32), 0.25, 1.75).astype(jnp.bfloat16)
    w_gu = noise(streams_of[15], (D, 2, FF), D ** -0.5, 0.1875, ((0, 16), (2, 2)))
    w_down = noise(streams_of[16], (FF, D), FF ** -0.5, 0.125, ((0, 2), (1, 16)))
    output_cotangent = noise(streams_of[17], (BATCH, LENGTH, D), 1.0, 6.0, ((0, 4), (1, 4)))
    return dict(hidden_in=hidden_in, positions=positions, gain_attn=gain_attn, w_qkv=w_qkv, w_attn_out=w_attn_out, w_zx=w_zx, w_bc=w_bc, w_dt=w_dt, conv_x=conv_x, conv_bc=conv_bc, a_log=a_log, dt_bias=dt_bias, d_skip=d_skip, w_mamba_out=w_mamba_out, gain_ffn=gain_ffn, w_gu=w_gu, w_down=w_down, output_cotangent=output_cotangent)


highest = lax.Precision.HIGHEST
rope_base = 100000000000.0

@jax.custom_vjp
def low(v):
    return lax.optimization_barrier(v.astype(jnp.bfloat16)).astype(jnp.float32)

@jax.custom_vjp
def low_back(v):
    return v

def low_keep(v):
    return (low(v), None)

def low_pass(kept, grad):
    return (grad,)

def back_keep(v):
    return (v, None)

def back_low(kept, grad):
    return (low(grad),)
low.defvjp(low_keep, low_pass)
low_back.defvjp(back_keep, back_low)

def normed(values, gain):
    return values * lax.rsqrt(lax.optimization_barrier(jnp.mean(values * values, axis=-1, keepdims=True)) + 1e-05) * gain

def matmul(left, right):
    return jnp.einsum('...i,ij->...j', left, right, precision=highest)

def angles(pos, width):
    frequency = jnp.power(jnp.float32(rope_base), -jnp.arange(0, width, 2).astype(jnp.float32) / width)
    turned = pos.astype(jnp.float32)[..., None] * frequency
    return (jnp.cos(turned), jnp.sin(turned))

def rotate(values, cosine, sine):
    half = values.shape[-1] // 2
    first, second = (values[..., :half], values[..., half:])
    return jnp.concatenate([first * cosine - second * sine, second * cosine + first * sine], axis=-1)

def conv_silu(values, tail, weights, pos):
    span = weights.shape[0]
    count = values.shape[1]
    joined = jnp.concatenate([tail, values], axis=1)
    total = jnp.zeros_like(values)
    for shift_by in range(span):
        piece = joined[:, span - 1 - shift_by:span - 1 - shift_by + count, :]
        total = total + weights[shift_by] * piece * (pos >= shift_by).astype(jnp.float32)[:, :, None]
    return jax.nn.silu(total)

def decay_sums(log_decay, pos):
    marks = jnp.cumsum((pos == 0).astype(jnp.int32), axis=1)
    return (jnp.cumsum(log_decay, axis=1), marks)

def stretch_end(inflow, b_vec, log_decay, pos):
    cumulated, marks = decay_sums(log_decay, pos)
    last = cumulated[:, -1, :]
    same = (marks == marks[:, -1:]).astype(jnp.float32)
    weight = jnp.exp(last[:, None, :] - cumulated) * same[:, :, None]
    ends = jnp.einsum('sthp,stn->shpn', weight[..., None] * inflow, b_vec, precision=highest)
    carry = jnp.exp(last) * (marks[:, -1] == 0).astype(jnp.float32)[:, None]
    return (ends, carry)

def stretch_inner(heads_x, inflow, b_vec, c_vec, log_decay, pos, d_skip):
    cumulated, marks = decay_sums(log_decay, pos)
    count = log_decay.shape[1]
    order = jnp.arange(count)
    valid = (order[:, None] >= order[None, :])[None] & (marks[:, :, None] == marks[:, None, :])
    differ = cumulated[:, :, None, :] - cumulated[:, None, :, :]
    mixing = jnp.exp(jnp.where(valid[..., None], differ, -1e+30))
    scores = jnp.einsum('stn,srn->str', c_vec, b_vec, precision=highest)
    result = jnp.einsum('strh,srhp->sthp', mixing * scores[..., None], inflow, precision=highest)
    return result + d_skip[None, None, :, None] * heads_x

def stretch_read(c_vec, log_decay, pos, state):
    cumulated, marks = decay_sums(log_decay, pos)
    weight = jnp.exp(cumulated) * (marks == 0).astype(jnp.float32)[:, :, None]
    readout = jnp.einsum('stn,shpn->sthp', c_vec, state, precision=highest)
    return weight[..., None] * readout

def mamba_inputs(gate_input_rows, bc, dtr, tail_x, tail_bc, conv_x, conv_bc, a_log, dt_bias, pos):
    heads = a_log.shape[0]
    gate = gate_input_rows[:, :, 0, :]
    convolved = conv_silu(gate_input_rows[:, :, 1, :], tail_x, conv_x, pos)
    bc_conv = conv_silu(bc, tail_bc, conv_bc, pos)
    states = bc_conv.shape[2] // 2
    b_vec, c_vec = (bc_conv[..., :states], bc_conv[..., states:])
    step_size = jax.nn.softplus(dtr + dt_bias)
    log_decay = -jnp.exp(a_log) * step_size
    heads_x = convolved.reshape(convolved.shape[0], convolved.shape[1], heads, -1)
    inflow = heads_x * step_size[..., None]
    return (gate, heads_x, inflow, b_vec, c_vec, log_decay)

def mamba_sequence(gate_input_rows, bc, dtr, conv_x, conv_bc, a_log, dt_bias, d_skip, pos):
    groups, length = pos.shape
    span = conv_x.shape[0] - 1
    tail_x = jnp.zeros((groups, span, gate_input_rows.shape[3]), jnp.float32)
    tail_bc = jnp.zeros((groups, span, bc.shape[2]), jnp.float32)
    gate, heads_x, inflow, b_vec, c_vec, log_decay = mamba_inputs(gate_input_rows, bc, dtr, tail_x, tail_bc, conv_x, conv_bc, a_log, dt_bias, pos)
    count = length // BLK

    def split(values):
        shaped = values.reshape((groups, count, BLK) + values.shape[2:])
        return jnp.moveaxis(shaped, 1, 0)

    def advance(state, pieces):
        part_x, part_flow, part_b, part_c, part_decay, part_pos = pieces
        result = stretch_inner(part_x, part_flow, part_b, part_c, part_decay, part_pos, d_skip)
        result = result + stretch_read(part_c, part_decay, part_pos, state)
        ends, carry = stretch_end(part_flow, part_b, part_decay, part_pos)
        return (carry[:, :, None, None] * state + ends, result)
    start = jnp.zeros((groups, a_log.shape[0], heads_x.shape[3], b_vec.shape[2]), jnp.float32)
    pieces = (split(heads_x), split(inflow), split(b_vec), split(c_vec), split(log_decay), split(pos))
    _, results = lax.scan(jax.checkpoint(advance), start, pieces)
    mixed = jnp.moveaxis(results, 0, 1).reshape(groups, length, -1)
    return mixed * jax.nn.silu(gate)

def attention(qkv, pos, per_group):
    groups, length = pos.shape
    kv_heads = qkv.shape[2]
    queries = qkv[..., :per_group * HD].reshape(groups, length, kv_heads, per_group, HD)
    keys = qkv[..., per_group * HD:(per_group + 1) * HD]
    values = qkv[..., (per_group + 1) * HD:]
    cosine, sine = angles(pos, HD)
    q_rot = low(rotate(queries, cosine[:, :, None, None, :], sine[:, :, None, None, :]))
    k_rot = low(rotate(keys, cosine[:, :, None, :], sine[:, :, None, :]))
    v_low = low(values)
    begins = jnp.arange(length)[None, :] - pos
    rows = math.gcd(512, length)
    key_index = jnp.arange(length)

    def one_block(number):
        q_part = lax.dynamic_slice_in_dim(q_rot, number * rows, rows, 1)
        b_part = lax.dynamic_slice_in_dim(begins, number * rows, rows, 1)
        q_index = number * rows + jnp.arange(rows)
        scores = low_back(jnp.einsum('gqcrd,gkcd->gcrqk', q_part, k_rot, precision=highest) * 0.125)
        valid = (key_index[None, None, :] <= q_index[None, :, None]) & (b_part[:, :, None] == begins[:, None, :])
        scores = jnp.where(valid[:, None, None], scores, -1e+30)
        top = lax.optimization_barrier(jnp.max(scores, axis=-1, keepdims=True))
        expd = jnp.exp(scores - top)
        probs = low(expd / lax.optimization_barrier(jnp.sum(expd, axis=-1, keepdims=True)))
        return jnp.einsum('gcrqk,gkcd->gqcrd', probs, v_low, precision=highest)
    outs = lax.map(jax.checkpoint(one_block), jnp.arange(length // rows))
    outs = jnp.moveaxis(outs, 0, 1)
    return outs.reshape(groups, length, kv_heads * per_group * HD)

def layer(x, pos, gain_attn, w_qkv, w_attn_out, w_zx, w_bc, w_dt, conv_x, conv_bc, a_log, dt_bias, d_skip, w_mamba_out, gain_ffn, w_gu, w_down):
    h1 = low(normed(x, gain_attn))
    qkv = low_back(jnp.einsum('gld,dce->glce', h1, w_qkv, precision=highest))
    per_group = w_qkv.shape[2] // HD - 2
    attended = attention(qkv, pos, per_group)
    att = matmul(low(low_back(attended)), w_attn_out)
    gate_input_rows = low_back(jnp.einsum('gld,dkm->glkm', h1, w_zx, precision=highest))
    bc = low_back(matmul(h1, w_bc))
    dtr = low_back(matmul(h1, w_dt))
    gated = mamba_sequence(gate_input_rows, bc, dtr, conv_x, conv_bc, a_log, dt_bias, d_skip, pos)
    mam = matmul(low(gated), w_mamba_out)
    mix = low_back(att + mam)
    resid = x + mix
    h2 = low(normed(resid, gain_ffn))
    gate_up_rows = low_back(jnp.einsum('gld,dkf->glkf', h2, w_gu, precision=highest))
    hid = low(jax.nn.silu(gate_up_rows[:, :, 0]) * gate_up_rows[:, :, 1])
    return resid + matmul(hid, w_down)

def reference(hidden_in, positions, gain_attn, w_qkv, w_attn_out, w_zx, w_bc, w_dt, conv_x, conv_bc, a_log, dt_bias, d_skip, w_mamba_out, gain_ffn, w_gu, w_down, output_cotangent):
    params = tuple((a.astype(jnp.float32) for a in (gain_attn, w_qkv, w_attn_out, w_zx, w_bc, w_dt, conv_x, conv_bc, a_log, dt_bias, d_skip, w_mamba_out, gain_ffn, w_gu, w_down)))
    group = math.gcd(BATCH, max(1, 4096 // LENGTH))
    count = BATCH // group

    def shaped(values):
        return values.reshape((count, group) + values.shape[1:])

    def advance(totals, pieces):
        x_part, pos_part, cot_part = pieces

        def forward(x_value, *weights):
            return layer(x_value, pos_part, *weights)
        result, pull = jax.vjp(forward, x_part, *params)
        grads = pull(cot_part)
        summed = tuple((t + g for t, g in zip(totals, grads[1:])))
        return (summed, (result, grads[0]))
    zero = tuple((jnp.zeros_like(p) for p in params))
    pieces = (shaped(hidden_in.astype(jnp.float32)), shaped(positions), shaped(output_cotangent.astype(jnp.float32)))
    totals, (results, input_grads) = lax.scan(advance, zero, pieces)
    block_out = results.reshape(hidden_in.shape).astype(jnp.bfloat16)
    d_hidden = input_grads.reshape(hidden_in.shape).astype(jnp.bfloat16)
    g_one, g_two, g_three, g_four, g_five, g_six, g_seven, g_eight, g_nine, g_ten, g_eleven, g_twelve, g_thirteen, g_fourteen, g_fifteen = totals
    return (block_out, d_hidden, g_one, g_two, g_three, g_four, g_five, g_six, g_seven, g_eight, g_nine, g_ten, g_eleven, g_twelve, g_thirteen, g_fourteen, g_fifteen)
```

```python
import functools

import jax
import jax.numpy as jnp
from jax import lax
from jax.experimental import pallas as pl
from jax.experimental.pallas import tpu as pltpu
from jax.sharding import PartitionSpec as P

HD = 64
KC = 4
TAIL = 8
LANES = 128
VMEM_LIMIT = 56 * 1024 * 1024

f32 = jnp.float32
bf16 = jnp.bfloat16
highest = lax.Precision.HIGHEST
rope_base = 100000000000.0


def small_mesh():
    return lax.axis_size("dp") == 4 and lax.axis_size("ctx") == 4


def swap(value, axis, bits):
    count = lax.axis_size(axis)
    return lax.ppermute(value, axis, [(i, i ^ bits) for i in range(count)])


def shifted(value, axis, distance):
    count = lax.axis_size(axis)
    route = [(i - distance, i) for i in range(count) if 0 <= i - distance < count]
    return lax.ppermute(value, axis, route)


def assemble(me, pieces, outs, copies):
    count = len(pieces)
    total = len(outs)

    def kernel(me_ref, *refs):
        ins = refs[:count]
        outputs = refs[count : count + total]
        sems = refs[count + total]
        place = me_ref[0]
        running = []
        for number, (piece, first, width, out, bits) in enumerate(copies):
            copy = pltpu.make_async_copy(
                ins[piece].at[:, pl.ds(first, width)],
                outputs[out].at[jnp.bitwise_xor(place, bits)],
                sems.at[number],
            )
            copy.start()
            running.append(copy)
        for copy in running:
            copy.wait()

    return pl.pallas_call(
        kernel,
        out_shape=[jax.ShapeDtypeStruct(shape, pieces[0].dtype) for shape in outs],
        in_specs=[pl.BlockSpec(memory_space=pltpu.SMEM)]
        + [pl.BlockSpec(memory_space=pl.ANY)] * count,
        out_specs=[pl.BlockSpec(memory_space=pltpu.VMEM)] * total,
        scratch_shapes=[pltpu.SemaphoreType.DMA((len(copies),))],
        compiler_params=pltpu.CompilerParams(vmem_limit_bytes=VMEM_LIMIT),
        name="assemble",
    )(me.reshape(1), *pieces)


def gather_rows(packed, widths):
    rows = packed.shape[0]
    if not small_mesh():
        whole = lax.all_gather(packed, ("dp", "ctx"), axis=0, tiled=True)
        outs, first = [], 0
        for width in widths:
            outs.append(whole[:, first : first + width])
            first += width
        return outs
    dp, ctx = lax.axis_index("dp"), lax.axis_index("ctx")
    along = [packed] + [swap(packed, "ctx", k) for k in (1, 2, 3)]
    copies, first = [], 0
    for number, width in enumerate(widths):
        copies += [(k, first, width, number, k) for k in range(4)]
        first += width
    held = assemble(ctx, along, [(4, rows, width) for width in widths], copies)
    held = [h.reshape(4 * rows, h.shape[2]) for h in held]
    pieces, copies = [], []
    if len(held) == 1:
        for k in range(4):
            pieces.append(held[0] if k == 0 else swap(held[0], "dp", k))
            copies.append((k, 0, widths[0], 0, k))
    else:
        for number, (one, two) in enumerate(((1, 2), (2, 1))):
            mine = held[number]
            near = swap(mine, "dp", one)
            for bits, piece in (
                (0, mine),
                (one, near),
                (two, swap(mine, "dp", two)),
                (3, swap(near, "dp", two)),
            ):
                copies.append((len(pieces), 0, widths[number], number, bits))
                pieces.append(piece)
    full = assemble(dp, pieces, [(4, 4 * rows, width) for width in widths], copies)
    return [w.reshape(16 * rows, w.shape[2]) for w in full]


def pick(value, index, axis):
    return lax.dynamic_index_in_dim(value, index, axis, keepdims=False)


def scatter_rows(grads):
    if not small_mesh():
        joined = jnp.concatenate(grads, axis=1) if len(grads) > 1 else grads[0]
        return lax.psum_scatter(
            joined, ("dp", "ctx"), scatter_dimension=0, tiled=True
        ).astype(f32)
    dp, ctx = lax.axis_index("dp"), lax.axis_index("ctx")
    y, x = dp // 2, dp % 2
    rows = grads[0].shape[0]
    if len(grads) == 1:
        blocks = grads[0].reshape(4, rows // 4, -1)
        total = pick(blocks, dp, 0).astype(f32)
        for k in (1, 2, 3):
            total = total + swap(pick(blocks, dp ^ k, 0), "dp", k).astype(f32)
        held = total.astype(bf16)
    else:
        parts = []
        for number, grad in enumerate(grads):
            blocks = grad.reshape(2, 2, rows // 4, -1)
            one, two = (2, 1) if number == 0 else (1, 2)
            axis = 0 if number == 0 else 1
            at, then = (y, x) if number == 0 else (x, y)
            got = swap(pick(blocks, 1 - at, axis), "dp", one)
            kept = pick(blocks, at, axis)
            send = (pick(kept, 1 - then, 0).astype(f32) + pick(got, 1 - then, 0).astype(f32)).astype(
                bf16
            )
            near = swap(send, "dp", two)
            parts.append(
                (
                    pick(kept, then, 0).astype(f32)
                    + pick(got, then, 0).astype(f32)
                    + near.astype(f32)
                ).astype(bf16)
            )
        held = jnp.concatenate(parts, axis=1)
    blocks = held.reshape(4, rows // 16, -1)
    total = pick(blocks, ctx, 0).astype(f32)
    for k in (1, 2, 3):
        total = total + swap(pick(blocks, ctx ^ k, 0), "ctx", k).astype(f32)
    return total


def sum_all(value, axes):
    for axis in axes:
        count = lax.axis_size(axis)
        if count & (count - 1):
            value = lax.psum(value, axis)
            continue
        bits = 1
        while bits < count:
            value = value + swap(value, axis, bits)
            bits *= 2
    return value


def pair_sum(value):
    if lax.axis_size("tp") != 2:
        return lax.psum(value.astype(bf16), "tp").astype(f32)
    low = value.astype(bf16)
    return low.astype(f32) + swap(low, "tp", 1).astype(f32)


def behind(value):
    count, me = lax.axis_size("ctx"), lax.axis_index("ctx")
    if count <= 4:
        return [value] + [shifted(value, "ctx", d) for d in range(1, count)]
    everything = lax.all_gather(value, "ctx")
    out = [value]
    for d in range(1, count):
        there = pick(everything, lax.rem(me - d + count, count), 0)
        out.append(jnp.where(me >= d, there, jnp.zeros_like(there)))
    return out


def chained(carry, ends, reverse):
    count, me = lax.axis_size("ctx"), lax.axis_index("ctx")
    low = ends.astype(bf16)
    if count <= 4:
        sign = -1 if reverse else 1
        total, factor = None, None
        for d in range(1, count):
            piece = shifted(low, "ctx", sign * d).astype(f32)
            if factor is None:
                total = piece
                factor = jnp.ones_like(carry[0])
            else:
                total = total + factor[:, None, :] * piece
            there = me - sign * d
            factor = factor * pick(carry, jnp.clip(there, 0, count - 1), 0)
        return total
    everything = lax.all_gather(low, "ctx")

    def hop(k, before):
        at = count - 1 - k if reverse else k
        reached = at > me if reverse else at < me
        new = pick(carry, at, 0)[:, None, :] * before + pick(everything, at, 0).astype(f32)
        return jnp.where(reached, new, before)

    return lax.fori_loop(0, count, hop, jnp.zeros(ends.shape, f32))


def dot(a, b):
    return jnp.dot(a, b, preferred_element_type=f32)


def dot_nt(a, b):
    return lax.dot_general(a, b, (((1,), (1,)), ((), ())), preferred_element_type=f32)


def sig(v):
    return 1.0 / (1.0 + jnp.exp(-v))


def conv_pre(joined, span, taps, pos, count):
    total = None
    for k in range(KC):
        piece = joined[TAIL - k : TAIL - k + count, span]
        term = taps[k : k + 1, :] * piece
        if k:
            term = term * (pos >= k).astype(f32)
        total = term if total is None else total + term
    return total


def lane_ids(shape):
    return lax.broadcasted_iota(jnp.int32, shape, 1)


def decay_parts(dtr, head_row, pos, heads):
    count = dtr.shape[0]
    lane = lane_ids(dtr.shape)
    pre = dtr + head_row[1:2, :]
    dt = jnp.where(lane < heads, jnp.maximum(pre, 0.0) + jnp.log(1.0 + jnp.exp(-jnp.abs(pre))), 0.0)
    la = -jnp.exp(head_row[0:1, :]) * dt
    marked = jnp.where(lane == LANES - 1, (pos == 0).astype(f32), la)
    row = lax.broadcasted_iota(jnp.int32, (count, count), 0)
    col = lax.broadcasted_iota(jnp.int32, (count, count), 1)
    lower = (row >= col).astype(f32)
    summed = jnp.dot(lower, marked, precision=highest, preferred_element_type=f32)
    return pre, dt, la, summed


def wide(value, lane):
    return jnp.broadcast_to(value[:, lane : lane + 1], (value.shape[0], LANES))


def pair(value, j, low_half):
    return jnp.where(low_half, wide(value, 2 * j), wide(value, 2 * j + 1))


def mixer_local_kernel(
    heads, xr_ref, xt_ref, bc_ref, bt_ref, dtr_ref, tx_ref, tb_ref, hr_ref, pos_ref,
    y_ref, e_ref, c_ref, l_ref, jx, jb,
):
    count = xr_ref.shape[1]
    pos = pos_ref[0]
    head_row = hr_ref[...]
    jx[0:TAIL, :] = xt_ref[0]
    jx[TAIL : TAIL + count, :] = xr_ref[0]
    jb[0:TAIL, :] = bt_ref[0]
    jb[TAIL : TAIL + count, :] = bc_ref[0]
    pre_b = conv_pre(jb, slice(0, 2 * LANES), tb_ref[...], pos, count)
    bc = pre_b * sig(pre_b)
    b_low = bc[:, :LANES].astype(bf16)
    c_low = bc[:, LANES:].astype(bf16)
    c_ref[0] = c_low
    bt_low = jnp.transpose(bc[:, :LANES]).astype(bf16)
    _, dt, _, summed = decay_parts(dtr_ref[0], head_row, pos, heads)
    l_ref[0] = summed
    rows = jnp.transpose(summed)
    row = lax.broadcasted_iota(jnp.int32, (count, count), 0)
    col = lax.broadcasted_iota(jnp.int32, (count, count), 1)
    marks = summed[:, LANES - 1 : LANES]
    valid = (row >= col) & (marks == rows[LANES - 1 : LANES, :])
    scores = dot_nt(c_low, b_low)
    last = summed[count - 1 : count, :]
    same = (marks == last[:, LANES - 1 : LANES]).astype(f32)
    low_half = lane_ids((count, LANES)) < HD
    for j in range(heads // 2):
        span = slice(j * LANES, (j + 1) * LANES)
        pre = conv_pre(jx, span, tx_ref[:, span], pos, count)
        xc = pre * sig(pre)
        u = xc * pair(dt, j, low_half)
        u_low = u.astype(bf16)
        results = []
        for h in (2 * j, 2 * j + 1):
            differ = summed[:, h : h + 1] - rows[h : h + 1, :]
            mixing = jnp.exp(jnp.where(valid, differ, -1e30)) * scores
            results.append(dot(mixing.astype(bf16), u_low))
        skip = pair(head_row[2:3, :], j, low_half[0:1, :])
        y_ref[0, :, span] = jnp.where(low_half, results[0], results[1]) + skip * xc
        left = jnp.exp(pair(last, j, low_half[0:1, :]) - pair(summed, j, low_half)) * same
        e_ref[0, :, span] = dot(bt_low, (left * u).astype(bf16))


def mixer_local(xr, xt, bc, bt, dtr, taps_x, taps_bc, head_row, pos, heads):
    seqs, count, width = xr.shape
    states = bc.shape[2] // 2

    def whole(a):
        return pl.BlockSpec(a.shape, lambda s: (0,) * a.ndim)

    def per_seq(a):
        return pl.BlockSpec((1,) + a.shape[1:], lambda s: (s,) + (0,) * (a.ndim - 1))

    outs = [
        jax.ShapeDtypeStruct((seqs, count, width), f32),
        jax.ShapeDtypeStruct((seqs, states, width), f32),
        jax.ShapeDtypeStruct((seqs, count, states), bf16),
        jax.ShapeDtypeStruct((seqs, count, LANES), f32),
    ]
    return pl.pallas_call(
        functools.partial(mixer_local_kernel, heads),
        grid=(seqs,),
        out_shape=outs,
        in_specs=[
            per_seq(xr), per_seq(xt), per_seq(bc), per_seq(bt), per_seq(dtr),
            whole(taps_x), whole(taps_bc), whole(head_row), per_seq(pos),
        ],
        out_specs=[per_seq(o) for o in outs],
        scratch_shapes=[
            pltpu.VMEM((count + TAIL, width), f32),
            pltpu.VMEM((count + TAIL, 2 * states), f32),
        ],
        compiler_params=pltpu.CompilerParams(vmem_limit_bytes=VMEM_LIMIT),
        name="mixer_local",
    )(xr, xt, bc, bt, dtr, taps_x, taps_bc, head_row, pos)


def mixer_back_kernel(
    heads, xr_ref, xt_ref, bc_ref, bt_ref, dtr_ref, tx_ref, tb_ref, hr_ref, pos_ref,
    dy_ref, y_ref, st_ref, de_ref, dcl_ref,
    dx_ref, dbc_ref, ddt_ref, gtx_ref, gtb_ref, gh_ref,
    jx, jb, ax, ab,
):
    count = xr_ref.shape[1]
    states = LANES
    pos = pos_ref[0]
    head_row = hr_ref[...]
    jx[0:TAIL, :] = xt_ref[0]
    jx[TAIL : TAIL + count, :] = xr_ref[0]
    jb[0:TAIL, :] = bt_ref[0]
    jb[TAIL : TAIL + count, :] = bc_ref[0]
    pre_b = conv_pre(jb, slice(0, 2 * LANES), tb_ref[...], pos, count)
    sig_b = sig(pre_b)
    bc = pre_b * sig_b
    b_low = bc[:, :states].astype(bf16)
    c_low = bc[:, states:].astype(bf16)
    pre_dt, dt, la, summed = decay_parts(dtr_ref[0], head_row, pos, heads)
    rows = jnp.transpose(summed)
    row = lax.broadcasted_iota(jnp.int32, (count, count), 0)
    col = lax.broadcasted_iota(jnp.int32, (count, count), 1)
    marks = summed[:, LANES - 1 : LANES]
    valid = (row <= col) & (marks == rows[LANES - 1 : LANES, :])
    scores = dot_nt(b_low, c_low)
    last = summed[count - 1 : count, :]
    same = (marks == last[:, LANES - 1 : LANES]).astype(f32)
    first = (marks == 0.0).astype(f32)
    low_half = lane_ids((count, LANES)) < HD
    low_row = low_half[0:1, :]
    lane = lane_ids((LANES, LANES))
    lane_row = lax.broadcasted_iota(jnp.int32, (LANES, LANES), 0)
    d_scores = jnp.zeros((count, count), f32)
    d_b = jnp.zeros((count, states), f32)
    d_c = jnp.zeros((count, states), f32)
    d_sum = jnp.zeros((count, LANES), f32)
    d_dt = jnp.zeros((count, LANES), f32)
    d_end = jnp.zeros((1, LANES), f32)
    d_skip = jnp.zeros((1, LANES), f32)
    ax[...] = jnp.zeros_like(ax)
    ab[...] = jnp.zeros_like(ab)
    for j in range(heads // 2):
        span = slice(j * LANES, (j + 1) * LANES)
        taps = tx_ref[:, span]
        pre = conv_pre(jx, span, taps, pos, count)
        sg = sig(pre)
        xc = pre * sg
        dt_wide = pair(dt, j, low_half)
        u = xc * dt_wide
        u_low = u.astype(bf16)
        dy = dy_ref[0, :, span].astype(f32)
        dy_low = dy.astype(bf16)
        state = st_ref[0, :, span].astype(bf16)
        d_state = de_ref[0, :, span].astype(bf16)
        results = []
        for i, h in enumerate((2 * j, 2 * j + 1)):
            differ = rows[h : h + 1, :] - summed[:, h : h + 1]
            decay = jnp.exp(jnp.where(valid, differ, -1e30))
            half = low_half if i == 0 else jnp.logical_not(low_half)
            u_half = jnp.where(half, u, 0.0).astype(bf16)
            d_scores = d_scores + decay * dot_nt(u_half, dy_low)
            results.append(dot((decay * scores).astype(bf16), dy_low))
        left = jnp.exp(pair(last, j, low_row) - pair(summed, j, low_half)) * same
        reads = jnp.exp(pair(summed, j, low_half)) * first
        du_end = left * dot(b_low, d_state)
        du_in = jnp.where(low_half, results[0], results[1])
        du = du_in + du_end
        d_c = d_c + dot_nt((reads * dy).astype(bf16), state)
        d_b = d_b + dot_nt((left * u).astype(bf16), d_state)
        skip = pair(head_row[2:3, :], j, low_row)
        chosen = (
            ((lane == 2 * j) & (lane_row < HD)) | ((lane == 2 * j + 1) & (lane_row >= HD))
        ).astype(f32)
        per_token = (
            dy_low.astype(f32) * (y_ref[0, :, span] - skip * xc)
            - u_low.astype(f32) * du_in
            - u * du_end
        )
        d_sum = d_sum + jnp.dot(per_token, chosen, precision=highest, preferred_element_type=f32)
        d_dt = d_dt + jnp.dot(du * xc, chosen, precision=highest, preferred_element_type=f32)
        d_end = d_end + jnp.dot(
            jnp.sum(u * du_end, axis=0, keepdims=True), chosen, precision=highest,
            preferred_element_type=f32,
        )
        d_skip = d_skip + jnp.dot(
            jnp.sum(dy * xc, axis=0, keepdims=True), chosen, precision=highest,
            preferred_element_type=f32,
        )
        d_pre = (du * dt_wide + skip * dy) * (sg * (1.0 + pre * (1.0 - sg)))
        for k in range(KC):
            masked = d_pre * (pos >= k).astype(f32) if k else d_pre
            gtx_ref[0, k : k + 1, span] = jnp.sum(
                masked * jx[TAIL - k : TAIL - k + count, span], axis=0, keepdims=True
            )
            ax[TAIL - k : TAIL - k + count, span] += taps[k : k + 1, :] * masked
    dx_ref[0] = ax[...].astype(dx_ref.dtype)
    d_b = d_b + dot(d_scores.astype(bf16), c_low)
    d_c = d_c + dot(jnp.transpose(d_scores).astype(bf16), b_low)
    d_pre = jnp.concatenate([d_b, d_c], axis=1) * (sig_b * (1.0 + pre_b * (1.0 - sig_b)))
    for k in range(KC):
        masked = d_pre * (pos >= k).astype(f32) if k else d_pre
        gtb_ref[0, k : k + 1, :] = jnp.sum(
            masked * jb[TAIL - k : TAIL - k + count, :], axis=0, keepdims=True
        )
        ab[TAIL - k : TAIL - k + count, :] += tb_ref[k : k + 1, :] * masked
    dbc_ref[0] = ab[...].astype(dbc_ref.dtype)
    token = lax.broadcasted_iota(jnp.int32, (count, LANES), 0)
    at_last = d_end + dcl_ref[0]
    d_sum = d_sum + jnp.where(token == count - 1, at_last, 0.0)
    upper = (row <= col).astype(f32)
    d_la = jnp.dot(upper, d_sum, precision=highest, preferred_element_type=f32)
    d_la = jnp.where(lane_ids(d_la.shape) < heads, d_la, 0.0)
    d_dt = d_dt - jnp.exp(head_row[0:1, :]) * d_la
    d_dtr = d_dt * sig(pre_dt)
    d_dtr = jnp.where(lane_ids(d_dtr.shape) < heads, d_dtr, 0.0)
    ddt_ref[0, 0:TAIL, :] = jnp.zeros((TAIL, LANES), ddt_ref.dtype)
    ddt_ref[0, TAIL:, :] = d_dtr.astype(ddt_ref.dtype)
    gh_ref[0, 0:1, :] = jnp.sum(d_la * la, axis=0, keepdims=True)
    gh_ref[0, 1:2, :] = jnp.sum(d_dtr, axis=0, keepdims=True)
    gh_ref[0, 2:3, :] = d_skip
    gh_ref[0, 3:8, :] = jnp.zeros((5, LANES), f32)


def mixer_back(
    xr, xt, bc, bt, dtr, taps_x, taps_bc, head_row, pos, dy, y, state, d_ends, d_carry, heads
):
    seqs, count, width = xr.shape
    states = bc.shape[2] // 2

    def whole(a):
        return pl.BlockSpec(a.shape, lambda s: (0,) * a.ndim)

    def per_seq(a):
        return pl.BlockSpec((1,) + a.shape[1:], lambda s: (s,) + (0,) * (a.ndim - 1))

    outs = [
        jax.ShapeDtypeStruct((seqs, count + TAIL, width), f32),
        jax.ShapeDtypeStruct((seqs, count + TAIL, 2 * states), f32),
        jax.ShapeDtypeStruct((seqs, count + TAIL, LANES), f32),
        jax.ShapeDtypeStruct((seqs, KC, width), f32),
        jax.ShapeDtypeStruct((seqs, KC, 2 * states), f32),
        jax.ShapeDtypeStruct((seqs, 8, LANES), f32),
    ]
    args = (xr, xt, bc, bt, dtr, taps_x, taps_bc, head_row, pos, dy, y, state, d_ends, d_carry)
    shared = (5, 6, 7)
    return pl.pallas_call(
        functools.partial(mixer_back_kernel, heads),
        grid=(seqs,),
        out_shape=outs,
        in_specs=[whole(a) if i in shared else per_seq(a) for i, a in enumerate(args)],
        out_specs=[per_seq(o) for o in outs],
        scratch_shapes=[
            pltpu.VMEM((count + TAIL, width), f32),
            pltpu.VMEM((count + TAIL, 2 * states), f32),
            pltpu.VMEM((count + TAIL, width), f32),
            pltpu.VMEM((count + TAIL, 2 * states), f32),
        ],
        compiler_params=pltpu.CompilerParams(vmem_limit_bytes=VMEM_LIMIT),
        name="mixer_back",
    )(*args)


def attention_mask(tokens, begins, key_tokens, key_begins):
    return (key_tokens[:, None, :] <= tokens[:, :, None]) & (
        key_begins[:, None, :] == begins[:, :, None]
    )


def attend_one(q, k, v, mask):
    scores = jnp.einsum("qrd,kd->rqk", q, k, preferred_element_type=f32) * 0.125
    scores = jnp.where(mask[None], scores, -1e30)
    top = jnp.max(scores, axis=-1, keepdims=True)
    weights = jnp.where(mask[None], jnp.exp(scores - top), 0.0)
    total = jnp.sum(weights, axis=-1, keepdims=True)
    out = jnp.einsum("rqk,kd->qrd", (weights / total).astype(bf16), v, preferred_element_type=f32)
    return out, (top + jnp.log(total))[..., 0]


def attend_one_back(q, k, v, mask, d_out, lse, row_dot):
    scores = jnp.einsum("qrd,kd->rqk", q, k, preferred_element_type=f32) * 0.125
    probs = jnp.where(mask[None], jnp.exp(scores - lse[..., None]), 0.0)
    d_probs = jnp.einsum("qrd,kd->rqk", d_out, v, preferred_element_type=f32)
    d_scores = (probs * (d_probs - row_dot[..., None])).astype(bf16)
    d_q = jnp.einsum("rqk,kd->qrd", d_scores, k, preferred_element_type=f32) * 0.125
    d_k = jnp.einsum("rqk,qrd->kd", d_scores, q, preferred_element_type=f32) * 0.125
    d_v = jnp.einsum("rqk,qrd->kd", probs.astype(bf16), d_out, preferred_element_type=f32)
    return d_q, jnp.concatenate([d_k, d_v], axis=-1)


def over_seqs(function, args):
    if small_mesh():
        return jax.vmap(function)(*args)
    return lax.map(lambda a: function(*a), args)


def return_to_owners(kept):
    count, me = lax.axis_size("ctx"), lax.axis_index("ctx")
    low = kept.astype(bf16)
    if count <= 4:
        total = kept[:, 0]
        for d in range(1, count):
            total = total + shifted(low[:, d], "ctx", -d).astype(f32)
        return total
    places = lax.rem(me - jnp.arange(count) + count, count)
    ordered = jnp.take(low, places, axis=1)
    seqs, _, rows, width = ordered.shape
    ordered = ordered.reshape(seqs, count * rows, width)
    return lax.psum_scatter(ordered, "ctx", scatter_dimension=1, tiled=True).astype(f32)


def turn_matrix(columns):
    source = jnp.arange(columns)[:, None]
    target = jnp.arange(columns)[None, :]
    half = HD // 2
    low = target % HD < half
    minus = low & (source == target + half)
    plus = jnp.logical_not(low) & (source == target - half)
    return plus.astype(f32) - minus.astype(f32)


def per_device(
    hidden_in,
    positions,
    gain_attn,
    w_qkv,
    w_attn_out,
    w_zx,
    w_bc,
    w_dt,
    conv_x,
    conv_bc,
    a_log,
    dt_bias,
    d_skip,
    w_mamba_out,
    gain_ffn,
    w_gu,
    w_down,
    output_cotangent,
):
    seqs, block = positions.shape
    features = hidden_in.shape[2]
    rows = w_qkv.shape[0]
    heads = a_log.shape[0]
    inner = w_zx.shape[2]
    both = w_bc.shape[1]
    states = both // 2
    columns = w_qkv.shape[2]
    per_group = columns // HD - 2
    qwidth = per_group * HD
    units = w_gu.shape[2]
    count = lax.axis_size("ctx")
    place = lax.axis_index("ctx")
    tokens_here = seqs * block

    pad = jnp.zeros((rows, LANES - heads - 2), bf16)
    first_pack = jnp.concatenate(
        [w_zx[:, 1, :], w_bc, w_dt, gain_attn[:, None], gain_ffn[:, None], pad], axis=1
    )
    second_pack = jnp.concatenate(
        [w_qkv[:, 0, :], w_zx[:, 0, :], w_attn_out.T, w_mamba_out.T], axis=1
    )
    third_pack = jnp.concatenate([w_gu[:, 0, :], w_gu[:, 1, :], w_down.T], axis=1)
    tail = shifted(hidden_in[:, block - TAIL :, :], "ctx", 1)
    (w_one,) = gather_rows(first_pack, [inner + both + LANES])
    w_two, w_three = gather_rows(second_pack, [columns + inner, qwidth + inner])
    w_four, w_five = gather_rows(third_pack, [2 * units, units])

    tokens = place * block + jnp.arange(block, dtype=jnp.int32)
    begins = tokens[None, :] - positions
    all_begins = behind(begins)
    key_begins = jnp.concatenate(
        [jnp.where(place >= d, b, -1) for d, b in enumerate(all_begins)], axis=1
    )
    key_tokens = jnp.concatenate([tokens - d * block for d in range(count)])
    key_tokens = jnp.broadcast_to(key_tokens[None], key_begins.shape)
    mask = attention_mask(
        jnp.broadcast_to(tokens[None], begins.shape), begins, key_tokens, key_begins
    )
    frequency = jnp.power(
        jnp.float32(rope_base), -jnp.arange(0, HD, 2).astype(f32) / HD
    )
    spread = jnp.tile(frequency, (qwidth + HD) * 2 // HD)
    turned = positions.astype(f32).reshape(tokens_here, 1) * spread
    cosine, sine = jnp.cos(turned), jnp.sin(turned)
    turn = turn_matrix(qwidth + HD)

    x_own = hidden_in.reshape(tokens_here, features).astype(f32)
    x_ext = jnp.concatenate([x_own, tail.reshape(seqs * TAIL, features).astype(f32)], axis=0)
    gain_a = w_one[:, inner + both + heads].astype(f32)
    gain_f = w_one[:, inner + both + heads + 1].astype(f32)
    r_ext = lax.rsqrt(jnp.mean(x_ext * x_ext, axis=-1, keepdims=True) + 1e-05)
    h_ext = (x_ext * r_ext * gain_a).astype(bf16)
    h_own = h_ext[:tokens_here]
    r_one = r_ext[:tokens_here]

    proj = dot(h_ext, w_one)
    xr, xt = (
        proj[:tokens_here, :inner].reshape(seqs, block, inner),
        proj[tokens_here:, :inner].reshape(seqs, TAIL, inner),
    )
    bc, bt = (
        proj[:tokens_here, inner : inner + both].reshape(seqs, block, both),
        proj[tokens_here:, inner : inner + both].reshape(seqs, TAIL, both),
    )
    dtr = proj[:tokens_here, inner + both :].reshape(seqs, block, LANES)
    taps_x = conv_x.astype(f32)
    taps_bc = conv_bc.astype(f32)
    head_row = jnp.zeros((8, LANES), f32)
    head_row = head_row.at[0, :heads].set(a_log).at[1, :heads].set(dt_bias).at[2, :heads].set(d_skip)
    pos = positions[:, :, None]
    y_local, ends, c_vec, summed = mixer_local(
        xr, xt, bc, bt, dtr, taps_x, taps_bc, head_row, pos, heads
    )
    last = summed[:, block - 1, :]
    own_carry = jnp.exp(last[:, :heads]) * (last[:, LANES - 1 :] == 0.0).astype(f32)
    own_carry = jnp.repeat(own_carry, HD, axis=1)
    if count <= 4:
        pieces = jnp.stack([own_carry] + [swap(own_carry, "ctx", k) for k in range(1, count)])
        carry = jnp.stack([pick(pieces, place ^ j, 0) for j in range(count)])
    else:
        carry = lax.all_gather(own_carry, "ctx")
    state = chained(carry, ends, False)

    qz = dot(h_own, w_two)
    qkv = qz[:, :columns]
    gate = qz[:, columns:].reshape(seqs, block, inner)
    rotated_in = qkv[:, : qwidth + HD]
    w_turned = dot(w_two[:, : qwidth + HD], turn.astype(bf16)).astype(bf16)
    rotated = (rotated_in * cosine + dot(h_own, w_turned) * sine).astype(bf16)
    q_low = rotated[:, :qwidth].reshape(seqs, block, per_group, HD)
    kv_low = jnp.concatenate([rotated[:, qwidth:], qkv[:, qwidth + HD :].astype(bf16)], axis=1)
    keys_values = jnp.concatenate(behind(kv_low.reshape(seqs, block, 2 * HD)), axis=1)
    keys, values = keys_values[..., :HD], keys_values[..., HD:]
    attended, lse = over_seqs(attend_one, (q_low, keys, values, mask))

    read_weight = jnp.exp(jnp.repeat(summed[:, :, :heads], HD, axis=2)) * (
        summed[:, :, LANES - 1 :] == 0.0
    ).astype(f32)
    state_low = state.astype(bf16)
    y = y_local + read_weight * jnp.einsum(
        "stn,snw->stw", c_vec, state_low, preferred_element_type=f32
    )
    sig_gate = jax.nn.sigmoid(gate)
    silu_gate = gate * sig_gate
    gated = (y * silu_gate).astype(bf16)
    mixer_out = jnp.concatenate(
        [attended.reshape(tokens_here, qwidth).astype(bf16), gated.reshape(tokens_here, inner)],
        axis=1,
    )
    resid = x_own + pair_sum(dot_nt(mixer_out, w_three))

    r_two = lax.rsqrt(jnp.mean(resid * resid, axis=-1, keepdims=True) + 1e-05)
    h_two = (resid * r_two * gain_f).astype(bf16)
    gate_up = dot(h_two, w_four)
    gate_ff, up_ff = gate_up[:, :units], gate_up[:, units:]
    sig_ff = jax.nn.sigmoid(gate_ff)
    silu_ff = gate_ff * sig_ff
    hidden_state = (silu_ff * up_ff).astype(bf16)
    ffn = pair_sum(dot_nt(hidden_state, w_five))
    block_out = (resid + ffn).astype(bf16).reshape(seqs, block, features)

    e_low = output_cotangent.reshape(tokens_here, features)
    d_hidden_state = dot(e_low, w_five)
    d_gate_up = jnp.concatenate(
        [
            d_hidden_state * up_ff * (sig_ff * (1.0 + gate_ff * (1.0 - sig_ff))),
            d_hidden_state * silu_ff,
        ],
        axis=1,
    ).astype(bf16)

    def tn(a, b):
        return lax.dot_general(a, b, (((0,), (0,)), ((), ())), preferred_element_type=f32)

    d_h_two_part = dot_nt(d_gate_up, w_four).astype(bf16)
    d_h_two = pair_sum(d_h_two_part)
    ffn_grads = scatter_rows([tn(h_two, d_gate_up).astype(bf16), tn(e_low, hidden_state).astype(bf16)])
    grad_gain_f = jnp.sum(d_h_two_part.astype(f32) * resid * r_two, axis=0)
    scaled = d_h_two * gain_f
    d_resid = (
        e_low.astype(f32)
        + r_two * scaled
        - resid * (r_two * r_two * r_two) * jnp.mean(resid * scaled, axis=-1, keepdims=True)
    )
    d_mix = d_resid.astype(bf16)

    d_mixer_out = dot(d_mix, w_three)
    d_att = d_mixer_out[:, :qwidth].astype(bf16).reshape(seqs, block, per_group, HD)
    d_gated = d_mixer_out[:, qwidth:].reshape(seqs, block, inner)
    d_y = d_gated * silu_gate
    d_z = (d_gated * y * (sig_gate * (1.0 + gate * (1.0 - sig_gate)))).astype(bf16)
    state_grad = jnp.einsum(
        "stn,stw->snw", c_vec, (read_weight * d_y).astype(bf16), preferred_element_type=f32
    )
    later_grad = chained(carry, state_grad, True)

    row_dot = jnp.transpose(jnp.sum(d_att.astype(f32) * attended, axis=-1), (0, 2, 1))
    d_q, kept = over_seqs(
        attend_one_back, (q_low, keys, values, mask, d_att, lse, row_dot)
    )
    d_kv = return_to_owners(kept.reshape(seqs, count, block, 2 * HD)).reshape(tokens_here, 2 * HD)
    d_rot = jnp.concatenate([d_q.reshape(tokens_here, qwidth), d_kv[:, :HD]], axis=1)
    d_qk = d_rot * cosine + jnp.dot(d_rot * sine, turn.T, precision=lax.Precision.HIGH)
    d_two = jnp.concatenate(
        [d_qk.astype(bf16), d_kv[:, HD:].astype(bf16), d_z.reshape(tokens_here, inner)], axis=1
    )
    two_grads = scatter_rows([tn(h_own, d_two).astype(bf16), tn(d_mix, mixer_out).astype(bf16)])

    d_carry = jnp.sum((later_grad * state).reshape(seqs, states, heads, HD), axis=(1, 3))
    d_carry = d_carry * own_carry.reshape(seqs, heads, HD)[:, :, 0]
    d_carry = jnp.pad(d_carry, ((0, 0), (0, LANES - heads)))[:, None, :]
    d_x, d_bc, d_dtr, g_taps_x, g_taps_bc, g_heads = mixer_back(
        xr, xt, bc, bt, dtr, taps_x, taps_bc, head_row, pos,
        d_y, y, state_low, later_grad.astype(bf16), d_carry, heads,
    )
    d_one = jnp.concatenate([d_x, d_bc, d_dtr], axis=2).astype(bf16)
    d_one = jnp.concatenate(
        [
            d_one[:, TAIL:].reshape(tokens_here, -1),
            d_one[:, :TAIL].reshape(seqs * TAIL, -1),
        ],
        axis=0,
    )
    one_grads = scatter_rows([tn(h_ext, d_one).astype(bf16)])

    d_tail = dot_nt(d_one[tokens_here:], w_one)
    d_tail = shifted(pair_sum(d_tail).astype(bf16), "ctx", -1).astype(f32)
    d_h_part = (dot_nt(d_two, w_two) + dot_nt(d_one[:tokens_here], w_one)).astype(bf16)
    d_h = pair_sum(d_h_part).reshape(seqs, block, features)
    d_h = d_h.at[:, block - TAIL :, :].add(d_tail.reshape(seqs, TAIL, features))
    d_h = d_h.reshape(tokens_here, features)
    grad_gain_a = jnp.sum(d_h * x_own * r_one, axis=0)
    scaled = d_h * gain_a
    d_hidden = (
        d_resid
        + r_one * scaled
        - x_own * (r_one * r_one * r_one) * jnp.mean(x_own * scaled, axis=-1, keepdims=True)
    )
    d_hidden = d_hidden.astype(bf16).reshape(seqs, block, features)

    over_pair = jnp.concatenate([jnp.sum(g_taps_bc, axis=0).reshape(-1), grad_gain_f])
    over_pair = sum_all(over_pair, ("tp",))
    over_rest = jnp.concatenate(
        [
            jnp.sum(g_taps_x, axis=0).reshape(-1),
            jnp.sum(g_heads, axis=0)[:3, :heads].reshape(-1),
            grad_gain_a,
            over_pair,
        ]
    )
    total = sum_all(over_rest, ("dp", "ctx"))
    sizes = (KC * inner, heads, heads, heads, features, KC * both, features)
    small, first = [], 0
    for size in sizes:
        small.append(total[first : first + size])
        first += size
    g_tx, g_decay, g_bias, g_skip, g_gain_a, g_tb, g_gain_f = small
    shard = lax.axis_index("dp") * count + place

    def own_rows(vector):
        return lax.dynamic_slice_in_dim(vector, shard * rows, rows, 0)

    bc_grad = one_grads[:, inner : inner + both]
    bc_grad = sum_all(bc_grad, ("tp",))
    zx_grad = jnp.stack(
        [two_grads[:, columns : columns + inner], one_grads[:, :inner]], axis=1
    )
    return (
        block_out,
        d_hidden,
        own_rows(g_gain_a),
        two_grads[:, None, :columns],
        two_grads[:, columns + inner : columns + inner + qwidth].T,
        zx_grad,
        bc_grad,
        one_grads[:, inner + both : inner + both + heads],
        g_tx.reshape(KC, inner),
        g_tb.reshape(KC, both),
        g_decay,
        g_bias,
        g_skip,
        two_grads[:, columns + inner + qwidth :].T,
        own_rows(g_gain_f),
        jnp.stack([ffn_grads[:, :units], ffn_grads[:, units : 2 * units]], axis=1),
        ffn_grads[:, 2 * units :].T,
    )


def solution(mesh):
    in_specs = (
        P("dp", "ctx", None),
        P("dp", "ctx"),
        P(("dp", "ctx")),
        P(("dp", "ctx"), "tp", None),
        P("tp", ("dp", "ctx")),
        P(("dp", "ctx"), None, "tp"),
        P(("dp", "ctx"), None),
        P(("dp", "ctx"), "tp"),
        P(None, "tp"),
        P(),
        P("tp"),
        P("tp"),
        P("tp"),
        P("tp", ("dp", "ctx")),
        P(("dp", "ctx")),
        P(("dp", "ctx"), None, "tp"),
        P("tp", ("dp", "ctx")),
        P("dp", "ctx", None),
    )
    out_specs = (
        P("dp", "ctx", None),
        P("dp", "ctx", None),
        P(("dp", "ctx")),
        P(("dp", "ctx"), "tp", None),
        P("tp", ("dp", "ctx")),
        P(("dp", "ctx"), None, "tp"),
        P(("dp", "ctx"), None),
        P(("dp", "ctx"), "tp"),
        P(None, "tp"),
        P(),
        P("tp"),
        P("tp"),
        P("tp"),
        P("tp", ("dp", "ctx")),
        P(("dp", "ctx")),
        P(("dp", "ctx"), None, "tp"),
        P("tp", ("dp", "ctx")),
    )
    return jax.shard_map(
        per_device, mesh=mesh, in_specs=in_specs, out_specs=out_specs, check_vma=False
    )
```

```python
import functools

import jax
import jax.numpy as jnp
from jax import lax
from jax.experimental import pallas as pl
from jax.experimental.pallas import tpu as pltpu
from jax.sharding import PartitionSpec as P

HD = 64
KC = 4
TAIL = 16
LANES = 128
VMEM_LIMIT = 56 * 1024 * 1024

f32 = jnp.float32
bf16 = jnp.bfloat16
highest = lax.Precision.HIGHEST
rope_base = 100000000000.0


def small_mesh():
    return lax.axis_size("dp") == 4 and lax.axis_size("ctx") == 4


def swap(value, axis, bits):
    count = lax.axis_size(axis)
    return lax.ppermute(value, axis, [(i, i ^ bits) for i in range(count)])


def shifted(value, axis, distance):
    count = lax.axis_size(axis)
    route = [(i - distance, i) for i in range(count) if 0 <= i - distance < count]
    return lax.ppermute(value, axis, route)


def place_blocks(pieces, outs, copies):
    count = len(pieces)
    total = len(outs)
    where = jnp.stack([lax.axis_index("dp"), lax.axis_index("ctx")]).astype(jnp.int32)

    def kernel(where_ref, *refs):
        ins = refs[:count]
        outputs = refs[count : count + total]
        sems = refs[count + total]
        running = []
        for number, (piece, first, width, out, axis, bits, to) in enumerate(copies):
            target = outputs[out]
            if axis is None:
                target = target.at[:, pl.ds(to, width)]
            else:
                target = target.at[jnp.bitwise_xor(where_ref[axis], bits), :, pl.ds(to, width)]
            copy = pltpu.make_async_copy(
                ins[piece].at[:, pl.ds(first, width)], target, sems.at[number]
            )
            copy.start()
            running.append(copy)
        for copy in running:
            copy.wait()

    return pl.pallas_call(
        kernel,
        out_shape=[jax.ShapeDtypeStruct(shape, pieces[0].dtype) for shape in outs],
        in_specs=[pl.BlockSpec(memory_space=pltpu.SMEM)]
        + [pl.BlockSpec(memory_space=pl.ANY)] * count,
        out_specs=[pl.BlockSpec(memory_space=pltpu.VMEM)] * total,
        scratch_shapes=[pltpu.SemaphoreType.DMA((len(copies),))],
        compiler_params=pltpu.CompilerParams(vmem_limit_bytes=VMEM_LIMIT),
        name="place_blocks",
    )(where, *pieces)


class Placing:
    def __init__(self):
        self.pieces, self.outs, self.copies = [], [], []

    def out(self, *shape):
        self.outs.append(shape)
        return len(self.outs) - 1

    def add(self, piece, out, axis=None, bits=0, to=0, first=0, width=None):
        for number, known in enumerate(self.pieces):
            if known is piece:
                break
        else:
            number = len(self.pieces)
            self.pieces.append(piece)
        width = piece.shape[1] if width is None else width
        self.copies.append((number, first, width, out, axis, bits, to))

    def after(self, *arrays):
        self.pieces.extend(arrays)

    def run(self):
        return place_blocks(self.pieces, self.outs, self.copies)


def along_ctx(packed):
    return [packed] + [swap(packed, "ctx", k) for k in (1, 2, 3)]


def along_dp(held, one, two):
    near = swap(held, "dp", one)
    return [(0, held), (one, near), (two, swap(held, "dp", two)), (3, swap(near, "dp", two))]


def gather_all(first, second, third, with_first):
    rows = first.shape[0]
    if not small_mesh():
        def whole(piece):
            return lax.all_gather(piece, ("dp", "ctx"), axis=0, tiled=True)

        w_two, w_three = [whole(jnp.concatenate(p, axis=1)) for p in second]
        w_four, w_five = [
            whole(
                jnp.concatenate(
                    [p for p, out, _ in sorted(third[0] + third[1], key=lambda t: t[2]) if out == o],
                    axis=1,
                )
            )
            for o in (0, 1)
        ]
        return with_first(whole(first)), w_two, w_three, w_four, w_five, []

    def flat(held):
        return held.reshape(held.shape[0] * held.shape[1], held.shape[2])

    wide_one = first.shape[1]
    wide_two = [sum(p.shape[1] for p in part) for part in second]
    wide_half = [sum(p.shape[1] for p, _, _ in half) for half in third]
    work = Placing()
    held_out = work.out(4, rows, wide_one)
    pack_out = work.out(rows, sum(wide_two))
    for k, piece in enumerate(along_ctx(first)):
        work.add(piece, held_out, 1, k)
    to = 0
    for piece in second[0] + second[1]:
        work.add(piece, pack_out, to=to)
        to += piece.shape[1]
    held_one, packed_two = work.run()
    held_one = flat(held_one)
    work = Placing()
    full = work.out(4, 4 * rows, wide_one)
    held_out = [work.out(4, rows, w) for w in wide_two]
    pack_out = work.out(rows, sum(wide_half))
    for k in range(4):
        work.add(held_one if k == 0 else swap(held_one, "dp", k), full, 0, k)
    for k, piece in enumerate(along_ctx(packed_two)):
        work.add(piece, held_out[0], 1, k, width=wide_two[0])
        work.add(piece, held_out[1], 1, k, first=wide_two[0], width=wide_two[1])
    to = 0
    for piece, _, _ in third[0] + third[1]:
        work.add(piece, pack_out, to=to)
        to += piece.shape[1]
    w_one, held_a, held_b, packed_three = work.run()
    made = with_first(flat(w_one))
    work = Placing()
    fulls = [work.out(4, 4 * rows, w) for w in wide_two]
    held_out = [work.out(4, rows, w) for w in wide_half]
    for bits, piece in along_dp(flat(held_a), 1, 2):
        work.add(piece, fulls[0], 0, bits)
    for bits, piece in along_dp(flat(held_b), 2, 1):
        work.add(piece, fulls[1], 0, bits)
    for k, piece in enumerate(along_ctx(packed_three)):
        work.add(piece, held_out[0], 1, k, width=wide_half[0])
        work.add(piece, held_out[1], 1, k, first=wide_half[0], width=wide_half[1])
    work.after(made[-1])
    w_two, w_three, held_a, held_b = work.run()
    work = Placing()
    ends = [0, 0]
    for part in third[0] + third[1]:
        ends[part[1]] += part[0].shape[1]
    fulls = [work.out(4, 4 * rows, w) for w in ends]
    nears = []
    for half, held, order in ((third[0], held_a, (1, 2)), (third[1], held_b, (2, 1))):
        blocks = along_dp(flat(held), *order)
        nears += [blocks[1][1], blocks[2][1]]
        for bits, piece in blocks:
            column = 0
            for part, out, to in half:
                work.add(piece, fulls[out], 0, bits, to=to, first=column, width=part.shape[1])
                column += part.shape[1]
    w_four, w_five = work.run()
    return made, flat(w_two), flat(w_three), flat(w_four), flat(w_five), nears


def pick(value, index, axis):
    return lax.dynamic_index_in_dim(value, index, axis, keepdims=False)


class Scatter:
    def __init__(self, grads):
        self.grads = grads
        self.staged = small_mesh()
        self.got, self.near, self.along = [], [], []
        if not self.staged:
            return
        self.dp, self.ctx = lax.axis_index("dp"), lax.axis_index("ctx")
        self.y, self.x = self.dp // 2, self.dp % 2
        rows = grads[0][0].shape[0]
        if len(grads) == 1:
            self.blocks = grads[0][0].reshape(4, rows // 4, -1)
            self.got = [swap(pick(self.blocks, self.dp ^ k, 0), "dp", k) for k in (1, 2, 3)]
            return
        self.kept = []
        for number, group in enumerate(grads):
            one, axis, at = (2, 0, self.y) if number == 0 else (1, 1, self.x)

            def part(index):
                return jnp.concatenate(
                    [pick(g.reshape(2, 2, rows // 4, -1), index, axis) for g in group], axis=2
                )

            self.got.append(swap(part(1 - at), "dp", one))
            self.kept.append(part(at))

    def second(self):
        if not self.staged or len(self.grads) == 1:
            return
        for number in range(2):
            then, two = (self.x, 1) if number == 0 else (self.y, 2)
            kept, got = self.kept[number], self.got[number]
            send = (
                pick(kept, 1 - then, 0).astype(f32) + pick(got, 1 - then, 0).astype(f32)
            ).astype(bf16)
            self.near.append(swap(send, "dp", two))

    def third(self):
        if not self.staged:
            return
        if len(self.grads) == 1:
            total = pick(self.blocks, self.dp, 0).astype(f32)
            for piece in self.got:
                total = total + piece.astype(f32)
            held = total.astype(bf16)
        else:
            parts = []
            for number in range(2):
                then = self.x if number == 0 else self.y
                parts.append(
                    (
                        pick(self.kept[number], then, 0).astype(f32)
                        + pick(self.got[number], then, 0).astype(f32)
                        + self.near[number].astype(f32)
                    ).astype(bf16)
                )
            held = jnp.concatenate(parts, axis=1)
        self.held = held.reshape(4, held.shape[0] // 4, -1)
        self.along = [swap(pick(self.held, self.ctx ^ k, 0), "ctx", k) for k in (1, 2, 3)]

    def result(self):
        if not self.staged:
            parts = [g for group in self.grads for g in group]
            joined = jnp.concatenate(parts, axis=1) if len(parts) > 1 else parts[0]
            return lax.psum_scatter(
                joined, ("dp", "ctx"), scatter_dimension=0, tiled=True
            ).astype(f32)
        total = pick(self.held, self.ctx, 0).astype(f32)
        for piece in self.along:
            total = total + piece.astype(f32)
        return total


def sum_all(value, axes):
    for axis in axes:
        count = lax.axis_size(axis)
        if count & (count - 1):
            value = lax.psum(value, axis)
            continue
        bits = 1
        while bits < count:
            value = value + swap(value, axis, bits)
            bits *= 2
    return value


def pair_sum(value):
    if lax.axis_size("tp") != 2:
        return lax.psum(value.astype(bf16), "tp").astype(f32)
    low = value.astype(bf16)
    return low.astype(f32) + swap(low, "tp", 1).astype(f32)


def chain_pieces(pack, reverse):
    count, me = lax.axis_size("ctx"), lax.axis_index("ctx")
    if count <= 4:
        sign = -1 if reverse else 1
        return [shifted(pack, "ctx", sign * d) for d in range(1, count)]
    everything = lax.all_gather(pack, "ctx")
    states = pack.shape[1] - TAIL

    def hop(k, before):
        at = count - 1 - k if reverse else k
        reached = at > me if reverse else at < me
        there = pick(everything, at, 0).astype(f32)
        new = there[:, states : states + 1] * before + there[:, :states]
        return jnp.where(reached, new, before)

    start = jnp.zeros((pack.shape[0], states, pack.shape[2]), f32)
    total = lax.fori_loop(0, count, hop, start).astype(bf16)
    return [jnp.pad(total, ((0, 0), (0, TAIL), (0, 0)))]


def dot(a, b):
    return jnp.dot(a, b, preferred_element_type=f32)


def dot_nt(a, b):
    return lax.dot_general(a, b, (((1,), (1,)), ((), ())), preferred_element_type=f32)


def sig(v):
    return 1.0 / (1.0 + jnp.exp(-v))


def conv_pre(joined, span, taps, pos, count):
    total = None
    for k in range(KC):
        piece = joined[TAIL - k : TAIL - k + count, span]
        term = taps[k : k + 1, :] * piece
        if k:
            term = term * (pos >= k).astype(f32)
        total = term if total is None else total + term
    return total


def lane_ids(shape):
    return lax.broadcasted_iota(jnp.int32, shape, 1)


def decay_parts(dtr, head_row, pos, heads):
    count = dtr.shape[0]
    lane = lane_ids(dtr.shape)
    pre = dtr + head_row[1:2, :]
    dt = jnp.where(lane < heads, jnp.maximum(pre, 0.0) + jnp.log(1.0 + jnp.exp(-jnp.abs(pre))), 0.0)
    la = -jnp.exp(head_row[0:1, :]) * dt
    marked = jnp.where(lane == LANES - 1, (pos == 0).astype(f32), la)
    row = lax.broadcasted_iota(jnp.int32, (count, count), 0)
    col = lax.broadcasted_iota(jnp.int32, (count, count), 1)
    lower = (row >= col).astype(f32)
    summed = jnp.dot(lower, marked, precision=highest, preferred_element_type=f32)
    return pre, dt, la, summed


def wide(value, lane):
    return jnp.broadcast_to(value[:, lane : lane + 1], (value.shape[0], LANES))


def pair(value, j, low_half):
    return jnp.where(low_half, wide(value, 2 * j), wide(value, 2 * j + 1))


def spec_whole(a):
    return pl.BlockSpec(a.shape, lambda s: (0,) * a.ndim)


def spec_rows(a, rows, base=0):
    return pl.BlockSpec((rows, a.shape[1]), lambda s: (base + s, 0))


def spec_seq(a):
    return pl.BlockSpec((1,) + a.shape[1:], lambda s: (s,) + (0,) * (a.ndim - 1))


def spec_any():
    return pl.BlockSpec(memory_space=pl.ANY)


def params():
    return pltpu.CompilerParams(vmem_limit_bytes=VMEM_LIMIT)


def cost(microseconds):
    return pl.CostEstimate(
        flops=int(microseconds * 1e8), bytes_accessed=int(microseconds * 3e5), transcendentals=0
    )


def chained_state(pieces, span, states):
    total, factor = None, None
    for piece in pieces:
        there = piece[0, :states, span].astype(f32)
        decay = piece[0, states : states + 1, span].astype(f32)
        if total is None:
            total, factor = there, decay
        else:
            total = total + factor * there
            factor = factor * decay
    return total


def mixer_local_kernel(
    heads, inner, both, proj_ref, tail_ref, tx_ref, tb_ref, hr_ref, pos_ref,
    y_ref, pack_ref, c_ref, l_ref, jx, jb,
):
    count = proj_ref.shape[0]
    states = both // 2
    pos = pos_ref[...]
    head_row = hr_ref[...]
    jx[0:TAIL, :] = tail_ref[:, :inner]
    jx[TAIL : TAIL + count, :] = proj_ref[:, :inner]
    jb[0:TAIL, :] = tail_ref[:, inner : inner + both]
    jb[TAIL : TAIL + count, :] = proj_ref[:, inner : inner + both]
    pre_b = conv_pre(jb, slice(0, both), tb_ref[...], pos, count)
    bc = pre_b * sig(pre_b)
    b_low = bc[:, :states].astype(bf16)
    c_low = bc[:, states:].astype(bf16)
    c_ref[...] = c_low
    bt_low = jnp.transpose(bc[:, :states]).astype(bf16)
    _, dt, _, summed = decay_parts(proj_ref[:, inner + both :], head_row, pos, heads)
    l_ref[...] = summed
    rows = jnp.transpose(summed)
    row = lax.broadcasted_iota(jnp.int32, (count, count), 0)
    col = lax.broadcasted_iota(jnp.int32, (count, count), 1)
    marks = summed[:, LANES - 1 : LANES]
    valid = (row >= col) & (marks == rows[LANES - 1 : LANES, :])
    scores = dot_nt(c_low, b_low)
    last = summed[count - 1 : count, :]
    same = (marks == last[:, LANES - 1 : LANES]).astype(f32)
    carry = jnp.exp(last) * (last[:, LANES - 1 : LANES] == 0.0).astype(f32)
    low_half = lane_ids((count, LANES)) < HD
    low_row = low_half[0:1, :]
    for j in range(heads // 2):
        span = slice(j * LANES, (j + 1) * LANES)
        pre = conv_pre(jx, span, tx_ref[:, span], pos, count)
        xc = pre * sig(pre)
        u = xc * pair(dt, j, low_half)
        u_low = u.astype(bf16)
        results = []
        for h in (2 * j, 2 * j + 1):
            differ = summed[:, h : h + 1] - rows[h : h + 1, :]
            mixing = jnp.exp(jnp.where(valid, differ, -1e30)) * scores
            results.append(dot(mixing.astype(bf16), u_low))
        skip = pair(head_row[2:3, :], j, low_row)
        y_ref[:, span] = jnp.where(low_half, results[0], results[1]) + skip * xc
        left = jnp.exp(pair(last, j, low_row) - pair(summed, j, low_half)) * same
        pack_ref[0, :states, span] = dot(bt_low, (left * u).astype(bf16)).astype(bf16)
        pack_ref[0, states:, span] = jnp.broadcast_to(pair(carry, j, low_row), (TAIL, LANES)).astype(bf16)


def mixer_local(proj, taps_x, taps_bc, head_row, pos, heads, seqs, count):
    inner, both = taps_x.shape[1], taps_bc.shape[1]
    states = both // 2
    outs = [
        jax.ShapeDtypeStruct((seqs * count, inner), f32),
        jax.ShapeDtypeStruct((seqs, states + TAIL, inner), bf16),
        jax.ShapeDtypeStruct((seqs * count, states), bf16),
        jax.ShapeDtypeStruct((seqs * count, LANES), f32),
    ]
    return pl.pallas_call(
        functools.partial(mixer_local_kernel, heads, inner, both),
        grid=(seqs,),
        out_shape=outs,
        in_specs=[
            spec_rows(proj, count),
            spec_rows(proj, TAIL, seqs * count // TAIL),
            spec_whole(taps_x), spec_whole(taps_bc), spec_whole(head_row), spec_rows(pos, count),
        ],
        out_specs=[
            spec_rows(outs[0], count), spec_seq(outs[1]), spec_rows(outs[2], count),
            spec_rows(outs[3], count),
        ],
        scratch_shapes=[
            pltpu.VMEM((count + TAIL, inner), f32),
            pltpu.VMEM((count + TAIL, both), f32),
        ],
        compiler_params=params(),
        cost_estimate=cost(8),
        name="mixer_local",
    )(proj, proj, taps_x, taps_bc, head_row, pos)


def mixer_read_kernel(
    heads, pieces, first, y0_ref, c_ref, l_ref, qz_ref, att_ref, *refs
):
    packs = refs[:pieces]
    y_ref, out_ref, state_ref = refs[-3:]
    count = y0_ref.shape[0]
    states = c_ref.shape[1]
    qwidth = att_ref.shape[1]
    summed = l_ref[...]
    alive = (summed[:, LANES - 1 : LANES] == 0.0).astype(f32)
    low_half = lane_ids((count, LANES)) < HD
    out_ref[:, :qwidth] = att_ref[...]
    for j in range(heads // 2):
        span = slice(j * LANES, (j + 1) * LANES)
        state = chained_state(packs, span, states).astype(bf16)
        state_ref[0, :, span] = state
        reads = jnp.exp(pair(summed, j, low_half)) * alive
        y = y0_ref[:, span] + reads * dot(c_ref[...], state)
        y_ref[:, span] = y
        gate = qz_ref[:, first + j * LANES : first + (j + 1) * LANES]
        out_ref[:, qwidth + j * LANES : qwidth + (j + 1) * LANES] = (y * gate * sig(gate)).astype(bf16)


def mixer_read(y_local, c_vec, summed, qz, att, packs, extra, heads, seqs, count, first):
    inner, states = y_local.shape[1], c_vec.shape[1]
    outs = [
        jax.ShapeDtypeStruct((seqs * count, inner), f32),
        jax.ShapeDtypeStruct((seqs * count, att.shape[1] + inner), bf16),
        jax.ShapeDtypeStruct((seqs, states, inner), bf16),
    ]
    args = (y_local, c_vec, summed, qz, att)
    return pl.pallas_call(
        functools.partial(mixer_read_kernel, heads, len(packs), first),
        grid=(seqs,),
        out_shape=outs,
        in_specs=[spec_rows(a, count) for a in args]
        + [spec_seq(p) for p in packs]
        + [spec_any()] * len(extra),
        out_specs=[spec_rows(outs[0], count), spec_rows(outs[1], count), spec_seq(outs[2])],
        compiler_params=params(),
        cost_estimate=cost(4),
        name="mixer_read",
    )(*args, *packs, *extra)


def gate_back_kernel(
    heads, first, qwidth, d_ref, y_ref, qz_ref, c_ref, l_ref,
    dy_ref, dz_ref, datt_ref, pack_ref,
):
    count = y_ref.shape[0]
    states = c_ref.shape[1]
    summed = l_ref[...]
    alive = (summed[:, LANES - 1 : LANES] == 0.0).astype(f32)
    last = summed[count - 1 : count, :]
    carry = jnp.exp(last) * (last[:, LANES - 1 : LANES] == 0.0).astype(f32)
    low_half = lane_ids((count, LANES)) < HD
    low_row = low_half[0:1, :]
    ct_low = jnp.transpose(c_ref[...].astype(f32)).astype(bf16)
    datt_ref[...] = d_ref[:, :qwidth].astype(bf16)
    for j in range(heads // 2):
        span = slice(j * LANES, (j + 1) * LANES)
        gate = qz_ref[:, first + j * LANES : first + (j + 1) * LANES]
        d_gated = d_ref[:, qwidth + j * LANES : qwidth + (j + 1) * LANES]
        sg = sig(gate)
        dy = d_gated * (gate * sg)
        dy_ref[:, span] = dy
        dz_ref[:, span] = (
            d_gated * y_ref[:, span] * (sg * (1.0 + gate * (1.0 - sg)))
        ).astype(bf16)
        reads = jnp.exp(pair(summed, j, low_half)) * alive
        pack_ref[0, :states, span] = dot(ct_low, (reads * dy).astype(bf16)).astype(bf16)
        pack_ref[0, states:, span] = jnp.broadcast_to(pair(carry, j, low_row), (TAIL, LANES)).astype(bf16)


def gate_back(d_mixer, y, qz, c_vec, summed, heads, seqs, count, first, qwidth):
    inner, states = y.shape[1], c_vec.shape[1]
    outs = [
        jax.ShapeDtypeStruct((seqs * count, inner), f32),
        jax.ShapeDtypeStruct((seqs * count, inner), bf16),
        jax.ShapeDtypeStruct((seqs * count, qwidth), bf16),
        jax.ShapeDtypeStruct((seqs, states + TAIL, inner), bf16),
    ]
    args = (d_mixer, y, qz, c_vec, summed)
    return pl.pallas_call(
        functools.partial(gate_back_kernel, heads, first, qwidth),
        grid=(seqs,),
        out_shape=outs,
        in_specs=[spec_rows(a, count) for a in args],
        out_specs=[spec_rows(o, count) for o in outs[:3]] + [spec_seq(outs[3])],
        compiler_params=params(),
        cost_estimate=cost(5),
        name="gate_back",
    )(*args)


def mixer_back_kernel(
    heads, inner, both, pieces, extra, proj_ref, tail_ref, tx_ref, tb_ref, hr_ref, pos_ref,
    dy_ref, y_ref, st_ref, *refs
):
    packs = refs[:pieces]
    main_ref, side_ref, gtx_ref, gtb_ref, gh_ref, jx, jb, ax, ab = refs[pieces + extra :]
    count = proj_ref.shape[0]
    states = both // 2
    pos = pos_ref[...]
    head_row = hr_ref[...]
    jx[0:TAIL, :] = tail_ref[:, :inner]
    jx[TAIL : TAIL + count, :] = proj_ref[:, :inner]
    jb[0:TAIL, :] = tail_ref[:, inner : inner + both]
    jb[TAIL : TAIL + count, :] = proj_ref[:, inner : inner + both]
    pre_b = conv_pre(jb, slice(0, both), tb_ref[...], pos, count)
    sig_b = sig(pre_b)
    bc = pre_b * sig_b
    b_low = bc[:, :states].astype(bf16)
    c_low = bc[:, states:].astype(bf16)
    pre_dt, dt, la, summed = decay_parts(proj_ref[:, inner + both :], head_row, pos, heads)
    rows = jnp.transpose(summed)
    row = lax.broadcasted_iota(jnp.int32, (count, count), 0)
    col = lax.broadcasted_iota(jnp.int32, (count, count), 1)
    marks = summed[:, LANES - 1 : LANES]
    valid = (row <= col) & (marks == rows[LANES - 1 : LANES, :])
    scores = dot_nt(b_low, c_low)
    last = summed[count - 1 : count, :]
    carry = jnp.exp(last) * (last[:, LANES - 1 : LANES] == 0.0).astype(f32)
    same = (marks == last[:, LANES - 1 : LANES]).astype(f32)
    first = (marks == 0.0).astype(f32)
    low_half = lane_ids((count, LANES)) < HD
    low_row = low_half[0:1, :]
    lane = lane_ids((LANES, LANES))
    lane_row = lax.broadcasted_iota(jnp.int32, (LANES, LANES), 0)
    d_scores = jnp.zeros((count, count), f32)
    d_b = jnp.zeros((count, states), f32)
    d_c = jnp.zeros((count, states), f32)
    d_sum = jnp.zeros((count, LANES), f32)
    d_dt = jnp.zeros((count, LANES), f32)
    d_rows = jnp.zeros((8, LANES), f32)
    ax[...] = jnp.zeros_like(ax)
    ab[...] = jnp.zeros_like(ab)
    for j in range(heads // 2):
        span = slice(j * LANES, (j + 1) * LANES)
        taps = tx_ref[:, span]
        pre = conv_pre(jx, span, taps, pos, count)
        sg = sig(pre)
        xc = pre * sg
        dt_wide = pair(dt, j, low_half)
        u = xc * dt_wide
        u_low = u.astype(bf16)
        dy = dy_ref[:, span]
        dy_low = dy.astype(bf16)
        state = st_ref[0, :, span]
        later = chained_state(packs, span, states)
        d_state = later.astype(bf16)
        results = []
        for i, h in enumerate((2 * j, 2 * j + 1)):
            differ = rows[h : h + 1, :] - summed[:, h : h + 1]
            decay = jnp.exp(jnp.where(valid, differ, -1e30))
            half = low_half if i == 0 else jnp.logical_not(low_half)
            u_half = jnp.where(half, u, 0.0).astype(bf16)
            d_scores = d_scores + decay * dot_nt(u_half, dy_low)
            results.append(dot((decay * scores).astype(bf16), dy_low))
        left = jnp.exp(pair(last, j, low_row) - pair(summed, j, low_half)) * same
        reads = jnp.exp(pair(summed, j, low_half)) * first
        du_end = left * dot(b_low, d_state)
        du_in = jnp.where(low_half, results[0], results[1])
        du = du_in + du_end
        d_c = d_c + dot_nt((reads * dy).astype(bf16), state)
        d_b = d_b + dot_nt((left * u).astype(bf16), d_state)
        skip = pair(head_row[2:3, :], j, low_row)
        chosen = (
            ((lane == 2 * j) & (lane_row < HD)) | ((lane == 2 * j + 1) & (lane_row >= HD))
        ).astype(f32)
        per_token = (
            dy_low.astype(f32) * (y_ref[:, span] - skip * xc)
            - u_low.astype(f32) * du_in
            - u * du_end
        )
        d_sum = d_sum + jnp.dot(per_token, chosen, precision=highest, preferred_element_type=f32)
        d_dt = d_dt + jnp.dot(du * xc, chosen, precision=highest, preferred_element_type=f32)
        sums = jnp.concatenate(
            [
                jnp.sum(u * du_end, axis=0, keepdims=True),
                jnp.sum(dy * xc, axis=0, keepdims=True),
                jnp.sum(later * state.astype(f32), axis=0, keepdims=True),
                jnp.zeros((5, LANES), f32),
            ],
            axis=0,
        )
        d_rows = d_rows + jnp.dot(sums, chosen, precision=highest, preferred_element_type=f32)
        d_pre = (du * dt_wide + skip * dy) * (sg * (1.0 + pre * (1.0 - sg)))
        for k in range(KC):
            masked = d_pre * (pos >= k).astype(f32) if k else d_pre
            gtx_ref[0, k : k + 1, span] = jnp.sum(
                masked * jx[TAIL - k : TAIL - k + count, span], axis=0, keepdims=True
            )
            ax[TAIL - k : TAIL - k + count, span] += taps[k : k + 1, :] * masked
    main_ref[:, :inner] = ax[TAIL:, :].astype(bf16)
    side_ref[:, :inner] = ax[:TAIL, :].astype(bf16)
    d_b = d_b + dot(d_scores.astype(bf16), c_low)
    d_c = d_c + dot(jnp.transpose(d_scores).astype(bf16), b_low)
    d_pre = jnp.concatenate([d_b, d_c], axis=1) * (sig_b * (1.0 + pre_b * (1.0 - sig_b)))
    for k in range(KC):
        masked = d_pre * (pos >= k).astype(f32) if k else d_pre
        gtb_ref[0, k : k + 1, :] = jnp.sum(
            masked * jb[TAIL - k : TAIL - k + count, :], axis=0, keepdims=True
        )
        ab[TAIL - k : TAIL - k + count, :] += tb_ref[k : k + 1, :] * masked
    main_ref[:, inner : inner + both] = ab[TAIL:, :].astype(bf16)
    side_ref[:, inner : inner + both] = ab[:TAIL, :].astype(bf16)
    token = lax.broadcasted_iota(jnp.int32, (count, LANES), 0)
    at_last = d_rows[0:1, :] + d_rows[2:3, :] * carry
    d_sum = d_sum + jnp.where(token == count - 1, at_last, 0.0)
    upper = (row <= col).astype(f32)
    d_la = jnp.dot(upper, d_sum, precision=highest, preferred_element_type=f32)
    d_la = jnp.where(lane_ids(d_la.shape) < heads, d_la, 0.0)
    d_dt = d_dt - jnp.exp(head_row[0:1, :]) * d_la
    d_dtr = d_dt * sig(pre_dt)
    d_dtr = jnp.where(lane_ids(d_dtr.shape) < heads, d_dtr, 0.0)
    main_ref[:, inner + both :] = d_dtr.astype(bf16)
    side_ref[:, inner + both :] = jnp.zeros((TAIL, LANES), bf16)
    gh_ref[0, 0:1, :] = jnp.sum(d_la * la, axis=0, keepdims=True)
    gh_ref[0, 1:2, :] = jnp.sum(d_dtr, axis=0, keepdims=True)
    gh_ref[0, 2:3, :] = d_rows[1:2, :]
    gh_ref[0, 3:8, :] = jnp.zeros((5, LANES), f32)


def mixer_back(
    number, made, proj, taps_x, taps_bc, head_row, pos, dy, y, state, packs, extra, heads, seqs, count
):
    inner, both = taps_x.shape[1], taps_bc.shape[1]
    width = proj.shape[1]
    outs = [
        jax.ShapeDtypeStruct((seqs * count, width), bf16),
        jax.ShapeDtypeStruct((seqs * TAIL, width), bf16),
        jax.ShapeDtypeStruct((1, KC, inner), f32),
        jax.ShapeDtypeStruct((1, KC, both), f32),
        jax.ShapeDtypeStruct((1, 8, LANES), f32),
    ]

    def rows_of(a, rows, block):
        return pl.BlockSpec((rows, a.shape[1]), lambda i: (block, 0))

    def seq_of(a):
        return pl.BlockSpec((1,) + a.shape[1:], lambda i: (number,) + (0,) * (a.ndim - 1))

    extra = list(made) + list(extra)
    first = 9 + len(packs)
    return pl.pallas_call(
        functools.partial(mixer_back_kernel, heads, inner, both, len(packs), len(extra)),
        grid=(1,),
        out_shape=outs,
        in_specs=[
            rows_of(proj, count, number),
            rows_of(proj, TAIL, seqs * count // TAIL + number),
            spec_whole(taps_x), spec_whole(taps_bc), spec_whole(head_row),
            rows_of(pos, count, number), rows_of(dy, count, number), rows_of(y, count, number),
            seq_of(state),
        ]
        + [seq_of(p) for p in packs]
        + [spec_any()] * len(extra),
        out_specs=[rows_of(outs[0], count, number), rows_of(outs[1], TAIL, number)]
        + [spec_seq(o) for o in outs[2:]],
        scratch_shapes=[
            pltpu.VMEM((count + TAIL, inner), f32),
            pltpu.VMEM((count + TAIL, both), f32),
            pltpu.VMEM((count + TAIL, inner), f32),
            pltpu.VMEM((count + TAIL, both), f32),
        ],
        input_output_aliases={first: 0, first + 1: 1} if made else {},
        compiler_params=params(),
        cost_estimate=cost(9),
        name="mixer_back",
    )(proj, proj, taps_x, taps_bc, head_row, pos, dy, y, state, *packs, *extra)


def half_turned(v):
    first = lane_ids(v.shape) % HD < HD // 2
    return jnp.where(
        first, -pltpu.roll(v, LANES - HD // 2, 1), pltpu.roll(v, HD // 2, 1)
    )


def rope_kernel(qwidth, qz_ref, cos_ref, sin_ref, q_ref, kv_ref):
    cosine, sine = cos_ref[...], sin_ref[...]
    for j in range(qwidth // LANES):
        v = qz_ref[:, j * LANES : (j + 1) * LANES]
        q_ref[:, j * LANES : (j + 1) * LANES] = (v * cosine + half_turned(v) * sine).astype(bf16)
    v = qz_ref[:, qwidth : qwidth + LANES]
    turned = v * cosine + half_turned(v) * sine
    kv_ref[...] = jnp.where(lane_ids(v.shape) < HD, turned, v).astype(bf16)


def rope(qz, cosine, sine, qwidth, seqs, count):
    outs = [
        jax.ShapeDtypeStruct((seqs * count, qwidth), bf16),
        jax.ShapeDtypeStruct((seqs * count, 2 * HD), bf16),
    ]
    return pl.pallas_call(
        functools.partial(rope_kernel, qwidth),
        grid=(seqs,),
        out_shape=outs,
        in_specs=[
            pl.BlockSpec((count, qwidth + LANES), lambda s: (s, 0)),
            spec_rows(cosine, count), spec_rows(sine, count),
        ],
        out_specs=[spec_rows(o, count) for o in outs],
        compiler_params=params(),
        cost_estimate=cost(2),
        name="rope",
    )(qz, cosine, sine)


def to_low(v, r, low_half):
    v = v.astype(f32)
    return jnp.where(low_half, v if r % 2 == 0 else pltpu.roll(v, HD, 1), 0.0)


def to_high(v, r, low_half):
    v = v.astype(f32)
    return jnp.where(low_half, 0.0, v if r % 2 else pltpu.roll(v, HD, 1))


def key_masks(pos, count, blocks):
    row = lax.broadcasted_iota(jnp.int32, (count, count), 0)
    col = lax.broadcasted_iota(jnp.int32, (count, count), 1)
    start = row - pos
    masks = []
    for d in range(blocks):
        mask = col - d * count >= start
        masks.append(mask & (col <= row) if d == 0 else mask)
    return masks


def attend_kernel(per_group, blocks, q_ref, pos_ref, *refs):
    kv = refs[:blocks]
    o_ref, lse_ref = refs[blocks:]
    count = q_ref.shape[0]
    masks = key_masks(pos_ref[...], count, blocks)
    low_half = lane_ids((count, LANES)) < HD
    lane = lane_ids((count, LANES))
    lse = jnp.zeros((count, LANES), f32)
    halves = []
    for r in range(per_group):
        span = slice(r // 2 * LANES, (r // 2 + 1) * LANES)
        q = to_low(q_ref[:, span], r, low_half).astype(bf16)
        scores = [
            jnp.where(masks[d], dot_nt(q, kv[d][...]) * 0.125, -1e30) for d in range(blocks)
        ]
        top = jnp.max(scores[0], axis=1, keepdims=True)
        for d in range(1, blocks):
            top = jnp.maximum(top, jnp.max(scores[d], axis=1, keepdims=True))
        weights = [jnp.exp(v - top) for v in scores]
        total = jnp.sum(weights[0], axis=1, keepdims=True)
        for d in range(1, blocks):
            total = total + jnp.sum(weights[d], axis=1, keepdims=True)
        scale = 1.0 / total
        out = dot((weights[0] * scale).astype(bf16), kv[0][...])
        for d in range(1, blocks):
            out = out + dot((weights[d] * scale).astype(bf16), kv[d][...])
        lse = jnp.where(lane == r, top + jnp.log(total), lse)
        halves.append(out)
        if r % 2:
            o_ref[:, span] = jnp.where(low_half, pltpu.roll(halves[r - 1], HD, 1), out).astype(bf16)
    lse_ref[...] = lse


def attend(q, pos, kv, seqs, count):
    per_group = q.shape[1] // HD
    outs = [
        jax.ShapeDtypeStruct(q.shape, bf16),
        jax.ShapeDtypeStruct((q.shape[0], LANES), f32),
    ]
    return pl.pallas_call(
        functools.partial(attend_kernel, per_group, len(kv)),
        grid=(seqs,),
        out_shape=outs,
        in_specs=[spec_rows(a, count) for a in (q, pos, *kv)],
        out_specs=[spec_rows(o, count) for o in outs],
        compiler_params=params(),
        cost_estimate=cost(8),
        name="attend",
    )(q, pos, *kv)


def attend_back_kernel(per_group, blocks, q_ref, pos_ref, do_ref, lse_ref, cos_ref, sin_ref, *refs):
    kv = refs[:blocks]
    dq_ref = refs[blocks]
    dkv = refs[blocks + 1 :]
    count = q_ref.shape[0]
    masks = key_masks(pos_ref[...], count, blocks)
    low_half = lane_ids((count, LANES)) < HD
    cosine, sine = cos_ref[...], sin_ref[...]
    totals = [jnp.zeros((LANES, count), f32) for _ in range(blocks)]
    halves = []
    for r in range(per_group):
        span = slice(r // 2 * LANES, (r // 2 + 1) * LANES)
        q = to_low(q_ref[:, span], r, low_half)
        do = to_high(do_ref[:, span], r, low_half)
        q_turned = (jnp.transpose(q) * 0.125).astype(bf16)
        do_turned = jnp.transpose(do).astype(bf16)
        q, do = q.astype(bf16), do.astype(bf16)
        lse = lse_ref[:, r : r + 1]
        probs, d_probs = [], []
        row_dot = None
        for d in range(blocks):
            scores = jnp.where(masks[d], dot_nt(q, kv[d][...]) * 0.125, -1e30)
            probs.append(jnp.exp(scores - lse))
            d_probs.append(dot_nt(do, kv[d][...]))
            part = jnp.sum(probs[d] * d_probs[d], axis=1, keepdims=True)
            row_dot = part if row_dot is None else row_dot + part
        dq = None
        for d in range(blocks):
            d_scores = (probs[d] * (d_probs[d] - row_dot)).astype(bf16)
            part = dot(d_scores, kv[d][...])
            dq = part if dq is None else dq + part
            totals[d] = (
                totals[d] + dot(q_turned, d_scores) + dot(do_turned, probs[d].astype(bf16))
            )
        halves.append(dq * 0.125)
        if r % 2:
            both = jnp.where(low_half, halves[r - 1], pltpu.roll(halves[r], HD, 1))
            dq_ref[:, span] = (both * cosine - half_turned(both) * sine).astype(bf16)
    for d in range(blocks):
        dkv[d][...] = jnp.transpose(totals[d]).astype(dkv[d].dtype)


def attend_back(q, pos, d_out, lse, cosine, sine, kv, seqs, count):
    per_group = q.shape[1] // HD
    outs = [jax.ShapeDtypeStruct(q.shape, bf16)] + [
        jax.ShapeDtypeStruct(kv[0].shape, bf16 if d else f32) for d in range(len(kv))
    ]
    args = (q, pos, d_out, lse, cosine, sine, *kv)
    return pl.pallas_call(
        functools.partial(attend_back_kernel, per_group, len(kv)),
        grid=(seqs,),
        out_shape=outs,
        in_specs=[spec_rows(a, count) for a in args],
        out_specs=[spec_rows(o, count) for o in outs],
        compiler_params=params(),
        cost_estimate=cost(14),
        name="attend_back",
    )(*args)


def join_back_kernel(pieces, dq_ref, dz_ref, cos_ref, sin_ref, *refs):
    out_ref = refs[-1]
    qwidth = dq_ref.shape[1]
    total = refs[0][...].astype(f32)
    for piece in refs[1:pieces]:
        total = total + piece[...].astype(f32)
    turned = total * cos_ref[...] - half_turned(total) * sin_ref[...]
    out_ref[:, :qwidth] = dq_ref[...]
    out_ref[:, qwidth : qwidth + LANES] = jnp.where(
        lane_ids(total.shape) < HD, turned, total
    ).astype(bf16)
    out_ref[:, qwidth + LANES :] = dz_ref[...]


def join_back(dq, dz, cosine, sine, pieces, extra, seqs, count):
    out = jax.ShapeDtypeStruct((dq.shape[0], dq.shape[1] + LANES + dz.shape[1]), bf16)
    args = (dq, dz, cosine, sine, *pieces)
    return pl.pallas_call(
        functools.partial(join_back_kernel, len(pieces)),
        grid=(seqs,),
        out_shape=out,
        in_specs=[spec_rows(a, count) for a in args] + [spec_any()] * len(extra),
        out_specs=spec_rows(out, count),
        compiler_params=params(),
        cost_estimate=cost(2),
        name="join_back",
    )(*args, *extra)


def attend_one(q, k, v, mask):
    scores = jnp.einsum("qrd,kd->rqk", q, k, preferred_element_type=f32) * 0.125
    scores = jnp.where(mask[None], scores, -1e30)
    top = jnp.max(scores, axis=-1, keepdims=True)
    weights = jnp.where(mask[None], jnp.exp(scores - top), 0.0)
    total = jnp.sum(weights, axis=-1, keepdims=True)
    out = jnp.einsum("rqk,kd->qrd", (weights / total).astype(bf16), v, preferred_element_type=f32)
    return out, jnp.transpose((top + jnp.log(total))[..., 0])


def attend_one_back(q, k, v, mask, d_out, lse):
    scores = jnp.einsum("qrd,kd->rqk", q, k, preferred_element_type=f32) * 0.125
    probs = jnp.where(mask[None], jnp.exp(scores - jnp.transpose(lse)[..., None]), 0.0)
    d_probs = jnp.einsum("qrd,kd->rqk", d_out, v, preferred_element_type=f32)
    row_dot = jnp.sum(probs * d_probs, axis=-1, keepdims=True)
    d_scores = (probs * (d_probs - row_dot)).astype(bf16)
    d_q = jnp.einsum("rqk,kd->qrd", d_scores, k, preferred_element_type=f32) * 0.125
    d_k = jnp.einsum("rqk,qrd->kd", d_scores, q, preferred_element_type=f32) * 0.125
    d_v = jnp.einsum("rqk,qrd->kd", probs.astype(bf16), d_out, preferred_element_type=f32)
    return d_q, jnp.concatenate([d_k, d_v], axis=-1)


class Attention:
    def __init__(self, q, kv, pos, seqs, count):
        self.q, self.pos, self.seqs, self.count = q, pos, seqs, count
        self.blocks = lax.axis_size("ctx")
        self.few = self.blocks <= 4
        if self.few:
            self.kv = [kv] + [shifted(kv, "ctx", d) for d in range(1, self.blocks)]
            return
        me = lax.axis_index("ctx")
        shaped = lax.all_gather(kv.reshape(seqs, count, -1), "ctx", axis=1, tiled=True)
        self.all_kv = shaped
        keys = jnp.arange(shaped.shape[1])
        tokens = me * count + jnp.arange(count)
        starts = tokens[None, :] - pos.reshape(seqs, count)
        self.mask = (keys[None, None, :] <= tokens[None, :, None]) & (
            keys[None, None, :] >= starts[:, :, None]
        )

    def heads_of(self, v):
        return v.reshape(self.seqs, self.count, -1, HD)

    def forward(self):
        if self.few:
            out, self.lse = attend(self.q, self.pos, self.kv, self.seqs, self.count)
            return out
        keys, values = self.all_kv[..., :HD], self.all_kv[..., HD:]
        out, self.lse = lax.map(
            lambda a: attend_one(*a), (self.heads_of(self.q), keys, values, self.mask)
        )
        return out.astype(bf16).reshape(self.q.shape)

    def backward(self, d_out, cosine, sine):
        if self.few:
            dq, own, *rest = attend_back(
                self.q, self.pos, d_out, self.lse, cosine, sine, self.kv, self.seqs, self.count
            )
            return dq, [own] + [
                shifted(piece, "ctx", -d) for d, piece in enumerate(rest, start=1)
            ]
        keys, values = self.all_kv[..., :HD], self.all_kv[..., HD:]
        dq, kept = lax.map(
            lambda a: attend_one_back(*a),
            (self.heads_of(self.q), keys, values, self.mask, self.heads_of(d_out), self.lse),
        )
        dq = dq.reshape(self.q.shape)
        cos_q = jnp.tile(cosine, (1, dq.shape[1] // LANES))
        sin_q = jnp.tile(sine, (1, dq.shape[1] // LANES))
        dq = dq * cos_q - jnp.dot(dq, turn_matrix(dq.shape[1]), precision=highest) * sin_q
        total = lax.psum_scatter(kept.astype(bf16), "ctx", scatter_dimension=1, tiled=True)
        return dq.astype(bf16), [total.astype(f32).reshape(-1, 2 * HD)]


def turn_matrix(columns):
    source = jnp.arange(columns)[:, None]
    target = jnp.arange(columns)[None, :]
    half = HD // 2
    low = target % HD < half
    minus = low & (source == target + half)
    plus = jnp.logical_not(low) & (source == target - half)
    return plus.astype(f32) - minus.astype(f32)


def per_device(
    hidden_in,
    positions,
    gain_attn,
    w_qkv,
    w_attn_out,
    w_zx,
    w_bc,
    w_dt,
    conv_x,
    conv_bc,
    a_log,
    dt_bias,
    d_skip,
    w_mamba_out,
    gain_ffn,
    w_gu,
    w_down,
    output_cotangent,
):
    seqs, block = positions.shape
    features = hidden_in.shape[2]
    rows = w_qkv.shape[0]
    heads = a_log.shape[0]
    inner = w_zx.shape[2]
    both = w_bc.shape[1]
    columns = w_qkv.shape[2]
    qwidth = columns - 2 * HD
    units = w_gu.shape[2]
    count = lax.axis_size("ctx")
    place = lax.axis_index("ctx")
    here = seqs * block

    pad = jnp.zeros((rows, LANES - heads - 2), bf16)
    first_pack = jnp.concatenate(
        [w_zx[:, 1, :], w_bc, w_dt, gain_attn[:, None], gain_ffn[:, None], pad], axis=1
    )
    tail = shifted(hidden_in[:, block - TAIL :, :], "ctx", 1)
    down = w_down.T
    half = units // 2
    pos = positions.reshape(here, 1)
    frequency = jnp.power(jnp.float32(rope_base), -jnp.arange(0, HD, 2).astype(f32) / HD)
    turned = pos.astype(f32) * jnp.tile(frequency, 2 * LANES // HD)
    cosine, sine = jnp.cos(turned), jnp.sin(turned)

    x_own = hidden_in.reshape(here, features).astype(f32)
    x_ext = jnp.concatenate([x_own, tail.reshape(seqs * TAIL, features).astype(f32)], axis=0)
    r_ext = lax.rsqrt(jnp.mean(x_ext * x_ext, axis=-1, keepdims=True) + 1e-05)
    r_one = r_ext[:here]
    taps_x = conv_x.astype(f32)
    taps_bc = conv_bc.astype(f32)
    head_row = jnp.pad(
        jnp.stack([a_log, dt_bias, d_skip]), ((0, 5), (0, LANES - heads))
    )

    def with_first(w_one):
        gain_a = w_one[:, inner + both + heads].astype(f32)
        h_ext = (x_ext * r_ext * gain_a).astype(bf16)
        proj = dot(h_ext, w_one)
        local = mixer_local(proj, taps_x, taps_bc, head_row, pos, heads, seqs, block)
        return w_one, gain_a, h_ext, proj, local, local[1]

    made, w_two, w_three, w_four, w_five, nears = gather_all(
        first_pack,
        ([w_qkv[:, 0, :], w_zx[:, 0, :]], [w_attn_out.T, w_mamba_out.T]),
        (
            [(w_gu[:, 0, :], 0, 0), (down[:, :half], 1, 0)],
            [(w_gu[:, 1, :], 0, units), (down[:, half:], 1, half)],
        ),
        with_first,
    )
    w_one, gain_a, h_ext, proj, (y_local, pack, c_vec, summed), _ = made
    gain_f = w_one[:, inner + both + heads + 1].astype(f32)
    h_own = h_ext[:here]
    packs = chain_pieces(pack, False)

    qz = dot(h_own, w_two)
    q_low, kv_low = rope(qz, cosine, sine, qwidth, seqs, block)
    attention = Attention(q_low, kv_low, pos, seqs, block)
    attended = attention.forward()

    y, mixer_out, state = mixer_read(
        y_local, c_vec, summed, qz, attended, packs, nears, heads, seqs, block, columns
    )
    resid = x_own + pair_sum(dot_nt(mixer_out, w_three))

    r_two = lax.rsqrt(jnp.mean(resid * resid, axis=-1, keepdims=True) + 1e-05)
    h_two = (resid * r_two * gain_f).astype(bf16)
    gate_up = dot(h_two, w_four)
    gate_ff, up_ff = gate_up[:, :units], gate_up[:, units:]
    sig_ff = jax.nn.sigmoid(gate_ff)
    silu_ff = gate_ff * sig_ff
    hidden_state = (silu_ff * up_ff).astype(bf16)
    ffn = pair_sum(dot_nt(hidden_state, w_five))
    block_out = (resid + ffn).astype(bf16).reshape(seqs, block, features)

    e_low = output_cotangent.reshape(here, features)
    d_hidden_state = dot(e_low, w_five)
    d_gate_up = jnp.concatenate(
        [
            d_hidden_state * up_ff * (sig_ff * (1.0 + gate_ff * (1.0 - sig_ff))),
            d_hidden_state * silu_ff,
        ],
        axis=1,
    ).astype(bf16)

    def tn(a, b):
        return lax.dot_general(a, b, (((0,), (0,)), ((), ())), preferred_element_type=f32)

    d_h_two_part = dot_nt(d_gate_up, w_four).astype(bf16)
    d_h_two = pair_sum(d_h_two_part)
    g_four, g_five = tn(h_two, d_gate_up).astype(bf16), tn(e_low, hidden_state).astype(bf16)
    ffn_sum = Scatter(
        [[g_four[:, :units], g_five[:, :half]], [g_four[:, units:], g_five[:, half:]]]
    )
    grad_gain_f = jnp.sum(d_h_two_part.astype(f32) * resid * r_two, axis=0)
    scaled = d_h_two * gain_f
    d_resid = (
        e_low.astype(f32)
        + r_two * scaled
        - resid * (r_two * r_two * r_two) * jnp.mean(resid * scaled, axis=-1, keepdims=True)
    )
    d_mix = d_resid.astype(bf16)

    d_mixer = dot(d_mix, w_three)
    d_y, d_z, d_att, d_pack = gate_back(
        d_mixer, y, qz, c_vec, summed, heads, seqs, block, columns, qwidth
    )
    later_packs = chain_pieces(d_pack, True)
    d_q, d_kv = attention.backward(d_att, cosine, sine)
    d_two = join_back(d_q, d_z, cosine, sine, d_kv, ffn_sum.got, seqs, block)
    two_sum = Scatter([[tn(h_own, d_two).astype(bf16)], [tn(d_mix, mixer_out).astype(bf16)]])
    ffn_sum.second()
    ffn_sum.third()
    d_main, d_side, small_grads = None, None, []
    for number in range(seqs):
        extra = []
        if number == 0:
            extra = ffn_sum.near
        if number == seqs - 1:
            extra = ffn_sum.along + two_sum.got
        d_main, d_side, *rest = mixer_back(
            number, (d_main, d_side) if number else (), proj, taps_x, taps_bc, head_row, pos,
            d_y, y, state, later_packs, extra, heads, seqs, block,
        )
        small_grads.append(rest)
    g_taps_x, g_taps_bc, g_heads = [sum(g[i] for g in small_grads) for i in range(3)]
    two_sum.second()
    one_sum = Scatter([[(tn(h_own, d_main) + tn(h_ext[here:], d_side)).astype(bf16)]])
    two_sum.third()
    one_sum.third()
    ffn_grads, two_grads, one_grads = ffn_sum.result(), two_sum.result(), one_sum.result()
    ffn_gate, ffn_up = ffn_grads[:, :units], ffn_grads[:, units + half : 2 * units + half]
    ffn_down = jnp.concatenate(
        [ffn_grads[:, units : units + half], ffn_grads[:, 2 * units + half :]], axis=1
    )

    d_tail = dot_nt(d_side, w_one)
    d_h_part = (dot_nt(d_two, w_two) + dot_nt(d_main, w_one)).astype(bf16)
    grad_gain_a = jnp.sum(d_h_part.astype(f32) * x_own * r_one, axis=0) + jnp.sum(
        d_tail * x_ext[here:] * r_ext[here:], axis=0
    )
    d_tail = shifted(pair_sum(d_tail).astype(bf16), "ctx", -1).astype(f32)
    d_h = pair_sum(d_h_part).reshape(seqs, block, features)
    d_h = d_h + jnp.pad(d_tail.reshape(seqs, TAIL, features), ((0, 0), (block - TAIL, 0), (0, 0)))
    d_h = d_h.reshape(here, features)
    scaled = d_h * gain_a
    d_hidden = (
        d_resid
        + r_one * scaled
        - x_own * (r_one * r_one * r_one) * jnp.mean(x_own * scaled, axis=-1, keepdims=True)
    )
    d_hidden = d_hidden.astype(bf16).reshape(seqs, block, features)

    over_pair = jnp.concatenate(
        [grad_gain_a, jnp.sum(g_taps_bc, axis=0).reshape(-1), grad_gain_f]
    )
    over_pair = sum_all(over_pair, ("tp",))
    over_rest = jnp.concatenate(
        [
            jnp.sum(g_taps_x, axis=0).reshape(-1),
            jnp.sum(g_heads, axis=0)[:3, :heads].reshape(-1),
            over_pair,
        ]
    )
    total = sum_all(over_rest, ("dp", "ctx"))
    sizes = (KC * inner, heads, heads, heads, features, KC * both, features)
    small, first = [], 0
    for size in sizes:
        small.append(total[first : first + size])
        first += size
    g_tx, g_decay, g_bias, g_skip, g_gain_a, g_tb, g_gain_f = small
    shard = lax.axis_index("dp") * count + place

    def own_rows(vector):
        return lax.dynamic_slice_in_dim(vector, shard * rows, rows, 0)

    bc_grad = one_grads[:, inner : inner + both]
    bc_grad = sum_all(bc_grad, ("tp",))
    zx_grad = jnp.stack(
        [two_grads[:, columns : columns + inner], one_grads[:, :inner]], axis=1
    )
    return (
        block_out,
        d_hidden,
        own_rows(g_gain_a),
        two_grads[:, None, :columns],
        two_grads[:, columns + inner : columns + inner + qwidth].T,
        zx_grad,
        bc_grad,
        one_grads[:, inner + both : inner + both + heads],
        g_tx.reshape(KC, inner),
        g_tb.reshape(KC, both),
        g_decay,
        g_bias,
        g_skip,
        two_grads[:, columns + inner + qwidth :].T,
        own_rows(g_gain_f),
        jnp.stack([ffn_gate, ffn_up], axis=1),
        ffn_down.T,
    )


def solution(mesh):
    in_specs = (
        P("dp", "ctx", None),
        P("dp", "ctx"),
        P(("dp", "ctx")),
        P(("dp", "ctx"), "tp", None),
        P("tp", ("dp", "ctx")),
        P(("dp", "ctx"), None, "tp"),
        P(("dp", "ctx"), None),
        P(("dp", "ctx"), "tp"),
        P(None, "tp"),
        P(),
        P("tp"),
        P("tp"),
        P("tp"),
        P("tp", ("dp", "ctx")),
        P(("dp", "ctx")),
        P(("dp", "ctx"), None, "tp"),
        P("tp", ("dp", "ctx")),
        P("dp", "ctx", None),
    )
    out_specs = (
        P("dp", "ctx", None),
        P("dp", "ctx", None),
        P(("dp", "ctx")),
        P(("dp", "ctx"), "tp", None),
        P("tp", ("dp", "ctx")),
        P(("dp", "ctx"), None, "tp"),
        P(("dp", "ctx"), None),
        P(("dp", "ctx"), "tp"),
        P(None, "tp"),
        P(),
        P("tp"),
        P("tp"),
        P("tp"),
        P("tp", ("dp", "ctx")),
        P(("dp", "ctx")),
        P(("dp", "ctx"), None, "tp"),
        P("tp", ("dp", "ctx")),
    )
    return jax.shard_map(
        per_device, mesh=mesh, in_specs=in_specs, out_specs=out_specs, check_vma=False
    )
```

```python
import functools

import jax
import jax.numpy as jnp
from jax import lax
from jax.experimental import pallas as pl
from jax.experimental.pallas import tpu as pltpu
from jax.sharding import PartitionSpec as P

HD = 64
KC = 4
TAIL = 16
LANES = 128
VMEM_LIMIT = 56 * 1024 * 1024
SMALL = 64

f32 = jnp.float32
bf16 = jnp.bfloat16
highest = lax.Precision.HIGHEST
rope_base = 100000000000.0


def small_mesh():
    return lax.axis_size("dp") == 4 and lax.axis_size("ctx") == 4


def swap(value, axis, bits):
    count = lax.axis_size(axis)
    return lax.ppermute(value, axis, [(i, i ^ bits) for i in range(count)])


def shifted(value, axis, distance):
    count = lax.axis_size(axis)
    route = [(i - distance, i) for i in range(count) if 0 <= i - distance < count]
    return lax.ppermute(value, axis, route)


def place_blocks(pieces, outs, copies):
    count = len(pieces)
    total = len(outs)
    where = jnp.stack([lax.axis_index("dp"), lax.axis_index("ctx")]).astype(jnp.int32)

    def kernel(where_ref, *refs):
        ins = refs[:count]
        outputs = refs[count : count + total]
        sems = refs[count + total]
        running = []
        for number, (piece, first, width, out, axis, bits, to) in enumerate(copies):
            target = outputs[out]
            if axis is None:
                target = target.at[:, pl.ds(to, width)]
            else:
                target = target.at[jnp.bitwise_xor(where_ref[axis], bits), :, pl.ds(to, width)]
            copy = pltpu.make_async_copy(
                ins[piece].at[:, pl.ds(first, width)], target, sems.at[number]
            )
            copy.start()
            running.append(copy)
        for copy in running:
            copy.wait()

    return pl.pallas_call(
        kernel,
        out_shape=[jax.ShapeDtypeStruct(shape, pieces[0].dtype) for shape in outs],
        in_specs=[pl.BlockSpec(memory_space=pltpu.SMEM)]
        + [pl.BlockSpec(memory_space=pl.ANY)] * count,
        out_specs=[pl.BlockSpec(memory_space=pltpu.VMEM)] * total,
        scratch_shapes=[pltpu.SemaphoreType.DMA((len(copies),))],
        compiler_params=pltpu.CompilerParams(vmem_limit_bytes=VMEM_LIMIT),
        name="place_blocks",
    )(where, *pieces)


class Placing:
    def __init__(self):
        self.pieces, self.outs, self.copies = [], [], []

    def out(self, *shape):
        self.outs.append(shape)
        return len(self.outs) - 1

    def add(self, piece, out, axis=None, bits=0, to=0, first=0, width=None):
        for number, known in enumerate(self.pieces):
            if known is piece:
                break
        else:
            number = len(self.pieces)
            self.pieces.append(piece)
        width = piece.shape[1] if width is None else width
        self.copies.append((number, first, width, out, axis, bits, to))

    def after(self, *arrays):
        self.pieces.extend(arrays)

    def run(self):
        return place_blocks(self.pieces, self.outs, self.copies)


def along_ctx(packed):
    return [packed] + [swap(packed, "ctx", k) for k in (1, 2, 3)]


def along_dp(held, one, two):
    near = swap(held, "dp", one)
    return [(0, held), (one, near), (two, swap(held, "dp", two)), (3, swap(near, "dp", two))]


def gather_all(first, second, third, with_first):
    rows = first.shape[0]
    if not small_mesh():
        def whole(piece):
            return lax.all_gather(piece, ("dp", "ctx"), axis=0, tiled=True)

        w_two, w_three = [whole(jnp.concatenate(p, axis=1)) for p in second]
        w_four, w_five = [
            whole(
                jnp.concatenate(
                    [p for p, out, _ in sorted(third[0] + third[1], key=lambda t: t[2]) if out == o],
                    axis=1,
                )
            )
            for o in (0, 1)
        ]
        return with_first(whole(first)), w_two, w_three, w_four, w_five, []

    def flat(held):
        return held.reshape(held.shape[0] * held.shape[1], held.shape[2])

    wide_one = first.shape[1]
    wide_two = [sum(p.shape[1] for p in part) for part in second]
    wide_half = [sum(p.shape[1] for p, _, _ in half) for half in third]
    work = Placing()
    held_out = work.out(4, rows, wide_one)
    pack_out = work.out(rows, sum(wide_two))
    for k, piece in enumerate(along_ctx(first)):
        work.add(piece, held_out, 1, k)
    to = 0
    for piece in second[0] + second[1]:
        work.add(piece, pack_out, to=to)
        to += piece.shape[1]
    held_one, packed_two = work.run()
    held_one = flat(held_one)
    work = Placing()
    full = work.out(4, 4 * rows, wide_one)
    held_out = [work.out(4, rows, w) for w in wide_two]
    pack_out = work.out(rows, sum(wide_half))
    for k in range(4):
        work.add(held_one if k == 0 else swap(held_one, "dp", k), full, 0, k)
    for k, piece in enumerate(along_ctx(packed_two)):
        work.add(piece, held_out[0], 1, k, width=wide_two[0])
        work.add(piece, held_out[1], 1, k, first=wide_two[0], width=wide_two[1])
    to = 0
    for piece, _, _ in third[0] + third[1]:
        work.add(piece, pack_out, to=to)
        to += piece.shape[1]
    w_one, held_a, held_b, packed_three = work.run()
    made = with_first(flat(w_one))
    work = Placing()
    fulls = [work.out(4, 4 * rows, w) for w in wide_two]
    held_out = [work.out(4, rows, w) for w in wide_half]
    for bits, piece in along_dp(flat(held_a), 1, 2):
        work.add(piece, fulls[0], 0, bits)
    for bits, piece in along_dp(flat(held_b), 2, 1):
        work.add(piece, fulls[1], 0, bits)
    for k, piece in enumerate(along_ctx(packed_three)):
        work.add(piece, held_out[0], 1, k, width=wide_half[0])
        work.add(piece, held_out[1], 1, k, first=wide_half[0], width=wide_half[1])
    work.after(made[-1])
    w_two, w_three, held_a, held_b = work.run()
    work = Placing()
    ends = [0, 0]
    for part in third[0] + third[1]:
        ends[part[1]] += part[0].shape[1]
    fulls = [work.out(4, 4 * rows, w) for w in ends]
    nears = []
    for half, held, order in ((third[0], held_a, (1, 2)), (third[1], held_b, (2, 1))):
        blocks = along_dp(flat(held), *order)
        nears += [piece for _, piece in blocks[1:]]
        for bits, piece in blocks:
            column = 0
            for part, out, to in half:
                work.add(piece, fulls[out], 0, bits, to=to, first=column, width=part.shape[1])
                column += part.shape[1]
    w_four, w_five = work.run()
    return made, flat(w_two), flat(w_three), flat(w_four), flat(w_five), nears


def pick(value, index, axis):
    return lax.dynamic_index_in_dim(value, index, axis, keepdims=False)


def split_sum(groups, place, after, small=False):
    counts = [len(g) for g in groups]
    widths = [g[0].shape[1] for g in groups]
    rows = groups[0][-1].shape[0] // 4
    arrays = [a for g in groups for a in g]
    total = sum(counts)

    def kernel(place_ref, *refs):
        outs, held = refs[-5:-1], refs[-1]
        number, to = 0, 0
        for count, width in zip(counts, widths):
            for quarter in range(4):
                part = pl.ds(quarter * rows, rows)
                parts = [ref[part, :].astype(f32) for ref in refs[number : number + count]]
                if count == 4:
                    value = (parts[0] + parts[1]) + (parts[2] + parts[3])
                else:
                    value = sum(parts[1:], parts[0])
                held[quarter, :, to : to + width] = value
            number += count
            to += width
        if small:
            end = slice(to - LANES, to)
            for quarter in range(4):
                held[quarter, :, end] = held[0, :, end].astype(bf16).astype(f32)
        for k, out in enumerate(outs):
            out[...] = held[jnp.bitwise_xor(place_ref[0], k)].astype(out.dtype)

    shape = (rows, sum(widths))
    return pl.pallas_call(
        kernel,
        out_shape=[jax.ShapeDtypeStruct(shape, bf16 if k else f32) for k in range(4)],
        in_specs=[pl.BlockSpec(memory_space=pltpu.SMEM)]
        + [pl.BlockSpec(memory_space=pltpu.VMEM)] * total
        + [pl.BlockSpec(memory_space=pl.ANY)] * len(after),
        out_specs=[pl.BlockSpec(memory_space=pltpu.VMEM)] * 4,
        scratch_shapes=[pltpu.VMEM((4, *shape), f32)],
        compiler_params=pltpu.CompilerParams(vmem_limit_bytes=VMEM_LIMIT),
        name="split_sum",
    )(place.reshape(1), *arrays, *after)


def tn(a, b):
    return lax.dot_general(a, b, (((0,), (0,)), ((), ())), preferred_element_type=f32)


def grad_blocks(groups, outputs, place, after, small=None):
    arrays = []

    def index_of(array):
        for number, known in enumerate(arrays):
            if known is array:
                return number
        arrays.append(array)
        return len(arrays) - 1

    plan = [
        [([(index_of(l), index_of(r), first) for l, r, first in terms], width) for terms, width in segments]
        for segments in groups
    ]
    rows = groups[0][0][0][0][0].shape[1] // 4
    if small is not None:
        arrays.append(small)
    count = len(arrays)

    def kernel(place_ref, *refs):
        outs = refs[count + len(after) :]
        for (group, offsets), out in zip(outputs, outs):
            for number, bits in enumerate(offsets):
                first_row = pl.multiple_of(jnp.bitwise_xor(place_ref[0], bits) * rows, rows)
                to = 0
                for terms, width in plan[group]:
                    value = None
                    for l, r, first in terms:
                        part = tn(
                            refs[l][:, pl.ds(first_row, rows)], refs[r][:, first : first + width]
                        )
                        value = part if value is None else value + part
                    out[number * rows : (number + 1) * rows, to : to + width] = value.astype(bf16)
                    to += width
                if small is not None:
                    end = small.shape[0]
                    out[number * rows : number * rows + end, to:] = refs[count - 1][...]
                    out[number * rows + end : (number + 1) * rows, to:] = jnp.zeros(
                        (rows - end, LANES), bf16
                    )

    more = 0 if small is None else LANES
    widths = [sum(width for _, width in segments) + more for segments in groups]
    return pl.pallas_call(
        kernel,
        out_shape=[
            jax.ShapeDtypeStruct((len(offsets) * rows, widths[group]), bf16)
            for group, offsets in outputs
        ],
        in_specs=[pl.BlockSpec(memory_space=pltpu.SMEM)]
        + [pl.BlockSpec(memory_space=pltpu.VMEM)] * count
        + [pl.BlockSpec(memory_space=pl.ANY)] * len(after),
        out_specs=[pl.BlockSpec(memory_space=pltpu.VMEM)] * len(outputs),
        compiler_params=pltpu.CompilerParams(vmem_limit_bytes=VMEM_LIMIT),
        name="grad_blocks",
    )(place.reshape(1), *arrays, *after)


class Scatter:
    def __init__(self, groups, after=(), small=None):
        self.groups = groups
        self.staged = small_mesh()
        self.widths = [sum(width for _, width in segments) for segments in groups]
        self.got, self.near, self.kept = [], [], []
        if not self.staged:
            return
        dp = lax.axis_index("dp")
        if len(groups) == 1:
            self.own, *sends = grad_blocks(
                groups, [(0, (k,)) for k in range(4)], dp, after, small
            )
            self.got = [swap(send, "dp", k) for k, send in enumerate(sends, start=1)]
            return
        self.rows = groups[0][0][0][0][0].shape[1] // 4
        outputs = [(0, (2, 3)), (1, (1, 3)), (0, (0, 1)), (1, (0, 2))]
        send_a, send_b, *self.kept = grad_blocks(groups, outputs, dp, after)
        self.got = [swap(send_a, "dp", 2), swap(send_b, "dp", 1)]

    def second(self, after=()):
        if not self.staged or len(self.groups) == 1:
            return
        rows, after = self.rows, list(after)

        def kernel(kept_a, kept_b, got_a, got_b, *refs):
            for kept, got, out in ((kept_a, got_a, refs[-2]), (kept_b, got_b, refs[-1])):
                out[...] = (kept[...].astype(f32) + got[...].astype(f32)).astype(bf16)

        arrays = [*self.kept, *self.got]
        self.sends = pl.pallas_call(
            kernel,
            grid=(1,),
            out_shape=[jax.ShapeDtypeStruct((rows, width), bf16) for width in self.widths],
            in_specs=[pl.BlockSpec((rows, a.shape[1]), lambda i: (1, 0)) for a in arrays]
            + [spec_any()] * len(after),
            out_specs=[pl.BlockSpec((rows, width), lambda i: (0, 0)) for width in self.widths],
            compiler_params=params(),
            cost_estimate=cost(2),
            name="second_add",
        )(*arrays, *after)
        self.near = [swap(send, "dp", bits) for send, bits in zip(self.sends, (1, 2))]

    def addends(self):
        if len(self.groups) == 1:
            return [[self.own, *self.got]]
        return [[self.kept[n], self.got[n], self.near[n]] for n in range(2)]


class Finish:
    def __init__(self, sums, after=(), small=False):
        self.sums = sums
        self.staged = small_mesh()
        self.sends, self.along = [], []
        if not self.staged:
            return
        groups = [g for one in sums for g in one.addends()]
        self.own, *self.sends = split_sum(groups, lax.axis_index("ctx"), after, small)
        self.along = [swap(send, "ctx", k) for k, send in enumerate(self.sends, start=1)]

    def results(self):
        if not self.staged:
            out = []
            for one in self.sums:
                parts = [
                    sum(tn(l, r[:, first : first + width]) for l, r, first in terms).astype(bf16)
                    for segments in one.groups
                    for terms, width in segments
                ]
                joined = jnp.concatenate(parts, axis=1)
                out.append(
                    lax.psum_scatter(
                        joined, ("dp", "ctx"), scatter_dimension=0, tiled=True
                    ).astype(f32)
                )
            return out
        one, two, three = [piece.astype(f32) for piece in self.along]
        total = (self.own + one) + (two + three)
        out, first = [], 0
        for one in self.sums:
            out.append(total[:, first : first + sum(one.widths)])
            first += sum(one.widths)
        self.small = total[:, first:]
        return out


def sum_all(value, axes):
    for axis in axes:
        count = lax.axis_size(axis)
        if count & (count - 1):
            value = lax.psum(value, axis)
            continue
        bits = 1
        while bits < count:
            value = value + swap(value, axis, bits)
            bits *= 2
    return value


def pair_sum(value):
    if lax.axis_size("tp") != 2:
        return lax.psum(value.astype(bf16), "tp").astype(f32)
    low = value.astype(bf16)
    return low.astype(f32) + swap(low, "tp", 1).astype(f32)


def chain_pieces(pack, reverse):
    count, me = lax.axis_size("ctx"), lax.axis_index("ctx")
    states = pack.shape[1] - TAIL
    if 2 < count <= 4:
        sign = -1 if reverse else 1
        near = shifted(pack, "ctx", sign)
        two = pack[:, :states].astype(f32) + pack[:, states : states + 1].astype(f32) * near[
            :, :states
        ].astype(f32)
        return [near, shifted(two.astype(bf16), "ctx", 2 * sign)]
    everything = lax.all_gather(pack, "ctx")

    def hop(k, before):
        at = count - 1 - k if reverse else k
        reached = at > me if reverse else at < me
        there = pick(everything, at, 0).astype(f32)
        new = there[:, states : states + 1] * before + there[:, :states]
        return jnp.where(reached, new, before)

    start = jnp.zeros((pack.shape[0], states, pack.shape[2]), f32)
    total = lax.fori_loop(0, count, hop, start).astype(bf16)
    return [jnp.pad(total, ((0, 0), (0, TAIL), (0, 0)))]


def dot(a, b):
    return jnp.dot(a, b, preferred_element_type=f32)


def dot_nt(a, b):
    return lax.dot_general(a, b, (((1,), (1,)), ((), ())), preferred_element_type=f32)


def sig(v):
    return 1.0 / (1.0 + jnp.exp(-v))


def conv_pre(joined, span, taps, pos, count):
    total = None
    for k in range(KC):
        piece = joined[TAIL - k : TAIL - k + count, span]
        term = taps[k : k + 1, :] * piece
        if k:
            term = term * (pos >= k).astype(f32)
        total = term if total is None else total + term
    return total


def lane_ids(shape):
    return lax.broadcasted_iota(jnp.int32, shape, 1)


def decay_parts(dtr, head_row, pos, heads):
    count = dtr.shape[0]
    lane = lane_ids(dtr.shape)
    pre = dtr + head_row[1:2, :]
    dt = jnp.where(lane < heads, jnp.maximum(pre, 0.0) + jnp.log(1.0 + jnp.exp(-jnp.abs(pre))), 0.0)
    la = -jnp.exp(head_row[0:1, :]) * dt
    marked = jnp.where(lane == LANES - 1, (pos == 0).astype(f32), la)
    row = lax.broadcasted_iota(jnp.int32, (count, count), 0)
    col = lax.broadcasted_iota(jnp.int32, (count, count), 1)
    lower = (row >= col).astype(f32)
    summed = jnp.dot(lower, marked, precision=highest, preferred_element_type=f32)
    return pre, dt, la, summed


def wide(value, lane):
    return jnp.broadcast_to(value[:, lane : lane + 1], (value.shape[0], LANES))


def pair(value, j, low_half):
    return jnp.where(low_half, wide(value, 2 * j), wide(value, 2 * j + 1))


def spec_whole(a):
    return pl.BlockSpec(a.shape, lambda s: (0,) * a.ndim)


def spec_rows(a, rows, base=0):
    return pl.BlockSpec((rows, a.shape[1]), lambda s: (base + s, 0))


def spec_seq(a):
    return pl.BlockSpec((1,) + a.shape[1:], lambda s: (s,) + (0,) * (a.ndim - 1))


def spec_any():
    return pl.BlockSpec(memory_space=pl.ANY)


def params():
    return pltpu.CompilerParams(vmem_limit_bytes=VMEM_LIMIT)


def cost(microseconds):
    return pl.CostEstimate(
        flops=int(microseconds * 1e8), bytes_accessed=int(microseconds * 3e5), transcendentals=0
    )


def chained_state(pieces, span, states):
    total, factor = None, None
    for piece in pieces:
        there = piece[0, :states, span].astype(f32)
        total = there if total is None else total + factor * there
        if piece is not pieces[-1]:
            decay = piece[0, states : states + 1, span].astype(f32)
            factor = decay if factor is None else factor * decay
    return total


def mixer_local_kernel(
    heads, inner, both, proj_ref, tail_ref, tx_ref, tb_ref, hr_ref, pos_ref,
    y_ref, pack_ref, c_ref, l_ref, jx, jb,
):
    count = proj_ref.shape[0]
    states = both // 2
    pos = pos_ref[...]
    head_row = hr_ref[...]
    jx[0:TAIL, :] = tail_ref[:, :inner]
    jx[TAIL : TAIL + count, :] = proj_ref[:, :inner]
    jb[0:TAIL, :] = tail_ref[:, inner : inner + both]
    jb[TAIL : TAIL + count, :] = proj_ref[:, inner : inner + both]
    pre_b = conv_pre(jb, slice(0, both), tb_ref[...], pos, count)
    bc = pre_b * sig(pre_b)
    b_low = bc[:, :states].astype(bf16)
    c_low = bc[:, states:].astype(bf16)
    c_ref[...] = c_low
    bt_low = jnp.transpose(bc[:, :states]).astype(bf16)
    _, dt, _, summed = decay_parts(proj_ref[:, inner + both :], head_row, pos, heads)
    l_ref[...] = summed
    rows = jnp.transpose(summed)
    row = lax.broadcasted_iota(jnp.int32, (count, count), 0)
    col = lax.broadcasted_iota(jnp.int32, (count, count), 1)
    marks = summed[:, LANES - 1 : LANES]
    valid = (row >= col) & (marks == rows[LANES - 1 : LANES, :])
    scores = dot_nt(c_low, b_low)
    last = summed[count - 1 : count, :]
    same = (marks == last[:, LANES - 1 : LANES]).astype(f32)
    carry = jnp.exp(last) * (last[:, LANES - 1 : LANES] == 0.0).astype(f32)
    low_half = lane_ids((count, LANES)) < HD
    low_row = low_half[0:1, :]
    for j in range(heads // 2):
        span = slice(j * LANES, (j + 1) * LANES)
        pre = conv_pre(jx, span, tx_ref[:, span], pos, count)
        xc = pre * sig(pre)
        u = xc * pair(dt, j, low_half)
        u_low = u.astype(bf16)
        results = []
        for h in (2 * j, 2 * j + 1):
            differ = summed[:, h : h + 1] - rows[h : h + 1, :]
            mixing = jnp.exp(jnp.where(valid, differ, -1e30)) * scores
            results.append(dot(mixing.astype(bf16), u_low))
        skip = pair(head_row[2:3, :], j, low_row)
        y_ref[:, span] = jnp.where(low_half, results[0], results[1]) + skip * xc
        left = jnp.exp(pair(last, j, low_row) - pair(summed, j, low_half)) * same
        pack_ref[0, :states, span] = dot(bt_low, (left * u).astype(bf16)).astype(bf16)
        pack_ref[0, states:, span] = jnp.broadcast_to(pair(carry, j, low_row), (TAIL, LANES)).astype(bf16)


def mixer_local(proj, taps_x, taps_bc, head_row, pos, heads, seqs, count):
    inner, both = taps_x.shape[1], taps_bc.shape[1]
    states = both // 2
    outs = [
        jax.ShapeDtypeStruct((seqs * count, inner), f32),
        jax.ShapeDtypeStruct((seqs, states + TAIL, inner), bf16),
        jax.ShapeDtypeStruct((seqs * count, states), bf16),
        jax.ShapeDtypeStruct((seqs * count, LANES), f32),
    ]
    return pl.pallas_call(
        functools.partial(mixer_local_kernel, heads, inner, both),
        grid=(seqs,),
        out_shape=outs,
        in_specs=[
            spec_rows(proj, count),
            spec_rows(proj, TAIL, seqs * count // TAIL),
            spec_whole(taps_x), spec_whole(taps_bc), spec_whole(head_row), spec_rows(pos, count),
        ],
        out_specs=[
            spec_rows(outs[0], count), spec_seq(outs[1]), spec_rows(outs[2], count),
            spec_rows(outs[3], count),
        ],
        scratch_shapes=[
            pltpu.VMEM((count + TAIL, inner), f32),
            pltpu.VMEM((count + TAIL, both), f32),
        ],
        compiler_params=params(),
        cost_estimate=cost(8),
        name="mixer_local",
    )(proj, proj, taps_x, taps_bc, head_row, pos)


def mixer_read_kernel(
    heads, pieces, first, y0_ref, c_ref, l_ref, qz_ref, att_ref, *refs
):
    packs = refs[:pieces]
    y_ref, out_ref, state_ref = refs[-3:]
    count = y0_ref.shape[0]
    states = c_ref.shape[1]
    qwidth = att_ref.shape[1]
    summed = l_ref[...]
    alive = (summed[:, LANES - 1 : LANES] == 0.0).astype(f32)
    low_half = lane_ids((count, LANES)) < HD
    out_ref[:, :qwidth] = att_ref[...]
    for j in range(heads // 2):
        span = slice(j * LANES, (j + 1) * LANES)
        state = chained_state(packs, span, states).astype(bf16)
        state_ref[0, :, span] = state
        reads = jnp.exp(pair(summed, j, low_half)) * alive
        y = y0_ref[:, span] + reads * dot(c_ref[...], state)
        y_ref[:, span] = y
        gate = qz_ref[:, first + j * LANES : first + (j + 1) * LANES]
        out_ref[:, qwidth + j * LANES : qwidth + (j + 1) * LANES] = (y * gate * sig(gate)).astype(bf16)


def mixer_read(y_local, c_vec, summed, qz, att, packs, extra, heads, seqs, count, first):
    inner, states = y_local.shape[1], c_vec.shape[1]
    outs = [
        jax.ShapeDtypeStruct((seqs * count, inner), f32),
        jax.ShapeDtypeStruct((seqs * count, att.shape[1] + inner), bf16),
        jax.ShapeDtypeStruct((seqs, states, inner), bf16),
    ]
    args = (y_local, c_vec, summed, qz, att)
    return pl.pallas_call(
        functools.partial(mixer_read_kernel, heads, len(packs), first),
        grid=(seqs,),
        out_shape=outs,
        in_specs=[spec_rows(a, count) for a in args]
        + [spec_seq(p) for p in packs]
        + [spec_any()] * len(extra),
        out_specs=[spec_rows(outs[0], count), spec_rows(outs[1], count), spec_seq(outs[2])],
        compiler_params=params(),
        cost_estimate=cost(4),
        name="mixer_read",
    )(*args, *packs, *extra)


def gate_back_kernel(
    heads, first, qwidth, d_ref, y_ref, qz_ref, c_ref, l_ref,
    dy_ref, dz_ref, datt_ref, pack_ref,
):
    count = y_ref.shape[0]
    states = c_ref.shape[1]
    summed = l_ref[...]
    alive = (summed[:, LANES - 1 : LANES] == 0.0).astype(f32)
    last = summed[count - 1 : count, :]
    carry = jnp.exp(last) * (last[:, LANES - 1 : LANES] == 0.0).astype(f32)
    low_half = lane_ids((count, LANES)) < HD
    low_row = low_half[0:1, :]
    ct_low = jnp.transpose(c_ref[...].astype(f32)).astype(bf16)
    datt_ref[...] = d_ref[:, :qwidth].astype(bf16)
    for j in range(heads // 2):
        span = slice(j * LANES, (j + 1) * LANES)
        gate = qz_ref[:, first + j * LANES : first + (j + 1) * LANES]
        d_gated = d_ref[:, qwidth + j * LANES : qwidth + (j + 1) * LANES]
        sg = sig(gate)
        dy = d_gated * (gate * sg)
        dy_ref[:, span] = dy
        dz_ref[:, span] = (
            d_gated * y_ref[:, span] * (sg * (1.0 + gate * (1.0 - sg)))
        ).astype(bf16)
        reads = jnp.exp(pair(summed, j, low_half)) * alive
        pack_ref[0, :states, span] = dot(ct_low, (reads * dy).astype(bf16)).astype(bf16)
        pack_ref[0, states:, span] = jnp.broadcast_to(pair(carry, j, low_row), (TAIL, LANES)).astype(bf16)


def gate_back(d_mixer, y, qz, c_vec, summed, heads, seqs, count, first, qwidth):
    inner, states = y.shape[1], c_vec.shape[1]
    outs = [
        jax.ShapeDtypeStruct((seqs * count, inner), f32),
        jax.ShapeDtypeStruct((seqs * count, inner), bf16),
        jax.ShapeDtypeStruct((seqs * count, qwidth), bf16),
        jax.ShapeDtypeStruct((seqs, states + TAIL, inner), bf16),
    ]
    args = (d_mixer, y, qz, c_vec, summed)
    return pl.pallas_call(
        functools.partial(gate_back_kernel, heads, first, qwidth),
        grid=(seqs,),
        out_shape=outs,
        in_specs=[spec_rows(a, count) for a in args],
        out_specs=[spec_rows(o, count) for o in outs[:3]] + [spec_seq(outs[3])],
        compiler_params=params(),
        cost_estimate=cost(5),
        name="gate_back",
    )(*args)


def small_rows(inner, both):
    taps_bc_at = inner // LANES * KC
    return taps_bc_at, taps_bc_at + both // LANES * KC


def mixer_back_kernel(
    heads, inner, both, pieces, extra, proj_ref, tail_ref, tx_ref, tb_ref, hr_ref, pos_ref,
    dy_ref, y_ref, st_ref, *refs
):
    packs = refs[:pieces]
    main_ref, side_ref, small_ref, jx, jb, ax, ab = refs[pieces + extra :]
    small_ref[...] = jnp.zeros_like(small_ref)
    taps_bc_at, heads_at = small_rows(inner, both)
    count = proj_ref.shape[0]
    states = both // 2
    pos = pos_ref[...]
    head_row = hr_ref[...]
    jx[0:TAIL, :] = tail_ref[:, :inner]
    jx[TAIL : TAIL + count, :] = proj_ref[:, :inner]
    jb[0:TAIL, :] = tail_ref[:, inner : inner + both]
    jb[TAIL : TAIL + count, :] = proj_ref[:, inner : inner + both]
    pre_b = conv_pre(jb, slice(0, both), tb_ref[...], pos, count)
    sig_b = sig(pre_b)
    bc = pre_b * sig_b
    b_low = bc[:, :states].astype(bf16)
    c_low = bc[:, states:].astype(bf16)
    pre_dt, dt, la, summed = decay_parts(proj_ref[:, inner + both :], head_row, pos, heads)
    rows = jnp.transpose(summed)
    row = lax.broadcasted_iota(jnp.int32, (count, count), 0)
    col = lax.broadcasted_iota(jnp.int32, (count, count), 1)
    marks = summed[:, LANES - 1 : LANES]
    valid = (row <= col) & (marks == rows[LANES - 1 : LANES, :])
    scores = dot_nt(b_low, c_low)
    last = summed[count - 1 : count, :]
    carry = jnp.exp(last) * (last[:, LANES - 1 : LANES] == 0.0).astype(f32)
    same = (marks == last[:, LANES - 1 : LANES]).astype(f32)
    first = (marks == 0.0).astype(f32)
    low_half = lane_ids((count, LANES)) < HD
    low_row = low_half[0:1, :]
    lane = lane_ids((LANES, LANES))
    lane_row = lax.broadcasted_iota(jnp.int32, (LANES, LANES), 0)
    d_scores = jnp.zeros((count, count), f32)
    d_b = jnp.zeros((count, states), f32)
    d_c = jnp.zeros((count, states), f32)
    d_sum = jnp.zeros((count, LANES), f32)
    d_dt = jnp.zeros((count, LANES), f32)
    d_rows = jnp.zeros((8, LANES), f32)
    ax[...] = jnp.zeros_like(ax)
    ab[...] = jnp.zeros_like(ab)
    for j in range(heads // 2):
        span = slice(j * LANES, (j + 1) * LANES)
        taps = tx_ref[:, span]
        pre = conv_pre(jx, span, taps, pos, count)
        sg = sig(pre)
        xc = pre * sg
        dt_wide = pair(dt, j, low_half)
        u = xc * dt_wide
        u_low = u.astype(bf16)
        dy = dy_ref[:, span]
        dy_low = dy.astype(bf16)
        state = st_ref[0, :, span]
        later = chained_state(packs, span, states)
        d_state = later.astype(bf16)
        results = []
        for i, h in enumerate((2 * j, 2 * j + 1)):
            differ = rows[h : h + 1, :] - summed[:, h : h + 1]
            decay = jnp.exp(jnp.where(valid, differ, -1e30))
            half = low_half if i == 0 else jnp.logical_not(low_half)
            u_half = jnp.where(half, u, 0.0).astype(bf16)
            d_scores = d_scores + decay * dot_nt(u_half, dy_low)
            results.append(dot((decay * scores).astype(bf16), dy_low))
        left = jnp.exp(pair(last, j, low_row) - pair(summed, j, low_half)) * same
        reads = jnp.exp(pair(summed, j, low_half)) * first
        du_end = left * dot(b_low, d_state)
        du_in = jnp.where(low_half, results[0], results[1])
        du = du_in + du_end
        d_c = d_c + dot_nt((reads * dy).astype(bf16), state)
        d_b = d_b + dot_nt((left * u).astype(bf16), d_state)
        skip = pair(head_row[2:3, :], j, low_row)
        chosen = (
            ((lane == 2 * j) & (lane_row < HD)) | ((lane == 2 * j + 1) & (lane_row >= HD))
        ).astype(f32)
        per_token = (
            dy_low.astype(f32) * (y_ref[:, span] - skip * xc)
            - u_low.astype(f32) * du_in
            - u * du_end
        )
        d_sum = d_sum + jnp.dot(per_token, chosen, precision=highest, preferred_element_type=f32)
        d_dt = d_dt + jnp.dot(du * xc, chosen, precision=highest, preferred_element_type=f32)
        sums = jnp.concatenate(
            [
                jnp.sum(u * du_end, axis=0, keepdims=True),
                jnp.sum(dy * xc, axis=0, keepdims=True),
                jnp.sum(later * state.astype(f32), axis=0, keepdims=True),
                jnp.zeros((5, LANES), f32),
            ],
            axis=0,
        )
        d_rows = d_rows + jnp.dot(sums, chosen, precision=highest, preferred_element_type=f32)
        d_pre = (du * dt_wide + skip * dy) * (sg * (1.0 + pre * (1.0 - sg)))
        for k in range(KC):
            masked = d_pre * (pos >= k).astype(f32) if k else d_pre
            small_ref[0, j * KC + k : j * KC + k + 1, :] = jnp.sum(
                masked * jx[TAIL - k : TAIL - k + count, span], axis=0, keepdims=True
            )
            ax[TAIL - k : TAIL - k + count, span] += taps[k : k + 1, :] * masked
    main_ref[:, :inner] = ax[TAIL:, :].astype(bf16)
    side_ref[:, :inner] = ax[:TAIL, :].astype(bf16)
    d_b = d_b + dot(d_scores.astype(bf16), c_low)
    d_c = d_c + dot(jnp.transpose(d_scores).astype(bf16), b_low)
    d_pre = jnp.concatenate([d_b, d_c], axis=1) * (sig_b * (1.0 + pre_b * (1.0 - sig_b)))
    for k in range(KC):
        masked = d_pre * (pos >= k).astype(f32) if k else d_pre
        sums = jnp.sum(masked * jb[TAIL - k : TAIL - k + count, :], axis=0, keepdims=True)
        for g in range(both // LANES):
            at = taps_bc_at + g * KC + k
            small_ref[0, at : at + 1, :] = sums[:, g * LANES : (g + 1) * LANES]
        ab[TAIL - k : TAIL - k + count, :] += tb_ref[k : k + 1, :] * masked
    main_ref[:, inner : inner + both] = ab[TAIL:, :].astype(bf16)
    side_ref[:, inner : inner + both] = ab[:TAIL, :].astype(bf16)
    token = lax.broadcasted_iota(jnp.int32, (count, LANES), 0)
    at_last = d_rows[0:1, :] + d_rows[2:3, :] * carry
    d_sum = d_sum + jnp.where(token == count - 1, at_last, 0.0)
    upper = (row <= col).astype(f32)
    d_la = jnp.dot(upper, d_sum, precision=highest, preferred_element_type=f32)
    d_la = jnp.where(lane_ids(d_la.shape) < heads, d_la, 0.0)
    d_dt = d_dt - jnp.exp(head_row[0:1, :]) * d_la
    d_dtr = d_dt * sig(pre_dt)
    d_dtr = jnp.where(lane_ids(d_dtr.shape) < heads, d_dtr, 0.0)
    main_ref[:, inner + both :] = d_dtr.astype(bf16)
    side_ref[:, inner + both :] = jnp.zeros((TAIL, LANES), bf16)
    small_ref[0, heads_at : heads_at + 1, :] = jnp.sum(d_la * la, axis=0, keepdims=True)
    small_ref[0, heads_at + 1 : heads_at + 2, :] = jnp.sum(d_dtr, axis=0, keepdims=True)
    small_ref[0, heads_at + 2 : heads_at + 3, :] = d_rows[1:2, :]


def mixer_back(
    number, made, proj, taps_x, taps_bc, head_row, pos, dy, y, state, packs, extra, heads, seqs, count
):
    inner, both = taps_x.shape[1], taps_bc.shape[1]
    width = proj.shape[1]
    outs = [
        jax.ShapeDtypeStruct((seqs * count, width), bf16),
        jax.ShapeDtypeStruct((seqs * TAIL, width), bf16),
        jax.ShapeDtypeStruct((1, SMALL, LANES), f32),
    ]

    def rows_of(a, rows, block):
        return pl.BlockSpec((rows, a.shape[1]), lambda i: (block, 0))

    def seq_of(a):
        return pl.BlockSpec((1,) + a.shape[1:], lambda i: (number,) + (0,) * (a.ndim - 1))

    extra = list(made) + list(extra)
    first = 9 + len(packs)
    return pl.pallas_call(
        functools.partial(mixer_back_kernel, heads, inner, both, len(packs), len(extra)),
        grid=(1,),
        out_shape=outs,
        in_specs=[
            rows_of(proj, count, number),
            rows_of(proj, TAIL, seqs * count // TAIL + number),
            spec_whole(taps_x), spec_whole(taps_bc), spec_whole(head_row),
            rows_of(pos, count, number), rows_of(dy, count, number), rows_of(y, count, number),
            seq_of(state),
        ]
        + [seq_of(p) for p in packs]
        + [spec_any()] * len(extra),
        out_specs=[rows_of(outs[0], count, number), rows_of(outs[1], TAIL, number)]
        + [spec_seq(o) for o in outs[2:]],
        scratch_shapes=[
            pltpu.VMEM((count + TAIL, inner), f32),
            pltpu.VMEM((count + TAIL, both), f32),
            pltpu.VMEM((count + TAIL, inner), f32),
            pltpu.VMEM((count + TAIL, both), f32),
        ],
        input_output_aliases={first: 0, first + 1: 1} if made else {},
        compiler_params=params(),
        cost_estimate=cost(9),
        name="mixer_back",
    )(proj, proj, taps_x, taps_bc, head_row, pos, dy, y, state, *packs, *extra)


def hidden_back_kernel(two_ref, main_ref, side_ref, w_two_ref, w_one_ref, *refs):
    out_ref, tail_ref = refs[-2:]
    half = two_ref.shape[0] // 2
    for part in (slice(0, half), slice(half, 2 * half)):
        out_ref[part, :] = dot_nt(two_ref[part, :], w_two_ref[...]) + dot_nt(
            main_ref[part, :], w_one_ref[...]
        )
    tail_ref[...] = dot_nt(side_ref[...], w_one_ref[...]).astype(bf16)


def hidden_back(d_two, d_main, d_side, w_two, w_one, after):
    args = (d_two, d_main, d_side, w_two, w_one)
    features = w_one.shape[0]
    return pl.pallas_call(
        hidden_back_kernel,
        out_shape=[
            jax.ShapeDtypeStruct((d_two.shape[0], features), f32),
            jax.ShapeDtypeStruct((d_side.shape[0], features), bf16),
        ],
        in_specs=[pl.BlockSpec(memory_space=pltpu.VMEM)] * len(args) + [spec_any()] * len(after),
        out_specs=[pl.BlockSpec(memory_space=pltpu.VMEM)] * 2,
        compiler_params=params(),
        cost_estimate=cost(5),
        name="hidden_back",
    )(*args, *after)


def half_turned(v):
    first = lane_ids(v.shape) % HD < HD // 2
    return jnp.where(
        first, -pltpu.roll(v, LANES - HD // 2, 1), pltpu.roll(v, HD // 2, 1)
    )


def rope_kernel(qwidth, qz_ref, cos_ref, sin_ref, q_ref, kv_ref):
    cosine, sine = cos_ref[...], sin_ref[...]
    for j in range(qwidth // LANES):
        v = qz_ref[:, j * LANES : (j + 1) * LANES]
        q_ref[:, j * LANES : (j + 1) * LANES] = (v * cosine + half_turned(v) * sine).astype(bf16)
    v = qz_ref[:, qwidth : qwidth + LANES]
    turned = v * cosine + half_turned(v) * sine
    kv_ref[...] = jnp.where(lane_ids(v.shape) < HD, turned, v).astype(bf16)


def rope(qz, cosine, sine, qwidth, seqs, count):
    outs = [
        jax.ShapeDtypeStruct((seqs * count, qwidth), bf16),
        jax.ShapeDtypeStruct((seqs * count, 2 * HD), bf16),
    ]
    return pl.pallas_call(
        functools.partial(rope_kernel, qwidth),
        grid=(seqs,),
        out_shape=outs,
        in_specs=[
            pl.BlockSpec((count, qwidth + LANES), lambda s: (s, 0)),
            spec_rows(cosine, count), spec_rows(sine, count),
        ],
        out_specs=[spec_rows(o, count) for o in outs],
        compiler_params=params(),
        cost_estimate=cost(2),
        name="rope",
    )(qz, cosine, sine)


def to_low(v, r, low_half):
    v = v.astype(f32)
    return jnp.where(low_half, v if r % 2 == 0 else pltpu.roll(v, HD, 1), 0.0)


def to_high(v, r, low_half):
    v = v.astype(f32)
    return jnp.where(low_half, 0.0, v if r % 2 else pltpu.roll(v, HD, 1))


def key_masks(pos, count, blocks):
    row = lax.broadcasted_iota(jnp.int32, (count, count), 0)
    col = lax.broadcasted_iota(jnp.int32, (count, count), 1)
    start = row - pos
    masks = []
    for d in range(blocks):
        mask = col - d * count >= start
        masks.append(mask & (col <= row) if d == 0 else mask)
    return masks


def attend_kernel(per_group, blocks, q_ref, pos_ref, *refs):
    kv = refs[:blocks]
    o_ref, lse_ref = refs[blocks:]
    count = q_ref.shape[0]
    masks = key_masks(pos_ref[...], count, blocks)
    low_half = lane_ids((count, LANES)) < HD
    lane = lane_ids((count, LANES))
    lse = jnp.zeros((count, LANES), f32)
    halves = []
    for r in range(per_group):
        span = slice(r // 2 * LANES, (r // 2 + 1) * LANES)
        q = to_low(q_ref[:, span], r, low_half).astype(bf16)
        scores = [
            jnp.where(masks[d], dot_nt(q, kv[d][...]) * 0.125, -1e30) for d in range(blocks)
        ]
        top = jnp.max(scores[0], axis=1, keepdims=True)
        for d in range(1, blocks):
            top = jnp.maximum(top, jnp.max(scores[d], axis=1, keepdims=True))
        weights = [jnp.exp(v - top) for v in scores]
        total = jnp.sum(weights[0], axis=1, keepdims=True)
        for d in range(1, blocks):
            total = total + jnp.sum(weights[d], axis=1, keepdims=True)
        scale = 1.0 / total
        out = dot((weights[0] * scale).astype(bf16), kv[0][...])
        for d in range(1, blocks):
            out = out + dot((weights[d] * scale).astype(bf16), kv[d][...])
        lse = jnp.where(lane == r, top + jnp.log(total), lse)
        halves.append(out)
        if r % 2:
            o_ref[:, span] = jnp.where(low_half, pltpu.roll(halves[r - 1], HD, 1), out).astype(bf16)
    lse_ref[...] = lse


def attend(q, pos, kv, seqs, count):
    per_group = q.shape[1] // HD
    outs = [
        jax.ShapeDtypeStruct(q.shape, bf16),
        jax.ShapeDtypeStruct((q.shape[0], LANES), f32),
    ]
    return pl.pallas_call(
        functools.partial(attend_kernel, per_group, len(kv)),
        grid=(seqs,),
        out_shape=outs,
        in_specs=[spec_rows(a, count) for a in (q, pos, *kv)],
        out_specs=[spec_rows(o, count) for o in outs],
        compiler_params=params(),
        cost_estimate=cost(8),
        name="attend",
    )(q, pos, *kv)


def attend_back_kernel(per_group, blocks, q_ref, pos_ref, do_ref, lse_ref, cos_ref, sin_ref, *refs):
    kv = refs[:blocks]
    dq_ref = refs[blocks]
    dkv = refs[blocks + 1 :]
    count = q_ref.shape[0]
    masks = key_masks(pos_ref[...], count, blocks)
    low_half = lane_ids((count, LANES)) < HD
    cosine, sine = cos_ref[...], sin_ref[...]
    totals = [jnp.zeros((LANES, count), f32) for _ in range(blocks)]
    halves = []
    for r in range(per_group):
        span = slice(r // 2 * LANES, (r // 2 + 1) * LANES)
        q = to_low(q_ref[:, span], r, low_half)
        do = to_high(do_ref[:, span], r, low_half)
        q_turned = (jnp.transpose(q) * 0.125).astype(bf16)
        do_turned = jnp.transpose(do).astype(bf16)
        q, do = q.astype(bf16), do.astype(bf16)
        lse = lse_ref[:, r : r + 1]
        probs, d_probs = [], []
        row_dot = None
        for d in range(blocks):
            scores = jnp.where(masks[d], dot_nt(q, kv[d][...]) * 0.125, -1e30)
            probs.append(jnp.exp(scores - lse))
            d_probs.append(dot_nt(do, kv[d][...]))
            part = jnp.sum(probs[d] * d_probs[d], axis=1, keepdims=True)
            row_dot = part if row_dot is None else row_dot + part
        dq = None
        for d in range(blocks):
            d_scores = (probs[d] * (d_probs[d] - row_dot)).astype(bf16)
            part = dot(d_scores, kv[d][...])
            dq = part if dq is None else dq + part
            totals[d] = (
                totals[d] + dot(q_turned, d_scores) + dot(do_turned, probs[d].astype(bf16))
            )
        halves.append(dq * 0.125)
        if r % 2:
            both = jnp.where(low_half, halves[r - 1], pltpu.roll(halves[r], HD, 1))
            dq_ref[:, span] = (both * cosine - half_turned(both) * sine).astype(bf16)
    for d in range(blocks):
        dkv[d][...] = jnp.transpose(totals[d]).astype(dkv[d].dtype)


def attend_back(q, pos, d_out, lse, cosine, sine, kv, seqs, count):
    per_group = q.shape[1] // HD
    outs = [jax.ShapeDtypeStruct(q.shape, bf16)] + [
        jax.ShapeDtypeStruct(kv[0].shape, bf16 if d else f32) for d in range(len(kv))
    ]
    args = (q, pos, d_out, lse, cosine, sine, *kv)
    return pl.pallas_call(
        functools.partial(attend_back_kernel, per_group, len(kv)),
        grid=(seqs,),
        out_shape=outs,
        in_specs=[spec_rows(a, count) for a in args],
        out_specs=[spec_rows(o, count) for o in outs],
        compiler_params=params(),
        cost_estimate=cost(14),
        name="attend_back",
    )(*args)


def join_back_kernel(pieces, dq_ref, dz_ref, cos_ref, sin_ref, *refs):
    out_ref = refs[-1]
    qwidth = dq_ref.shape[1]
    total = refs[0][...].astype(f32)
    for piece in refs[1:pieces]:
        total = total + piece[...].astype(f32)
    turned = total * cos_ref[...] - half_turned(total) * sin_ref[...]
    out_ref[:, :qwidth] = dq_ref[...]
    out_ref[:, qwidth : qwidth + LANES] = jnp.where(
        lane_ids(total.shape) < HD, turned, total
    ).astype(bf16)
    out_ref[:, qwidth + LANES :] = dz_ref[...]


def join_back(dq, dz, cosine, sine, pieces, extra, seqs, count):
    out = jax.ShapeDtypeStruct((dq.shape[0], dq.shape[1] + LANES + dz.shape[1]), bf16)
    args = (dq, dz, cosine, sine, *pieces)
    return pl.pallas_call(
        functools.partial(join_back_kernel, len(pieces)),
        grid=(seqs,),
        out_shape=out,
        in_specs=[spec_rows(a, count) for a in args] + [spec_any()] * len(extra),
        out_specs=spec_rows(out, count),
        compiler_params=params(),
        cost_estimate=cost(2),
        name="join_back",
    )(*args, *extra)


def attend_one(q, k, v, mask):
    scores = jnp.einsum("qrd,kd->rqk", q, k, preferred_element_type=f32) * 0.125
    scores = jnp.where(mask[None], scores, -1e30)
    top = jnp.max(scores, axis=-1, keepdims=True)
    weights = jnp.where(mask[None], jnp.exp(scores - top), 0.0)
    total = jnp.sum(weights, axis=-1, keepdims=True)
    out = jnp.einsum("rqk,kd->qrd", (weights / total).astype(bf16), v, preferred_element_type=f32)
    return out, jnp.transpose((top + jnp.log(total))[..., 0])


def attend_one_back(q, k, v, mask, d_out, lse):
    scores = jnp.einsum("qrd,kd->rqk", q, k, preferred_element_type=f32) * 0.125
    probs = jnp.where(mask[None], jnp.exp(scores - jnp.transpose(lse)[..., None]), 0.0)
    d_probs = jnp.einsum("qrd,kd->rqk", d_out, v, preferred_element_type=f32)
    row_dot = jnp.sum(probs * d_probs, axis=-1, keepdims=True)
    d_scores = (probs * (d_probs - row_dot)).astype(bf16)
    d_q = jnp.einsum("rqk,kd->qrd", d_scores, k, preferred_element_type=f32) * 0.125
    d_k = jnp.einsum("rqk,qrd->kd", d_scores, q, preferred_element_type=f32) * 0.125
    d_v = jnp.einsum("rqk,qrd->kd", probs.astype(bf16), d_out, preferred_element_type=f32)
    return d_q, jnp.concatenate([d_k, d_v], axis=-1)


class Attention:
    def __init__(self, q, kv, pos, seqs, count):
        self.q, self.pos, self.seqs, self.count = q, pos, seqs, count
        self.blocks = lax.axis_size("ctx")
        self.few = self.blocks <= 4
        if self.few:
            self.kv = [kv] + [shifted(kv, "ctx", d) for d in range(1, self.blocks)]
            return
        me = lax.axis_index("ctx")
        shaped = lax.all_gather(kv.reshape(seqs, count, -1), "ctx", axis=1, tiled=True)
        self.all_kv = shaped
        keys = jnp.arange(shaped.shape[1])
        tokens = me * count + jnp.arange(count)
        starts = tokens[None, :] - pos.reshape(seqs, count)
        self.mask = (keys[None, None, :] <= tokens[None, :, None]) & (
            keys[None, None, :] >= starts[:, :, None]
        )

    def heads_of(self, v):
        return v.reshape(self.seqs, self.count, -1, HD)

    def forward(self):
        if self.few:
            out, self.lse = attend(self.q, self.pos, self.kv, self.seqs, self.count)
            return out
        keys, values = self.all_kv[..., :HD], self.all_kv[..., HD:]
        out, self.lse = lax.map(
            lambda a: attend_one(*a), (self.heads_of(self.q), keys, values, self.mask)
        )
        return out.astype(bf16).reshape(self.q.shape)

    def backward(self, d_out, cosine, sine):
        if self.few:
            dq, own, *rest = attend_back(
                self.q, self.pos, d_out, self.lse, cosine, sine, self.kv, self.seqs, self.count
            )
            return dq, [own] + [
                shifted(piece, "ctx", -d) for d, piece in enumerate(rest, start=1)
            ]
        keys, values = self.all_kv[..., :HD], self.all_kv[..., HD:]
        dq, kept = lax.map(
            lambda a: attend_one_back(*a),
            (self.heads_of(self.q), keys, values, self.mask, self.heads_of(d_out), self.lse),
        )
        dq = dq.reshape(self.q.shape)
        cos_q = jnp.tile(cosine, (1, dq.shape[1] // LANES))
        sin_q = jnp.tile(sine, (1, dq.shape[1] // LANES))
        dq = dq * cos_q - jnp.dot(dq, turn_matrix(dq.shape[1]), precision=highest) * sin_q
        total = lax.psum_scatter(kept.astype(bf16), "ctx", scatter_dimension=1, tiled=True)
        return dq.astype(bf16), [total.astype(f32).reshape(-1, 2 * HD)]


def turn_matrix(columns):
    source = jnp.arange(columns)[:, None]
    target = jnp.arange(columns)[None, :]
    half = HD // 2
    low = target % HD < half
    minus = low & (source == target + half)
    plus = jnp.logical_not(low) & (source == target - half)
    return plus.astype(f32) - minus.astype(f32)


def per_device(
    hidden_in,
    positions,
    gain_attn,
    w_qkv,
    w_attn_out,
    w_zx,
    w_bc,
    w_dt,
    conv_x,
    conv_bc,
    a_log,
    dt_bias,
    d_skip,
    w_mamba_out,
    gain_ffn,
    w_gu,
    w_down,
    output_cotangent,
):
    seqs, block = positions.shape
    features = hidden_in.shape[2]
    rows = w_qkv.shape[0]
    heads = a_log.shape[0]
    inner = w_zx.shape[2]
    both = w_bc.shape[1]
    columns = w_qkv.shape[2]
    qwidth = columns - 2 * HD
    units = w_gu.shape[2]
    count = lax.axis_size("ctx")
    place = lax.axis_index("ctx")
    here = seqs * block

    pad = jnp.zeros((rows, LANES - heads - 2), bf16)
    first_pack = jnp.concatenate(
        [w_zx[:, 1, :], w_bc, w_dt, gain_attn[:, None], gain_ffn[:, None], pad], axis=1
    )
    tail = shifted(hidden_in[:, block - TAIL :, :], "ctx", 1)
    down = w_down.T
    half = units // 2
    pos = positions.reshape(here, 1)
    frequency = jnp.power(jnp.float32(rope_base), -jnp.arange(0, HD, 2).astype(f32) / HD)
    turned = pos.astype(f32) * jnp.tile(frequency, 2 * LANES // HD)
    cosine, sine = jnp.cos(turned), jnp.sin(turned)

    x_own = hidden_in.reshape(here, features).astype(f32)
    x_ext = jnp.concatenate([x_own, tail.reshape(seqs * TAIL, features).astype(f32)], axis=0)
    r_ext = lax.rsqrt(jnp.mean(x_ext * x_ext, axis=-1, keepdims=True) + 1e-05)
    r_one = r_ext[:here]
    taps_x = conv_x.astype(f32)
    taps_bc = conv_bc.astype(f32)
    head_row = jnp.pad(
        jnp.stack([a_log, dt_bias, d_skip]), ((0, 5), (0, LANES - heads))
    )

    def with_first(w_one):
        gain_a = w_one[:, inner + both + heads].astype(f32)
        h_ext = (x_ext * r_ext * gain_a).astype(bf16)
        proj = dot(h_ext, w_one)
        local = mixer_local(proj, taps_x, taps_bc, head_row, pos, heads, seqs, block)
        return w_one, gain_a, h_ext, proj, local, local[1]

    made, w_two, w_three, w_four, w_five, nears = gather_all(
        first_pack,
        ([w_qkv[:, 0, :], w_zx[:, 0, :]], [w_attn_out.T, w_mamba_out.T]),
        (
            [(w_gu[:, 0, :], 0, 0), (down[:, :half], 1, 0)],
            [(w_gu[:, 1, :], 0, units), (down[:, half:], 1, half)],
        ),
        with_first,
    )
    w_one, gain_a, h_ext, proj, (y_local, pack, c_vec, summed), _ = made
    gain_f = w_one[:, inner + both + heads + 1].astype(f32)
    h_own = h_ext[:here]
    packs = chain_pieces(pack, False)

    qz = dot(h_own, w_two)
    q_low, kv_low = rope(qz, cosine, sine, qwidth, seqs, block)
    attention = Attention(q_low, kv_low, pos, seqs, block)
    attended = attention.forward()

    y, mixer_out, state = mixer_read(
        y_local, c_vec, summed, qz, attended, packs, nears, heads, seqs, block, columns
    )
    resid = x_own + pair_sum(dot_nt(mixer_out, w_three))

    r_two = lax.rsqrt(jnp.mean(resid * resid, axis=-1, keepdims=True) + 1e-05)
    h_two = (resid * r_two * gain_f).astype(bf16)
    gate_up = dot(h_two, w_four)
    gate_ff, up_ff = gate_up[:, :units], gate_up[:, units:]
    sig_ff = jax.nn.sigmoid(gate_ff)
    silu_ff = gate_ff * sig_ff
    hidden_state = (silu_ff * up_ff).astype(bf16)
    ffn = pair_sum(dot_nt(hidden_state, w_five))
    block_out = (resid + ffn).astype(bf16).reshape(seqs, block, features)

    e_low = output_cotangent.reshape(here, features)
    d_hidden_state = dot(e_low, w_five)
    d_gate_up = jnp.concatenate(
        [
            d_hidden_state * up_ff * (sig_ff * (1.0 + gate_ff * (1.0 - sig_ff))),
            d_hidden_state * silu_ff,
        ],
        axis=1,
    ).astype(bf16)

    d_h_two_part = dot_nt(d_gate_up, w_four).astype(bf16)
    d_h_two = pair_sum(d_h_two_part)
    ffn_sum = Scatter(
        [
            [([(h_two, d_gate_up, 0)], units), ([(e_low, hidden_state, 0)], half)],
            [([(h_two, d_gate_up, units)], units), ([(e_low, hidden_state, half)], half)],
        ]
    )
    scaled = d_h_two * gain_f
    d_resid = (
        e_low.astype(f32)
        + r_two * scaled
        - resid * (r_two * r_two * r_two) * jnp.mean(resid * scaled, axis=-1, keepdims=True)
    )
    d_mix = d_resid.astype(bf16)

    d_mixer = dot(d_mix, w_three)
    d_y, d_z, d_att, d_pack = gate_back(
        d_mixer, y, qz, c_vec, summed, heads, seqs, block, columns, qwidth
    )
    later_packs = chain_pieces(d_pack, True)
    d_q, d_kv = attention.backward(d_att, cosine, sine)
    ffn_sum.second([d_q])
    early = [later_packs[0], *ffn_sum.sends] if ffn_sum.staged else []
    d_two = join_back(d_q, d_z, cosine, sine, d_kv, early, seqs, block)
    two_sum = Scatter(
        [
            [([(h_own, d_two, 0)], columns + inner)],
            [([(d_mix, mixer_out, 0)], qwidth + inner)],
        ]
    )
    ffn_end = Finish([ffn_sum])
    d_main, d_side, small = None, None, None
    for number in range(seqs):
        extra = []
        if number == 0:
            extra = two_sum.kept
        d_main, d_side, more = mixer_back(
            number, (d_main, d_side) if number else (), proj, taps_x, taps_bc, head_row, pos,
            d_y, y, state, later_packs, extra, heads, seqs, block,
        )
        small = more[0] if small is None else small + more[0]
    h_side = h_ext[here:]
    one_width = inner + both + LANES
    riding = small_mesh() and SMALL == rows
    one_sum = Scatter(
        [[([(h_own, d_main, 0), (h_side, d_side, 0)], one_width)]],
        two_sum.got,
        small=small.astype(bf16) if riding else None,
    )
    two_sum.second()
    after = [*ffn_end.along, one_sum.own] if one_sum.staged else []
    two_end = Finish([two_sum], after)
    one_end = Finish([one_sum], [*ffn_end.along, *two_sum.near], small=riding)

    d_h_part, d_tail = hidden_back(
        d_two, d_main, d_side, w_two, w_one,
        [one_sum.got[0], *ffn_end.sends] if one_sum.staged else [],
    )
    d_tail = shifted(d_tail, "ctx", -1).astype(f32)
    d_tail = jnp.pad(d_tail.reshape(seqs, TAIL, features), ((0, 0), (block - TAIL, 0), (0, 0)))
    d_h = pair_sum(d_h_part + d_tail.reshape(here, features))
    scaled = d_h * gain_a
    d_hidden = (
        d_resid
        + r_one * scaled
        - x_own * (r_one * r_one * r_one) * jnp.mean(x_own * scaled, axis=-1, keepdims=True)
    )
    d_hidden = d_hidden.astype(bf16).reshape(seqs, block, features)

    (ffn_grads,) = ffn_end.results()
    (two_grads,) = two_end.results()
    (one_grads,) = one_end.results()
    ffn_gate, ffn_up = ffn_grads[:, :units], ffn_grads[:, units + half : 2 * units + half]
    ffn_down = jnp.concatenate(
        [ffn_grads[:, units : units + half], ffn_grads[:, 2 * units + half :]], axis=1
    )
    small = one_end.small if riding else sum_all(small, ("dp", "ctx"))
    taps_bc_at, heads_at = small_rows(inner, both)

    def taps_of(tile):
        parts = tile.reshape(-1, KC, LANES)
        return jnp.concatenate([parts[j] for j in range(parts.shape[0])], axis=1)

    g_tx, g_tb = taps_of(small[:taps_bc_at]), small[taps_bc_at:heads_at]
    g_decay, g_bias, g_skip = [small[heads_at + i, :heads] for i in range(3)]

    def row_dots(weights, grads):
        return jnp.sum(weights.astype(f32) * grads, axis=1, keepdims=True)

    two_width = columns + inner
    gain_a_sum = (
        row_dots(first_pack[:, : inner + both + heads], one_grads[:, : inner + both + heads])
        + row_dots(w_qkv[:, 0, :], two_grads[:, :columns])
        + row_dots(w_zx[:, 0, :], two_grads[:, columns:two_width])
    )
    gain_f_sum = row_dots(w_gu[:, 0, :], ffn_gate) + row_dots(w_gu[:, 1, :], ffn_up)
    over_cores = sum_all(
        jnp.concatenate(
            [
                jnp.pad(g_tb, ((0, 0), (0, both + 2 - LANES))),
                jnp.concatenate(
                    [one_grads[:, inner : inner + both], gain_a_sum, gain_f_sum], axis=1
                ),
            ],
            axis=0,
        ),
        ("tp",),
    )
    g_tb, over_cores = taps_of(over_cores[: g_tb.shape[0], :LANES]), over_cores[g_tb.shape[0] :]
    bc_grad = over_cores[:, :both]
    g_gain_a = over_cores[:, both] / gain_attn.astype(f32)
    g_gain_f = over_cores[:, both + 1] / gain_ffn.astype(f32)
    zx_grad = jnp.stack(
        [two_grads[:, columns : columns + inner], one_grads[:, :inner]], axis=1
    )
    return (
        block_out,
        d_hidden,
        g_gain_a,
        two_grads[:, None, :columns],
        two_grads[:, columns + inner : columns + inner + qwidth].T,
        zx_grad,
        bc_grad,
        one_grads[:, inner + both : inner + both + heads],
        g_tx,
        g_tb,
        g_decay,
        g_bias,
        g_skip,
        two_grads[:, columns + inner + qwidth :].T,
        g_gain_f,
        jnp.stack([ffn_gate, ffn_up], axis=1),
        ffn_down.T,
    )


def solution(mesh):
    in_specs = (
        P("dp", "ctx", None),
        P("dp", "ctx"),
        P(("dp", "ctx")),
        P(("dp", "ctx"), "tp", None),
        P("tp", ("dp", "ctx")),
        P(("dp", "ctx"), None, "tp"),
        P(("dp", "ctx"), None),
        P(("dp", "ctx"), "tp"),
        P(None, "tp"),
        P(),
        P("tp"),
        P("tp"),
        P("tp"),
        P("tp", ("dp", "ctx")),
        P(("dp", "ctx")),
        P(("dp", "ctx"), None, "tp"),
        P("tp", ("dp", "ctx")),
        P("dp", "ctx", None),
    )
    out_specs = (
        P("dp", "ctx", None),
        P("dp", "ctx", None),
        P(("dp", "ctx")),
        P(("dp", "ctx"), "tp", None),
        P("tp", ("dp", "ctx")),
        P(("dp", "ctx"), None, "tp"),
        P(("dp", "ctx"), None),
        P(("dp", "ctx"), "tp"),
        P(None, "tp"),
        P(),
        P("tp"),
        P("tp"),
        P("tp"),
        P("tp", ("dp", "ctx")),
        P(("dp", "ctx")),
        P(("dp", "ctx"), None, "tp"),
        P("tp", ("dp", "ctx")),
    )
    return jax.shard_map(
        per_device, mesh=mesh, in_specs=in_specs, out_specs=out_specs, check_vma=False
    )
```

```python
import functools

import jax
import jax.numpy as jnp
from jax import lax
from jax.experimental import pallas as pl
from jax.experimental.pallas import tpu as pltpu
from jax.sharding import PartitionSpec as P

HD = 64
KC = 4
TAIL = 16
LANES = 128
VMEM_LIMIT = 56 * 1024 * 1024
SMALL = 64

f32 = jnp.float32
bf16 = jnp.bfloat16
highest = lax.Precision.HIGHEST
rope_base = 100000000000.0


def small_mesh():
    return lax.axis_size("dp") == 4 and lax.axis_size("ctx") == 4


def swap(value, axis, bits):
    count = lax.axis_size(axis)
    return lax.ppermute(value, axis, [(i, i ^ bits) for i in range(count)])


def shifted(value, axis, distance):
    count = lax.axis_size(axis)
    route = [(i - distance, i) for i in range(count) if 0 <= i - distance < count]
    return lax.ppermute(value, axis, route)


def place_blocks(pieces, outs, copies):
    count = len(pieces)
    total = len(outs)
    where = jnp.stack([lax.axis_index("dp"), lax.axis_index("ctx")]).astype(jnp.int32)

    def kernel(where_ref, *refs):
        ins = refs[:count]
        outputs = refs[count : count + total]
        sems = refs[count + total]
        running = []
        for number, (piece, first, width, out, axis, bits, to) in enumerate(copies):
            target = outputs[out]
            if axis is None:
                target = target.at[:, pl.ds(to, width)]
            else:
                target = target.at[jnp.bitwise_xor(where_ref[axis], bits), :, pl.ds(to, width)]
            copy = pltpu.make_async_copy(
                ins[piece].at[:, pl.ds(first, width)], target, sems.at[number]
            )
            copy.start()
            running.append(copy)
        for copy in running:
            copy.wait()

    return pl.pallas_call(
        kernel,
        out_shape=[jax.ShapeDtypeStruct(shape, pieces[0].dtype) for shape in outs],
        in_specs=[pl.BlockSpec(memory_space=pltpu.SMEM)]
        + [pl.BlockSpec(memory_space=pl.ANY)] * count,
        out_specs=[pl.BlockSpec(memory_space=pltpu.VMEM)] * total,
        scratch_shapes=[pltpu.SemaphoreType.DMA((len(copies),))],
        compiler_params=pltpu.CompilerParams(vmem_limit_bytes=VMEM_LIMIT),
        cost_estimate=cost(1),
        name="place_blocks",
    )(where, *pieces)


class Placing:
    def __init__(self):
        self.pieces, self.outs, self.copies = [], [], []

    def out(self, *shape):
        self.outs.append(shape)
        return len(self.outs) - 1

    def add(self, piece, out, axis=None, bits=0, to=0, first=0, width=None):
        for number, known in enumerate(self.pieces):
            if known is piece:
                break
        else:
            number = len(self.pieces)
            self.pieces.append(piece)
        width = piece.shape[1] if width is None else width
        self.copies.append((number, first, width, out, axis, bits, to))

    def after(self, *arrays):
        self.pieces.extend(arrays)

    def run(self):
        return place_blocks(self.pieces, self.outs, self.copies)


def along_ctx(packed):
    return [packed] + [swap(packed, "ctx", k) for k in (1, 2, 3)]


def along_dp(held, one, two):
    near = swap(held, "dp", one)
    return [(0, held), (one, near), (two, swap(held, "dp", two)), (3, swap(near, "dp", two))]


def gather_all(first, second, third, with_first):
    rows = first.shape[0]
    if not small_mesh():
        def whole(piece):
            return lax.all_gather(piece, ("dp", "ctx"), axis=0, tiled=True)

        w_two, w_three = [whole(jnp.concatenate(p, axis=1)) for p in second]
        w_four, w_five = [
            whole(
                jnp.concatenate(
                    [p for p, out, _ in sorted(third[0] + third[1], key=lambda t: t[2]) if out == o],
                    axis=1,
                )
            )
            for o in (0, 1)
        ]
        return with_first(whole(first)), w_two, w_three, w_four, w_five, []

    def flat(held):
        return held.reshape(held.shape[0] * held.shape[1], held.shape[2])

    wide_one = first.shape[1]
    wide_two = [sum(p.shape[1] for p in part) for part in second]
    wide_half = [sum(p.shape[1] for p, _, _ in half) for half in third]
    work = Placing()
    held_out = work.out(4, rows, wide_one)
    pack_out = work.out(rows, sum(wide_two))
    for k, piece in enumerate(along_ctx(first)):
        work.add(piece, held_out, 1, k)
    to = 0
    for piece in second[0] + second[1]:
        work.add(piece, pack_out, to=to)
        to += piece.shape[1]
    held_one, packed_two = work.run()
    held_one = flat(held_one)
    work = Placing()
    full = work.out(4, 4 * rows, wide_one)
    held_out = [work.out(4, rows, w) for w in wide_two]
    pack_out = work.out(rows, sum(wide_half))
    for k in range(4):
        work.add(held_one if k == 0 else swap(held_one, "dp", k), full, 0, k)
    for k, piece in enumerate(along_ctx(packed_two)):
        work.add(piece, held_out[0], 1, k, width=wide_two[0])
        work.add(piece, held_out[1], 1, k, first=wide_two[0], width=wide_two[1])
    to = 0
    for piece, _, _ in third[0] + third[1]:
        work.add(piece, pack_out, to=to)
        to += piece.shape[1]
    w_one, held_a, held_b, packed_three = work.run()
    made = with_first(flat(w_one))
    work = Placing()
    fulls = [work.out(4, 4 * rows, w) for w in wide_two]
    held_out = [work.out(4, rows, w) for w in wide_half]
    for bits, piece in along_dp(flat(held_a), 1, 2):
        work.add(piece, fulls[0], 0, bits)
    for bits, piece in along_dp(flat(held_b), 2, 1):
        work.add(piece, fulls[1], 0, bits)
    for k, piece in enumerate(along_ctx(packed_three)):
        work.add(piece, held_out[0], 1, k, width=wide_half[0])
        work.add(piece, held_out[1], 1, k, first=wide_half[0], width=wide_half[1])
    work.after(made[-1])
    w_two, w_three, held_a, held_b = work.run()
    work = Placing()
    ends = [0, 0]
    for part in third[0] + third[1]:
        ends[part[1]] += part[0].shape[1]
    fulls = [work.out(4, 4 * rows, w) for w in ends]
    nears = []
    for half, held, order in ((third[0], held_a, (1, 2)), (third[1], held_b, (2, 1))):
        blocks = along_dp(flat(held), *order)
        nears += [piece for _, piece in blocks[1:]]
        for bits, piece in blocks:
            column = 0
            for part, out, to in half:
                work.add(piece, fulls[out], 0, bits, to=to, first=column, width=part.shape[1])
                column += part.shape[1]
    w_four, w_five = work.run()
    return made, flat(w_two), flat(w_three), flat(w_four), flat(w_five), nears


def pick(value, index, axis):
    return lax.dynamic_index_in_dim(value, index, axis, keepdims=False)


def split_sum(groups, place, after, small=False):
    counts = [len(g) for g in groups]
    widths = [g[0].shape[1] for g in groups]
    rows = groups[0][-1].shape[0] // 4
    arrays = [a for g in groups for a in g]
    total = sum(counts)

    def kernel(place_ref, *refs):
        outs, held = refs[-5:-1], refs[-1]
        number, to = 0, 0
        for count, width in zip(counts, widths):
            for quarter in range(4):
                part = pl.ds(quarter * rows, rows)
                parts = [ref[part, :].astype(f32) for ref in refs[number : number + count]]
                if count == 4:
                    value = (parts[0] + parts[1]) + (parts[2] + parts[3])
                else:
                    value = sum(parts[1:], parts[0])
                held[quarter, :, to : to + width] = value
            number += count
            to += width
        if small:
            end = slice(to - LANES, to)
            for quarter in range(4):
                held[quarter, :, end] = held[0, :, end].astype(bf16).astype(f32)
        for k, out in enumerate(outs):
            out[...] = held[jnp.bitwise_xor(place_ref[0], k)].astype(out.dtype)

    shape = (rows, sum(widths))
    return pl.pallas_call(
        kernel,
        out_shape=[jax.ShapeDtypeStruct(shape, bf16 if k else f32) for k in range(4)],
        in_specs=[pl.BlockSpec(memory_space=pltpu.SMEM)]
        + [pl.BlockSpec(memory_space=pltpu.VMEM)] * total
        + [pl.BlockSpec(memory_space=pl.ANY)] * len(after),
        out_specs=[pl.BlockSpec(memory_space=pltpu.VMEM)] * 4,
        scratch_shapes=[pltpu.VMEM((4, *shape), f32)],
        compiler_params=pltpu.CompilerParams(vmem_limit_bytes=VMEM_LIMIT),
        cost_estimate=cost(1),
        name="split_sum",
    )(place.reshape(1), *arrays, *after)


def tn(a, b):
    return lax.dot_general(a, b, (((0,), (0,)), ((), ())), preferred_element_type=f32)


def grad_blocks(groups, outputs, place, after, small=None):
    arrays = []

    def index_of(array):
        for number, known in enumerate(arrays):
            if known is array:
                return number
        arrays.append(array)
        return len(arrays) - 1

    plan = [
        [([(index_of(l), index_of(r), first) for l, r, first in terms], width) for terms, width in segments]
        for segments in groups
    ]
    rows = groups[0][0][0][0][0].shape[1] // 4
    if small is not None:
        arrays.append(small)
    count = len(arrays)

    def kernel(place_ref, *refs):
        outs = refs[count + len(after) :]
        for (group, offsets), out in zip(outputs, outs):
            for number, bits in enumerate(offsets):
                first_row = pl.multiple_of(jnp.bitwise_xor(place_ref[0], bits) * rows, rows)
                to = 0
                for terms, width in plan[group]:
                    value = None
                    for l, r, first in terms:
                        part = tn(
                            refs[l][:, pl.ds(first_row, rows)], refs[r][:, first : first + width]
                        )
                        value = part if value is None else value + part
                    out[number * rows : (number + 1) * rows, to : to + width] = value.astype(bf16)
                    to += width
                if small is not None:
                    end = small.shape[0]
                    out[number * rows : number * rows + end, to:] = refs[count - 1][...]
                    out[number * rows + end : (number + 1) * rows, to:] = jnp.zeros(
                        (rows - end, LANES), bf16
                    )

    more = 0 if small is None else LANES
    widths = [sum(width for _, width in segments) + more for segments in groups]
    return pl.pallas_call(
        kernel,
        out_shape=[
            jax.ShapeDtypeStruct((len(offsets) * rows, widths[group]), bf16)
            for group, offsets in outputs
        ],
        in_specs=[pl.BlockSpec(memory_space=pltpu.SMEM)]
        + [pl.BlockSpec(memory_space=pltpu.VMEM)] * count
        + [pl.BlockSpec(memory_space=pl.ANY)] * len(after),
        out_specs=[pl.BlockSpec(memory_space=pltpu.VMEM)] * len(outputs),
        compiler_params=pltpu.CompilerParams(vmem_limit_bytes=VMEM_LIMIT),
        cost_estimate=cost(1),
        name="grad_blocks",
    )(place.reshape(1), *arrays, *after)


class Scatter:
    def __init__(self, groups, after=(), small=None):
        self.groups = groups
        self.staged = small_mesh()
        self.widths = [sum(width for _, width in segments) for segments in groups]
        self.got, self.near, self.kept = [], [], []
        if not self.staged:
            return
        dp = lax.axis_index("dp")
        if len(groups) == 1:
            self.own, *sends = grad_blocks(
                groups, [(0, (k,)) for k in range(4)], dp, after, small
            )
            self.got = [swap(send, "dp", k) for k, send in enumerate(sends, start=1)]
            return
        self.rows = groups[0][0][0][0][0].shape[1] // 4
        outputs = [(0, (2, 3)), (1, (1, 3)), (0, (0, 1)), (1, (0, 2))]
        send_a, send_b, *self.kept = grad_blocks(groups, outputs, dp, after)
        self.got = [swap(send_a, "dp", 2), swap(send_b, "dp", 1)]

    def second(self, after=()):
        if not self.staged or len(self.groups) == 1:
            return
        rows, after = self.rows, list(after)

        def kernel(kept_a, kept_b, got_a, got_b, *refs):
            for kept, got, out in ((kept_a, got_a, refs[-2]), (kept_b, got_b, refs[-1])):
                out[...] = (kept[...].astype(f32) + got[...].astype(f32)).astype(bf16)

        arrays = [*self.kept, *self.got]
        self.sends = pl.pallas_call(
            kernel,
            grid=(1,),
            out_shape=[jax.ShapeDtypeStruct((rows, width), bf16) for width in self.widths],
            in_specs=[pl.BlockSpec((rows, a.shape[1]), lambda i: (1, 0)) for a in arrays]
            + [spec_any()] * len(after),
            out_specs=[pl.BlockSpec((rows, width), lambda i: (0, 0)) for width in self.widths],
            compiler_params=params(),
            cost_estimate=cost(2),
            name="second_add",
        )(*arrays, *after)
        self.near = [swap(send, "dp", bits) for send, bits in zip(self.sends, (1, 2))]

    def addends(self):
        if len(self.groups) == 1:
            return [[self.own, *self.got]]
        return [[self.kept[n], self.got[n], self.near[n]] for n in range(2)]


class Finish:
    def __init__(self, sums, after=(), small=False):
        self.sums = sums
        self.staged = small_mesh()
        self.sends, self.along = [], []
        if not self.staged:
            return
        groups = [g for one in sums for g in one.addends()]
        self.own, *self.sends = split_sum(groups, lax.axis_index("ctx"), after, small)
        self.along = [swap(send, "ctx", k) for k, send in enumerate(self.sends, start=1)]

    def results(self):
        if not self.staged:
            out = []
            for one in self.sums:
                parts = [
                    sum(tn(l, r[:, first : first + width]) for l, r, first in terms).astype(bf16)
                    for segments in one.groups
                    for terms, width in segments
                ]
                joined = jnp.concatenate(parts, axis=1)
                out.append(
                    lax.psum_scatter(
                        joined, ("dp", "ctx"), scatter_dimension=0, tiled=True
                    ).astype(f32)
                )
            return out
        one, two, three = [piece.astype(f32) for piece in self.along]
        total = (self.own + one) + (two + three)
        out, first = [], 0
        for one in self.sums:
            out.append(total[:, first : first + sum(one.widths)])
            first += sum(one.widths)
        self.small = total[:, first:]
        return out


def sum_all(value, axes):
    for axis in axes:
        count = lax.axis_size(axis)
        if count & (count - 1):
            value = lax.psum(value, axis)
            continue
        bits = 1
        while bits < count:
            value = value + swap(value, axis, bits)
            bits *= 2
    return value


def pair_sum(value):
    if lax.axis_size("tp") != 2:
        return lax.psum(value.astype(bf16), "tp").astype(f32)
    low = value.astype(bf16)
    return low.astype(f32) + swap(low, "tp", 1).astype(f32)


def chain_pieces(pack, reverse):
    count, me = lax.axis_size("ctx"), lax.axis_index("ctx")
    states = pack.shape[1] - TAIL
    if 2 < count <= 4:
        sign = -1 if reverse else 1
        near = shifted(pack, "ctx", sign)
        two = pack[:, :states].astype(f32) + pack[:, states : states + 1].astype(f32) * near[
            :, :states
        ].astype(f32)
        two = two.astype(bf16)
        return [near, shifted(two, "ctx", 2 * sign)], [two]
    everything = lax.all_gather(pack, "ctx")

    def hop(k, before):
        at = count - 1 - k if reverse else k
        reached = at > me if reverse else at < me
        there = pick(everything, at, 0).astype(f32)
        new = there[:, states : states + 1] * before + there[:, :states]
        return jnp.where(reached, new, before)

    start = jnp.zeros((pack.shape[0], states, pack.shape[2]), f32)
    total = lax.fori_loop(0, count, hop, start).astype(bf16)
    return [jnp.pad(total, ((0, 0), (0, TAIL), (0, 0)))], []


def dot(a, b):
    return jnp.dot(a, b, preferred_element_type=f32)


def dot_nt(a, b):
    return lax.dot_general(a, b, (((1,), (1,)), ((), ())), preferred_element_type=f32)


def sig(v):
    return 1.0 / (1.0 + jnp.exp(-v))


def conv_pre(joined, span, taps, pos, count):
    total = None
    for k in range(KC):
        piece = joined[TAIL - k : TAIL - k + count, span]
        term = taps[k : k + 1, :] * piece
        if k:
            term = term * (pos >= k).astype(f32)
        total = term if total is None else total + term
    return total


def lane_ids(shape):
    return lax.broadcasted_iota(jnp.int32, shape, 1)


def decay_parts(dtr, head_row, pos, heads):
    count = dtr.shape[0]
    lane = lane_ids(dtr.shape)
    pre = dtr + head_row[1:2, :]
    dt = jnp.where(lane < heads, jnp.maximum(pre, 0.0) + jnp.log(1.0 + jnp.exp(-jnp.abs(pre))), 0.0)
    la = -jnp.exp(head_row[0:1, :]) * dt
    marked = jnp.where(lane == LANES - 1, (pos == 0).astype(f32), la)
    row = lax.broadcasted_iota(jnp.int32, (count, count), 0)
    col = lax.broadcasted_iota(jnp.int32, (count, count), 1)
    lower = (row >= col).astype(f32)
    summed = jnp.dot(lower, marked, precision=highest, preferred_element_type=f32)
    return pre, dt, la, summed


def wide(value, lane):
    return jnp.broadcast_to(value[:, lane : lane + 1], (value.shape[0], LANES))


def pair(value, j, low_half):
    return jnp.where(low_half, wide(value, 2 * j), wide(value, 2 * j + 1))


def spec_whole(a):
    return pl.BlockSpec(a.shape, lambda s: (0,) * a.ndim)


def spec_rows(a, rows, base=0):
    return pl.BlockSpec((rows, a.shape[1]), lambda s: (base + s, 0))


def spec_seq(a):
    return pl.BlockSpec((1,) + a.shape[1:], lambda s: (s,) + (0,) * (a.ndim - 1))


def spec_any():
    return pl.BlockSpec(memory_space=pl.ANY)


def params():
    return pltpu.CompilerParams(vmem_limit_bytes=VMEM_LIMIT)


def cost(microseconds):
    return pl.CostEstimate(
        flops=int(microseconds * 1e8), bytes_accessed=int(microseconds * 3e5), transcendentals=0
    )


def chained_state(pieces, span, states):
    total, factor = None, None
    for piece in pieces:
        there = piece[0, :states, span].astype(f32)
        total = there if total is None else total + factor * there
        if piece is not pieces[-1]:
            decay = piece[0, states : states + 1, span].astype(f32)
            factor = decay if factor is None else factor * decay
    return total


def mixer_local_kernel(
    heads, inner, both, proj_ref, tail_ref, tx_ref, tb_ref, hr_ref, pos_ref,
    y_ref, pack_ref, c_ref, l_ref, jx, jb,
):
    count = proj_ref.shape[0]
    states = both // 2
    pos = pos_ref[...]
    head_row = hr_ref[...]
    jx[0:TAIL, :] = tail_ref[:, :inner]
    jx[TAIL : TAIL + count, :] = proj_ref[:, :inner]
    jb[0:TAIL, :] = tail_ref[:, inner : inner + both]
    jb[TAIL : TAIL + count, :] = proj_ref[:, inner : inner + both]
    pre_b = conv_pre(jb, slice(0, both), tb_ref[...], pos, count)
    bc = pre_b * sig(pre_b)
    b_low = bc[:, :states].astype(bf16)
    c_low = bc[:, states:].astype(bf16)
    c_ref[...] = c_low
    bt_low = jnp.transpose(bc[:, :states]).astype(bf16)
    _, dt, _, summed = decay_parts(proj_ref[:, inner + both :], head_row, pos, heads)
    l_ref[...] = summed
    rows = jnp.transpose(summed)
    row = lax.broadcasted_iota(jnp.int32, (count, count), 0)
    col = lax.broadcasted_iota(jnp.int32, (count, count), 1)
    marks = summed[:, LANES - 1 : LANES]
    valid = (row >= col) & (marks == rows[LANES - 1 : LANES, :])
    scores = dot_nt(c_low, b_low)
    last = summed[count - 1 : count, :]
    same = (marks == last[:, LANES - 1 : LANES]).astype(f32)
    carry = jnp.exp(last) * (last[:, LANES - 1 : LANES] == 0.0).astype(f32)
    low_half = lane_ids((count, LANES)) < HD
    low_row = low_half[0:1, :]
    for j in range(heads // 2):
        span = slice(j * LANES, (j + 1) * LANES)
        pre = conv_pre(jx, span, tx_ref[:, span], pos, count)
        xc = pre * sig(pre)
        u = xc * pair(dt, j, low_half)
        u_low = u.astype(bf16)
        results = []
        for h in (2 * j, 2 * j + 1):
            differ = summed[:, h : h + 1] - rows[h : h + 1, :]
            mixing = jnp.exp(jnp.where(valid, differ, -1e30)) * scores
            results.append(dot(mixing.astype(bf16), u_low))
        skip = pair(head_row[2:3, :], j, low_row)
        y_ref[:, span] = jnp.where(low_half, results[0], results[1]) + skip * xc
        left = jnp.exp(pair(last, j, low_row) - pair(summed, j, low_half)) * same
        pack_ref[0, :states, span] = dot(bt_low, (left * u).astype(bf16)).astype(bf16)
        pack_ref[0, states:, span] = jnp.broadcast_to(pair(carry, j, low_row), (TAIL, LANES)).astype(bf16)


def mixer_local(proj, taps_x, taps_bc, head_row, pos, heads, seqs, count):
    inner, both = taps_x.shape[1], taps_bc.shape[1]
    states = both // 2
    outs = [
        jax.ShapeDtypeStruct((seqs * count, inner), f32),
        jax.ShapeDtypeStruct((seqs, states + TAIL, inner), bf16),
        jax.ShapeDtypeStruct((seqs * count, states), bf16),
        jax.ShapeDtypeStruct((seqs * count, LANES), f32),
    ]
    return pl.pallas_call(
        functools.partial(mixer_local_kernel, heads, inner, both),
        grid=(seqs,),
        out_shape=outs,
        in_specs=[
            spec_rows(proj, count),
            spec_rows(proj, TAIL, seqs * count // TAIL),
            spec_whole(taps_x), spec_whole(taps_bc), spec_whole(head_row), spec_rows(pos, count),
        ],
        out_specs=[
            spec_rows(outs[0], count), spec_seq(outs[1]), spec_rows(outs[2], count),
            spec_rows(outs[3], count),
        ],
        scratch_shapes=[
            pltpu.VMEM((count + TAIL, inner), f32),
            pltpu.VMEM((count + TAIL, both), f32),
        ],
        compiler_params=params(),
        cost_estimate=cost(8),
        name="mixer_local",
    )(proj, proj, taps_x, taps_bc, head_row, pos)


def mixer_read_kernel(
    heads, pieces, first, y0_ref, c_ref, l_ref, qz_ref, att_ref, *refs
):
    packs = refs[:pieces]
    y_ref, out_ref, state_ref = refs[-3:]
    count = y0_ref.shape[0]
    states = c_ref.shape[1]
    qwidth = att_ref.shape[1]
    summed = l_ref[...]
    alive = (summed[:, LANES - 1 : LANES] == 0.0).astype(f32)
    low_half = lane_ids((count, LANES)) < HD
    out_ref[:, :qwidth] = att_ref[...]
    for j in range(heads // 2):
        span = slice(j * LANES, (j + 1) * LANES)
        state = chained_state(packs, span, states).astype(bf16)
        state_ref[0, :, span] = state
        reads = jnp.exp(pair(summed, j, low_half)) * alive
        y = y0_ref[:, span] + reads * dot(c_ref[...], state)
        y_ref[:, span] = y
        gate = qz_ref[:, first + j * LANES : first + (j + 1) * LANES]
        out_ref[:, qwidth + j * LANES : qwidth + (j + 1) * LANES] = (y * gate * sig(gate)).astype(bf16)


def mixer_read(y_local, c_vec, summed, qz, att, packs, extra, heads, seqs, count, first):
    inner, states = y_local.shape[1], c_vec.shape[1]
    outs = [
        jax.ShapeDtypeStruct((seqs * count, inner), f32),
        jax.ShapeDtypeStruct((seqs * count, att.shape[1] + inner), bf16),
        jax.ShapeDtypeStruct((seqs, states, inner), bf16),
    ]
    args = (y_local, c_vec, summed, qz, att)
    return pl.pallas_call(
        functools.partial(mixer_read_kernel, heads, len(packs), first),
        grid=(seqs,),
        out_shape=outs,
        in_specs=[spec_rows(a, count) for a in args]
        + [spec_seq(p) for p in packs]
        + [spec_any()] * len(extra),
        out_specs=[spec_rows(outs[0], count), spec_rows(outs[1], count), spec_seq(outs[2])],
        compiler_params=params(),
        cost_estimate=cost(4),
        name="mixer_read",
    )(*args, *packs, *extra)


def gate_back_kernel(
    heads, first, qwidth, d_ref, y_ref, qz_ref, c_ref, l_ref,
    dy_ref, dz_ref, datt_ref, pack_ref,
):
    count = y_ref.shape[0]
    states = c_ref.shape[1]
    summed = l_ref[...]
    alive = (summed[:, LANES - 1 : LANES] == 0.0).astype(f32)
    last = summed[count - 1 : count, :]
    carry = jnp.exp(last) * (last[:, LANES - 1 : LANES] == 0.0).astype(f32)
    low_half = lane_ids((count, LANES)) < HD
    low_row = low_half[0:1, :]
    ct_low = jnp.transpose(c_ref[...].astype(f32)).astype(bf16)
    datt_ref[...] = d_ref[:, :qwidth].astype(bf16)
    for j in range(heads // 2):
        span = slice(j * LANES, (j + 1) * LANES)
        gate = qz_ref[:, first + j * LANES : first + (j + 1) * LANES]
        d_gated = d_ref[:, qwidth + j * LANES : qwidth + (j + 1) * LANES]
        sg = sig(gate)
        dy = d_gated * (gate * sg)
        dy_ref[:, span] = dy
        dz_ref[:, span] = (
            d_gated * y_ref[:, span] * (sg * (1.0 + gate * (1.0 - sg)))
        ).astype(bf16)
        reads = jnp.exp(pair(summed, j, low_half)) * alive
        pack_ref[0, :states, span] = dot(ct_low, (reads * dy).astype(bf16)).astype(bf16)
        pack_ref[0, states:, span] = jnp.broadcast_to(pair(carry, j, low_row), (TAIL, LANES)).astype(bf16)


def gate_back(d_mixer, y, qz, c_vec, summed, heads, seqs, count, first, qwidth):
    inner, states = y.shape[1], c_vec.shape[1]
    outs = [
        jax.ShapeDtypeStruct((seqs * count, inner), f32),
        jax.ShapeDtypeStruct((seqs * count, inner), bf16),
        jax.ShapeDtypeStruct((seqs * count, qwidth), bf16),
        jax.ShapeDtypeStruct((seqs, states + TAIL, inner), bf16),
    ]
    args = (d_mixer, y, qz, c_vec, summed)
    return pl.pallas_call(
        functools.partial(gate_back_kernel, heads, first, qwidth),
        grid=(seqs,),
        out_shape=outs,
        in_specs=[spec_rows(a, count) for a in args],
        out_specs=[spec_rows(o, count) for o in outs[:3]] + [spec_seq(outs[3])],
        compiler_params=params(),
        cost_estimate=cost(5),
        name="gate_back",
    )(*args)


def small_rows(inner, both):
    taps_bc_at = inner // LANES * KC
    return taps_bc_at, taps_bc_at + both // LANES * KC


def mixer_back_kernel(
    heads, inner, both, pieces, extra, proj_ref, tail_ref, tx_ref, tb_ref, hr_ref, pos_ref,
    dy_ref, y_ref, st_ref, *refs
):
    packs = refs[:pieces]
    main_ref, side_ref, small_ref, jx, jb, ax, ab = refs[pieces + extra :]
    small_ref[...] = jnp.zeros_like(small_ref)
    taps_bc_at, heads_at = small_rows(inner, both)
    count = proj_ref.shape[0]
    states = both // 2
    pos = pos_ref[...]
    head_row = hr_ref[...]
    jx[0:TAIL, :] = tail_ref[:, :inner]
    jx[TAIL : TAIL + count, :] = proj_ref[:, :inner]
    jb[0:TAIL, :] = tail_ref[:, inner : inner + both]
    jb[TAIL : TAIL + count, :] = proj_ref[:, inner : inner + both]
    pre_b = conv_pre(jb, slice(0, both), tb_ref[...], pos, count)
    sig_b = sig(pre_b)
    bc = pre_b * sig_b
    b_low = bc[:, :states].astype(bf16)
    c_low = bc[:, states:].astype(bf16)
    pre_dt, dt, la, summed = decay_parts(proj_ref[:, inner + both :], head_row, pos, heads)
    rows = jnp.transpose(summed)
    row = lax.broadcasted_iota(jnp.int32, (count, count), 0)
    col = lax.broadcasted_iota(jnp.int32, (count, count), 1)
    marks = summed[:, LANES - 1 : LANES]
    valid = (row <= col) & (marks == rows[LANES - 1 : LANES, :])
    scores = dot_nt(b_low, c_low)
    last = summed[count - 1 : count, :]
    carry = jnp.exp(last) * (last[:, LANES - 1 : LANES] == 0.0).astype(f32)
    same = (marks == last[:, LANES - 1 : LANES]).astype(f32)
    first = (marks == 0.0).astype(f32)
    low_half = lane_ids((count, LANES)) < HD
    low_row = low_half[0:1, :]
    lane = lane_ids((LANES, LANES))
    lane_row = lax.broadcasted_iota(jnp.int32, (LANES, LANES), 0)
    d_scores = jnp.zeros((count, count), f32)
    d_b = jnp.zeros((count, states), f32)
    d_c = jnp.zeros((count, states), f32)
    d_sum = jnp.zeros((count, LANES), f32)
    d_dt = jnp.zeros((count, LANES), f32)
    d_rows = jnp.zeros((8, LANES), f32)
    ax[...] = jnp.zeros_like(ax)
    ab[...] = jnp.zeros_like(ab)
    for j in range(heads // 2):
        span = slice(j * LANES, (j + 1) * LANES)
        taps = tx_ref[:, span]
        pre = conv_pre(jx, span, taps, pos, count)
        sg = sig(pre)
        xc = pre * sg
        dt_wide = pair(dt, j, low_half)
        u = xc * dt_wide
        u_low = u.astype(bf16)
        dy = dy_ref[:, span]
        dy_low = dy.astype(bf16)
        state = st_ref[0, :, span]
        later = chained_state(packs, span, states)
        d_state = later.astype(bf16)
        results = []
        for i, h in enumerate((2 * j, 2 * j + 1)):
            differ = rows[h : h + 1, :] - summed[:, h : h + 1]
            decay = jnp.exp(jnp.where(valid, differ, -1e30))
            half = low_half if i == 0 else jnp.logical_not(low_half)
            u_half = jnp.where(half, u, 0.0).astype(bf16)
            d_scores = d_scores + decay * dot_nt(u_half, dy_low)
            results.append(dot((decay * scores).astype(bf16), dy_low))
        left = jnp.exp(pair(last, j, low_row) - pair(summed, j, low_half)) * same
        reads = jnp.exp(pair(summed, j, low_half)) * first
        du_end = left * dot(b_low, d_state)
        du_in = jnp.where(low_half, results[0], results[1])
        du = du_in + du_end
        d_c = d_c + dot_nt((reads * dy).astype(bf16), state)
        d_b = d_b + dot_nt((left * u).astype(bf16), d_state)
        skip = pair(head_row[2:3, :], j, low_row)
        chosen = (
            ((lane == 2 * j) & (lane_row < HD)) | ((lane == 2 * j + 1) & (lane_row >= HD))
        ).astype(f32)
        per_token = (
            dy_low.astype(f32) * (y_ref[:, span] - skip * xc)
            - u_low.astype(f32) * du_in
            - u * du_end
        )
        d_sum = d_sum + jnp.dot(per_token, chosen, precision=highest, preferred_element_type=f32)
        d_dt = d_dt + jnp.dot(du * xc, chosen, precision=highest, preferred_element_type=f32)
        sums = jnp.concatenate(
            [
                jnp.sum(u * du_end, axis=0, keepdims=True),
                jnp.sum(dy * xc, axis=0, keepdims=True),
                jnp.sum(later * state.astype(f32), axis=0, keepdims=True),
                jnp.zeros((5, LANES), f32),
            ],
            axis=0,
        )
        d_rows = d_rows + jnp.dot(sums, chosen, precision=highest, preferred_element_type=f32)
        d_pre = (du * dt_wide + skip * dy) * (sg * (1.0 + pre * (1.0 - sg)))
        for k in range(KC):
            masked = d_pre * (pos >= k).astype(f32) if k else d_pre
            small_ref[0, j * KC + k : j * KC + k + 1, :] = jnp.sum(
                masked * jx[TAIL - k : TAIL - k + count, span], axis=0, keepdims=True
            )
            ax[TAIL - k : TAIL - k + count, span] += taps[k : k + 1, :] * masked
    main_ref[:, :inner] = ax[TAIL:, :].astype(bf16)
    side_ref[:, :inner] = ax[:TAIL, :].astype(bf16)
    d_b = d_b + dot(d_scores.astype(bf16), c_low)
    d_c = d_c + dot(jnp.transpose(d_scores).astype(bf16), b_low)
    d_pre = jnp.concatenate([d_b, d_c], axis=1) * (sig_b * (1.0 + pre_b * (1.0 - sig_b)))
    for k in range(KC):
        masked = d_pre * (pos >= k).astype(f32) if k else d_pre
        sums = jnp.sum(masked * jb[TAIL - k : TAIL - k + count, :], axis=0, keepdims=True)
        for g in range(both // LANES):
            at = taps_bc_at + g * KC + k
            small_ref[0, at : at + 1, :] = sums[:, g * LANES : (g + 1) * LANES]
        ab[TAIL - k : TAIL - k + count, :] += tb_ref[k : k + 1, :] * masked
    main_ref[:, inner : inner + both] = ab[TAIL:, :].astype(bf16)
    side_ref[:, inner : inner + both] = ab[:TAIL, :].astype(bf16)
    token = lax.broadcasted_iota(jnp.int32, (count, LANES), 0)
    at_last = d_rows[0:1, :] + d_rows[2:3, :] * carry
    d_sum = d_sum + jnp.where(token == count - 1, at_last, 0.0)
    upper = (row <= col).astype(f32)
    d_la = jnp.dot(upper, d_sum, precision=highest, preferred_element_type=f32)
    d_la = jnp.where(lane_ids(d_la.shape) < heads, d_la, 0.0)
    d_dt = d_dt - jnp.exp(head_row[0:1, :]) * d_la
    d_dtr = d_dt * sig(pre_dt)
    d_dtr = jnp.where(lane_ids(d_dtr.shape) < heads, d_dtr, 0.0)
    main_ref[:, inner + both :] = d_dtr.astype(bf16)
    side_ref[:, inner + both :] = jnp.zeros((TAIL, LANES), bf16)
    small_ref[0, heads_at : heads_at + 1, :] = jnp.sum(d_la * la, axis=0, keepdims=True)
    small_ref[0, heads_at + 1 : heads_at + 2, :] = jnp.sum(d_dtr, axis=0, keepdims=True)
    small_ref[0, heads_at + 2 : heads_at + 3, :] = d_rows[1:2, :]


def mixer_back(
    number, made, proj, taps_x, taps_bc, head_row, pos, dy, y, state, packs, extra, heads, seqs, count
):
    inner, both = taps_x.shape[1], taps_bc.shape[1]
    width = proj.shape[1]
    outs = [
        jax.ShapeDtypeStruct((seqs * count, width), bf16),
        jax.ShapeDtypeStruct((seqs * TAIL, width), bf16),
        jax.ShapeDtypeStruct((1, SMALL, LANES), f32),
    ]

    def rows_of(a, rows, block):
        return pl.BlockSpec((rows, a.shape[1]), lambda i: (block, 0))

    def seq_of(a):
        return pl.BlockSpec((1,) + a.shape[1:], lambda i: (number,) + (0,) * (a.ndim - 1))

    extra = list(made) + list(extra)
    first = 9 + len(packs)
    return pl.pallas_call(
        functools.partial(mixer_back_kernel, heads, inner, both, len(packs), len(extra)),
        grid=(1,),
        out_shape=outs,
        in_specs=[
            rows_of(proj, count, number),
            rows_of(proj, TAIL, seqs * count // TAIL + number),
            spec_whole(taps_x), spec_whole(taps_bc), spec_whole(head_row),
            rows_of(pos, count, number), rows_of(dy, count, number), rows_of(y, count, number),
            seq_of(state),
        ]
        + [seq_of(p) for p in packs]
        + [spec_any()] * len(extra),
        out_specs=[rows_of(outs[0], count, number), rows_of(outs[1], TAIL, number)]
        + [spec_seq(o) for o in outs[2:]],
        scratch_shapes=[
            pltpu.VMEM((count + TAIL, inner), f32),
            pltpu.VMEM((count + TAIL, both), f32),
            pltpu.VMEM((count + TAIL, inner), f32),
            pltpu.VMEM((count + TAIL, both), f32),
        ],
        input_output_aliases={first: 0, first + 1: 1} if made else {},
        compiler_params=params(),
        cost_estimate=cost(9),
        name="mixer_back",
    )(proj, proj, taps_x, taps_bc, head_row, pos, dy, y, state, *packs, *extra)


def hidden_back_kernel(two_ref, main_ref, side_ref, w_two_ref, w_one_ref, *refs):
    out_ref, tail_ref = refs[-2:]
    half = two_ref.shape[0] // 2
    for part in (slice(0, half), slice(half, 2 * half)):
        out_ref[part, :] = dot_nt(two_ref[part, :], w_two_ref[...]) + dot_nt(
            main_ref[part, :], w_one_ref[...]
        )
    tail_ref[...] = dot_nt(side_ref[...], w_one_ref[...]).astype(bf16)


def hidden_back(d_two, d_main, d_side, w_two, w_one, after):
    args = (d_two, d_main, d_side, w_two, w_one)
    features = w_one.shape[0]
    return pl.pallas_call(
        hidden_back_kernel,
        out_shape=[
            jax.ShapeDtypeStruct((d_two.shape[0], features), f32),
            jax.ShapeDtypeStruct((d_side.shape[0], features), bf16),
        ],
        in_specs=[pl.BlockSpec(memory_space=pltpu.VMEM)] * len(args) + [spec_any()] * len(after),
        out_specs=[pl.BlockSpec(memory_space=pltpu.VMEM)] * 2,
        compiler_params=params(),
        cost_estimate=cost(5),
        name="hidden_back",
    )(*args, *after)


def half_turned(v):
    first = lane_ids(v.shape) % HD < HD // 2
    return jnp.where(
        first, -pltpu.roll(v, LANES - HD // 2, 1), pltpu.roll(v, HD // 2, 1)
    )


def rope_kernel(qwidth, qz_ref, cos_ref, sin_ref, q_ref, kv_ref):
    cosine, sine = cos_ref[...], sin_ref[...]
    for j in range(qwidth // LANES):
        v = qz_ref[:, j * LANES : (j + 1) * LANES]
        q_ref[:, j * LANES : (j + 1) * LANES] = (v * cosine + half_turned(v) * sine).astype(bf16)
    v = qz_ref[:, qwidth : qwidth + LANES]
    turned = v * cosine + half_turned(v) * sine
    kv_ref[...] = jnp.where(lane_ids(v.shape) < HD, turned, v).astype(bf16)


def rope(qz, cosine, sine, qwidth, seqs, count):
    outs = [
        jax.ShapeDtypeStruct((seqs * count, qwidth), bf16),
        jax.ShapeDtypeStruct((seqs * count, 2 * HD), bf16),
    ]
    return pl.pallas_call(
        functools.partial(rope_kernel, qwidth),
        grid=(seqs,),
        out_shape=outs,
        in_specs=[
            pl.BlockSpec((count, qwidth + LANES), lambda s: (s, 0)),
            spec_rows(cosine, count), spec_rows(sine, count),
        ],
        out_specs=[spec_rows(o, count) for o in outs],
        compiler_params=params(),
        cost_estimate=cost(2),
        name="rope",
    )(qz, cosine, sine)


def to_low(v, r, low_half):
    v = v.astype(f32)
    return jnp.where(low_half, v if r % 2 == 0 else pltpu.roll(v, HD, 1), 0.0)


def to_high(v, r, low_half):
    v = v.astype(f32)
    return jnp.where(low_half, 0.0, v if r % 2 else pltpu.roll(v, HD, 1))


def key_masks(pos, count, blocks):
    row = lax.broadcasted_iota(jnp.int32, (count, count), 0)
    col = lax.broadcasted_iota(jnp.int32, (count, count), 1)
    start = row - pos
    masks = []
    for d in range(blocks):
        mask = col - d * count >= start
        masks.append(mask & (col <= row) if d == 0 else mask)
    return masks


def attend_kernel(per_group, blocks, q_ref, pos_ref, *refs):
    kv = refs[:blocks]
    o_ref, lse_ref = refs[blocks:]
    count = q_ref.shape[0]
    masks = key_masks(pos_ref[...], count, blocks)
    low_half = lane_ids((count, LANES)) < HD
    lane = lane_ids((count, LANES))
    lse = jnp.zeros((count, LANES), f32)
    halves = []
    for r in range(per_group):
        span = slice(r // 2 * LANES, (r // 2 + 1) * LANES)
        q = to_low(q_ref[:, span], r, low_half).astype(bf16)
        scores = [
            jnp.where(masks[d], dot_nt(q, kv[d][...]) * 0.125, -1e30) for d in range(blocks)
        ]
        top = jnp.max(scores[0], axis=1, keepdims=True)
        for d in range(1, blocks):
            top = jnp.maximum(top, jnp.max(scores[d], axis=1, keepdims=True))
        weights = [jnp.exp(v - top) for v in scores]
        total = jnp.sum(weights[0], axis=1, keepdims=True)
        for d in range(1, blocks):
            total = total + jnp.sum(weights[d], axis=1, keepdims=True)
        scale = 1.0 / total
        out = dot((weights[0] * scale).astype(bf16), kv[0][...])
        for d in range(1, blocks):
            out = out + dot((weights[d] * scale).astype(bf16), kv[d][...])
        lse = jnp.where(lane == r, top + jnp.log(total), lse)
        halves.append(out)
        if r % 2:
            o_ref[:, span] = jnp.where(low_half, pltpu.roll(halves[r - 1], HD, 1), out).astype(bf16)
    lse_ref[...] = lse


def attend(q, pos, kv, seqs, count):
    per_group = q.shape[1] // HD
    outs = [
        jax.ShapeDtypeStruct(q.shape, bf16),
        jax.ShapeDtypeStruct((q.shape[0], LANES), f32),
    ]
    return pl.pallas_call(
        functools.partial(attend_kernel, per_group, len(kv)),
        grid=(seqs,),
        out_shape=outs,
        in_specs=[spec_rows(a, count) for a in (q, pos, *kv)],
        out_specs=[spec_rows(o, count) for o in outs],
        compiler_params=params(),
        cost_estimate=cost(8),
        name="attend",
    )(q, pos, *kv)


def attend_back_kernel(per_group, blocks, q_ref, pos_ref, do_ref, lse_ref, cos_ref, sin_ref, *refs):
    kv = refs[:blocks]
    dq_ref = refs[blocks]
    dkv = refs[blocks + 1 :]
    count = q_ref.shape[0]
    masks = key_masks(pos_ref[...], count, blocks)
    low_half = lane_ids((count, LANES)) < HD
    cosine, sine = cos_ref[...], sin_ref[...]
    totals = [jnp.zeros((LANES, count), f32) for _ in range(blocks)]
    halves = []
    for r in range(per_group):
        span = slice(r // 2 * LANES, (r // 2 + 1) * LANES)
        q = to_low(q_ref[:, span], r, low_half)
        do = to_high(do_ref[:, span], r, low_half)
        q_turned = (jnp.transpose(q) * 0.125).astype(bf16)
        do_turned = jnp.transpose(do).astype(bf16)
        q, do = q.astype(bf16), do.astype(bf16)
        lse = lse_ref[:, r : r + 1]
        probs, d_probs = [], []
        row_dot = None
        for d in range(blocks):
            scores = jnp.where(masks[d], dot_nt(q, kv[d][...]) * 0.125, -1e30)
            probs.append(jnp.exp(scores - lse))
            d_probs.append(dot_nt(do, kv[d][...]))
            part = jnp.sum(probs[d] * d_probs[d], axis=1, keepdims=True)
            row_dot = part if row_dot is None else row_dot + part
        dq = None
        for d in range(blocks):
            d_scores = (probs[d] * (d_probs[d] - row_dot)).astype(bf16)
            part = dot(d_scores, kv[d][...])
            dq = part if dq is None else dq + part
            totals[d] = (
                totals[d] + dot(q_turned, d_scores) + dot(do_turned, probs[d].astype(bf16))
            )
        halves.append(dq * 0.125)
        if r % 2:
            both = jnp.where(low_half, halves[r - 1], pltpu.roll(halves[r], HD, 1))
            dq_ref[:, span] = (both * cosine - half_turned(both) * sine).astype(bf16)
    for d in range(blocks):
        dkv[d][...] = jnp.transpose(totals[d]).astype(dkv[d].dtype)


def attend_back(q, pos, d_out, lse, cosine, sine, kv, seqs, count):
    per_group = q.shape[1] // HD
    outs = [jax.ShapeDtypeStruct(q.shape, bf16)] + [
        jax.ShapeDtypeStruct(kv[0].shape, bf16 if d else f32) for d in range(len(kv))
    ]
    args = (q, pos, d_out, lse, cosine, sine, *kv)
    return pl.pallas_call(
        functools.partial(attend_back_kernel, per_group, len(kv)),
        grid=(seqs,),
        out_shape=outs,
        in_specs=[spec_rows(a, count) for a in args],
        out_specs=[spec_rows(o, count) for o in outs],
        compiler_params=params(),
        cost_estimate=cost(14),
        name="attend_back",
    )(*args)


def join_back_kernel(pieces, dq_ref, dz_ref, cos_ref, sin_ref, *refs):
    out_ref = refs[-1]
    qwidth = dq_ref.shape[1]
    total = refs[0][...].astype(f32)
    for piece in refs[1:pieces]:
        total = total + piece[...].astype(f32)
    turned = total * cos_ref[...] - half_turned(total) * sin_ref[...]
    out_ref[:, :qwidth] = dq_ref[...]
    out_ref[:, qwidth : qwidth + LANES] = jnp.where(
        lane_ids(total.shape) < HD, turned, total
    ).astype(bf16)
    out_ref[:, qwidth + LANES :] = dz_ref[...]


def join_back(dq, dz, cosine, sine, pieces, extra, seqs, count):
    out = jax.ShapeDtypeStruct((dq.shape[0], dq.shape[1] + LANES + dz.shape[1]), bf16)
    args = (dq, dz, cosine, sine, *pieces)
    return pl.pallas_call(
        functools.partial(join_back_kernel, len(pieces)),
        grid=(seqs,),
        out_shape=out,
        in_specs=[spec_rows(a, count) for a in args] + [spec_any()] * len(extra),
        out_specs=spec_rows(out, count),
        compiler_params=params(),
        cost_estimate=cost(2),
        name="join_back",
    )(*args, *extra)


def attend_one(q, k, v, mask):
    scores = jnp.einsum("qrd,kd->rqk", q, k, preferred_element_type=f32) * 0.125
    scores = jnp.where(mask[None], scores, -1e30)
    top = jnp.max(scores, axis=-1, keepdims=True)
    weights = jnp.where(mask[None], jnp.exp(scores - top), 0.0)
    total = jnp.sum(weights, axis=-1, keepdims=True)
    out = jnp.einsum("rqk,kd->qrd", (weights / total).astype(bf16), v, preferred_element_type=f32)
    return out, jnp.transpose((top + jnp.log(total))[..., 0])


def attend_one_back(q, k, v, mask, d_out, lse):
    scores = jnp.einsum("qrd,kd->rqk", q, k, preferred_element_type=f32) * 0.125
    probs = jnp.where(mask[None], jnp.exp(scores - jnp.transpose(lse)[..., None]), 0.0)
    d_probs = jnp.einsum("qrd,kd->rqk", d_out, v, preferred_element_type=f32)
    row_dot = jnp.sum(probs * d_probs, axis=-1, keepdims=True)
    d_scores = (probs * (d_probs - row_dot)).astype(bf16)
    d_q = jnp.einsum("rqk,kd->qrd", d_scores, k, preferred_element_type=f32) * 0.125
    d_k = jnp.einsum("rqk,qrd->kd", d_scores, q, preferred_element_type=f32) * 0.125
    d_v = jnp.einsum("rqk,qrd->kd", probs.astype(bf16), d_out, preferred_element_type=f32)
    return d_q, jnp.concatenate([d_k, d_v], axis=-1)


class Attention:
    def __init__(self, q, kv, pos, seqs, count):
        self.q, self.pos, self.seqs, self.count = q, pos, seqs, count
        self.blocks = lax.axis_size("ctx")
        self.few = self.blocks <= 4
        if self.few:
            self.kv = [kv] + [shifted(kv, "ctx", d) for d in range(1, self.blocks)]
            return
        me = lax.axis_index("ctx")
        shaped = lax.all_gather(kv.reshape(seqs, count, -1), "ctx", axis=1, tiled=True)
        self.all_kv = shaped
        keys = jnp.arange(shaped.shape[1])
        tokens = me * count + jnp.arange(count)
        starts = tokens[None, :] - pos.reshape(seqs, count)
        self.mask = (keys[None, None, :] <= tokens[None, :, None]) & (
            keys[None, None, :] >= starts[:, :, None]
        )

    def heads_of(self, v):
        return v.reshape(self.seqs, self.count, -1, HD)

    def forward(self):
        if self.few:
            out, self.lse = attend(self.q, self.pos, self.kv, self.seqs, self.count)
            return out
        keys, values = self.all_kv[..., :HD], self.all_kv[..., HD:]
        out, self.lse = lax.map(
            lambda a: attend_one(*a), (self.heads_of(self.q), keys, values, self.mask)
        )
        return out.astype(bf16).reshape(self.q.shape)

    def backward(self, d_out, cosine, sine):
        if self.few:
            dq, own, *rest = attend_back(
                self.q, self.pos, d_out, self.lse, cosine, sine, self.kv, self.seqs, self.count
            )
            return dq, [own] + [
                shifted(piece, "ctx", -d) for d, piece in enumerate(rest, start=1)
            ]
        keys, values = self.all_kv[..., :HD], self.all_kv[..., HD:]
        dq, kept = lax.map(
            lambda a: attend_one_back(*a),
            (self.heads_of(self.q), keys, values, self.mask, self.heads_of(d_out), self.lse),
        )
        dq = dq.reshape(self.q.shape)
        cos_q = jnp.tile(cosine, (1, dq.shape[1] // LANES))
        sin_q = jnp.tile(sine, (1, dq.shape[1] // LANES))
        dq = dq * cos_q - jnp.dot(dq, turn_matrix(dq.shape[1]), precision=highest) * sin_q
        total = lax.psum_scatter(kept.astype(bf16), "ctx", scatter_dimension=1, tiled=True)
        return dq.astype(bf16), [total.astype(f32).reshape(-1, 2 * HD)]


def turn_matrix(columns):
    source = jnp.arange(columns)[:, None]
    target = jnp.arange(columns)[None, :]
    half = HD // 2
    low = target % HD < half
    minus = low & (source == target + half)
    plus = jnp.logical_not(low) & (source == target - half)
    return plus.astype(f32) - minus.astype(f32)


def per_device(
    hidden_in,
    positions,
    gain_attn,
    w_qkv,
    w_attn_out,
    w_zx,
    w_bc,
    w_dt,
    conv_x,
    conv_bc,
    a_log,
    dt_bias,
    d_skip,
    w_mamba_out,
    gain_ffn,
    w_gu,
    w_down,
    output_cotangent,
):
    seqs, block = positions.shape
    features = hidden_in.shape[2]
    rows = w_qkv.shape[0]
    heads = a_log.shape[0]
    inner = w_zx.shape[2]
    both = w_bc.shape[1]
    columns = w_qkv.shape[2]
    qwidth = columns - 2 * HD
    units = w_gu.shape[2]
    count = lax.axis_size("ctx")
    place = lax.axis_index("ctx")
    here = seqs * block

    pad = jnp.zeros((rows, LANES - heads - 2), bf16)
    first_pack = jnp.concatenate(
        [w_zx[:, 1, :], w_bc, w_dt, gain_attn[:, None], gain_ffn[:, None], pad], axis=1
    )
    tail = shifted(hidden_in[:, block - TAIL :, :], "ctx", 1)
    down = w_down.T
    half = units // 2
    pos = positions.reshape(here, 1)
    frequency = jnp.power(jnp.float32(rope_base), -jnp.arange(0, HD, 2).astype(f32) / HD)
    turned = pos.astype(f32) * jnp.tile(frequency, 2 * LANES // HD)
    cosine, sine = jnp.cos(turned), jnp.sin(turned)

    x_own = hidden_in.reshape(here, features).astype(f32)
    x_ext = jnp.concatenate([x_own, tail.reshape(seqs * TAIL, features).astype(f32)], axis=0)
    r_ext = lax.rsqrt(jnp.mean(x_ext * x_ext, axis=-1, keepdims=True) + 1e-05)
    r_one = r_ext[:here]
    taps_x = conv_x.astype(f32)
    taps_bc = conv_bc.astype(f32)
    head_row = jnp.pad(
        jnp.stack([a_log, dt_bias, d_skip]), ((0, 5), (0, LANES - heads))
    )

    def with_first(w_one):
        gain_a = w_one[:, inner + both + heads].astype(f32)
        h_ext = (x_ext * r_ext * gain_a).astype(bf16)
        proj = dot(h_ext, w_one)
        local = mixer_local(proj, taps_x, taps_bc, head_row, pos, heads, seqs, block)
        return w_one, gain_a, h_ext, proj, local, local[1]

    made, w_two, w_three, w_four, w_five, nears = gather_all(
        first_pack,
        ([w_qkv[:, 0, :], w_zx[:, 0, :]], [w_attn_out.T, w_mamba_out.T]),
        (
            [(w_gu[:, 0, :], 0, 0), (down[:, :half], 1, 0)],
            [(w_gu[:, 1, :], 0, units), (down[:, half:], 1, half)],
        ),
        with_first,
    )
    w_one, gain_a, h_ext, proj, (y_local, pack, c_vec, summed), _ = made
    gain_f = w_one[:, inner + both + heads + 1].astype(f32)
    h_own = h_ext[:here]
    packs, _ = chain_pieces(pack, False)

    qz = dot(h_own, w_two)
    q_low, kv_low = rope(qz, cosine, sine, qwidth, seqs, block)
    attention = Attention(q_low, kv_low, pos, seqs, block)
    attended = attention.forward()

    y, mixer_out, state = mixer_read(
        y_local, c_vec, summed, qz, attended, packs, nears, heads, seqs, block, columns
    )
    resid = x_own + pair_sum(dot_nt(mixer_out, w_three))

    r_two = lax.rsqrt(jnp.mean(resid * resid, axis=-1, keepdims=True) + 1e-05)
    h_two = (resid * r_two * gain_f).astype(bf16)
    gate_up = dot(h_two, w_four)
    gate_ff, up_ff = gate_up[:, :units], gate_up[:, units:]
    sig_ff = jax.nn.sigmoid(gate_ff)
    silu_ff = gate_ff * sig_ff
    hidden_state = (silu_ff * up_ff).astype(bf16)
    ffn = pair_sum(dot_nt(hidden_state, w_five))
    block_out = (resid + ffn).astype(bf16).reshape(seqs, block, features)

    e_low = output_cotangent.reshape(here, features)
    d_hidden_state = dot(e_low, w_five)
    d_gate_up = jnp.concatenate(
        [
            d_hidden_state * up_ff * (sig_ff * (1.0 + gate_ff * (1.0 - sig_ff))),
            d_hidden_state * silu_ff,
        ],
        axis=1,
    ).astype(bf16)

    d_h_two_part = dot_nt(d_gate_up, w_four).astype(bf16)
    d_h_two = pair_sum(d_h_two_part)
    ffn_sum = Scatter(
        [
            [([(h_two, d_gate_up, 0)], units), ([(e_low, hidden_state, 0)], half)],
            [([(h_two, d_gate_up, units)], units), ([(e_low, hidden_state, half)], half)],
        ]
    )
    scaled = d_h_two * gain_f
    d_resid = (
        e_low.astype(f32)
        + r_two * scaled
        - resid * (r_two * r_two * r_two) * jnp.mean(resid * scaled, axis=-1, keepdims=True)
    )
    d_mix = d_resid.astype(bf16)

    d_mixer = dot(d_mix, w_three)
    d_y, d_z, d_att, d_pack = gate_back(
        d_mixer, y, qz, c_vec, summed, heads, seqs, block, columns, qwidth
    )
    later_packs, ready = chain_pieces(d_pack, True)
    d_q, d_kv = attention.backward(d_att, cosine, sine)
    ffn_sum.second([d_q])
    early = [*ready, *ffn_sum.sends] if ffn_sum.staged else []
    d_two = join_back(d_q, d_z, cosine, sine, d_kv, early, seqs, block)
    two_sum = Scatter(
        [
            [([(h_own, d_two, 0)], columns + inner)],
            [([(d_mix, mixer_out, 0)], qwidth + inner)],
        ]
    )
    ffn_end = Finish([ffn_sum])
    d_main, d_side, small = None, None, None
    for number in range(seqs):
        extra = []
        if number == 0:
            extra = two_sum.kept
        d_main, d_side, more = mixer_back(
            number, (d_main, d_side) if number else (), proj, taps_x, taps_bc, head_row, pos,
            d_y, y, state, later_packs, extra, heads, seqs, block,
        )
        small = more[0] if small is None else small + more[0]
    h_side = h_ext[here:]
    one_width = inner + both + LANES
    riding = small_mesh() and SMALL == rows
    one_sum = Scatter(
        [[([(h_own, d_main, 0), (h_side, d_side, 0)], one_width)]],
        two_sum.got,
        small=small.astype(bf16) if riding else None,
    )
    two_sum.second()
    after = [*ffn_end.along, one_sum.own] if one_sum.staged else []
    two_end = Finish([two_sum], after)
    one_end = Finish([one_sum], [*ffn_end.along, *two_sum.near], small=riding)

    d_h_part, d_tail = hidden_back(
        d_two, d_main, d_side, w_two, w_one,
        [one_sum.got[0], *ffn_end.sends] if one_sum.staged else [],
    )
    d_tail = shifted(d_tail, "ctx", -1).astype(f32)
    d_tail = jnp.pad(d_tail.reshape(seqs, TAIL, features), ((0, 0), (block - TAIL, 0), (0, 0)))
    d_h = pair_sum(d_h_part + d_tail.reshape(here, features))
    scaled = d_h * gain_a
    d_hidden = (
        d_resid
        + r_one * scaled
        - x_own * (r_one * r_one * r_one) * jnp.mean(x_own * scaled, axis=-1, keepdims=True)
    )
    d_hidden = d_hidden.astype(bf16).reshape(seqs, block, features)

    (ffn_grads,) = ffn_end.results()
    (two_grads,) = two_end.results()
    (one_grads,) = one_end.results()
    ffn_gate, ffn_up = ffn_grads[:, :units], ffn_grads[:, units + half : 2 * units + half]
    ffn_down = jnp.concatenate(
        [ffn_grads[:, units : units + half], ffn_grads[:, 2 * units + half :]], axis=1
    )
    small = one_end.small if riding else sum_all(small, ("dp", "ctx"))
    taps_bc_at, heads_at = small_rows(inner, both)

    def taps_of(tile):
        parts = tile.reshape(-1, KC, LANES)
        return jnp.concatenate([parts[j] for j in range(parts.shape[0])], axis=1)

    g_tx, g_tb = taps_of(small[:taps_bc_at]), small[taps_bc_at:heads_at]
    g_decay, g_bias, g_skip = [small[heads_at + i, :heads] for i in range(3)]

    def row_dots(weights, grads):
        return jnp.sum(weights.astype(f32) * grads, axis=1, keepdims=True)

    two_width = columns + inner
    gain_a_sum = (
        row_dots(first_pack[:, : inner + both + heads], one_grads[:, : inner + both + heads])
        + row_dots(w_qkv[:, 0, :], two_grads[:, :columns])
        + row_dots(w_zx[:, 0, :], two_grads[:, columns:two_width])
    )
    gain_f_sum = row_dots(w_gu[:, 0, :], ffn_gate) + row_dots(w_gu[:, 1, :], ffn_up)
    over_cores = sum_all(
        jnp.concatenate(
            [
                jnp.pad(g_tb, ((0, 0), (0, both + 2 - LANES))),
                jnp.concatenate(
                    [one_grads[:, inner : inner + both], gain_a_sum, gain_f_sum], axis=1
                ),
            ],
            axis=0,
        ),
        ("tp",),
    )
    g_tb, over_cores = taps_of(over_cores[: g_tb.shape[0], :LANES]), over_cores[g_tb.shape[0] :]
    bc_grad = over_cores[:, :both]
    g_gain_a = over_cores[:, both] / gain_attn.astype(f32)
    g_gain_f = over_cores[:, both + 1] / gain_ffn.astype(f32)
    zx_grad = jnp.stack(
        [two_grads[:, columns : columns + inner], one_grads[:, :inner]], axis=1
    )
    return (
        block_out,
        d_hidden,
        g_gain_a,
        two_grads[:, None, :columns],
        two_grads[:, columns + inner : columns + inner + qwidth].T,
        zx_grad,
        bc_grad,
        one_grads[:, inner + both : inner + both + heads],
        g_tx,
        g_tb,
        g_decay,
        g_bias,
        g_skip,
        two_grads[:, columns + inner + qwidth :].T,
        g_gain_f,
        jnp.stack([ffn_gate, ffn_up], axis=1),
        ffn_down.T,
    )


def solution(mesh):
    in_specs = (
        P("dp", "ctx", None),
        P("dp", "ctx"),
        P(("dp", "ctx")),
        P(("dp", "ctx"), "tp", None),
        P("tp", ("dp", "ctx")),
        P(("dp", "ctx"), None, "tp"),
        P(("dp", "ctx"), None),
        P(("dp", "ctx"), "tp"),
        P(None, "tp"),
        P(),
        P("tp"),
        P("tp"),
        P("tp"),
        P("tp", ("dp", "ctx")),
        P(("dp", "ctx")),
        P(("dp", "ctx"), None, "tp"),
        P("tp", ("dp", "ctx")),
        P("dp", "ctx", None),
    )
    out_specs = (
        P("dp", "ctx", None),
        P("dp", "ctx", None),
        P(("dp", "ctx")),
        P(("dp", "ctx"), "tp", None),
        P("tp", ("dp", "ctx")),
        P(("dp", "ctx"), None, "tp"),
        P(("dp", "ctx"), None),
        P(("dp", "ctx"), "tp"),
        P(None, "tp"),
        P(),
        P("tp"),
        P("tp"),
        P("tp"),
        P("tp", ("dp", "ctx")),
        P(("dp", "ctx")),
        P(("dp", "ctx"), None, "tp"),
        P("tp", ("dp", "ctx")),
    )
    return jax.shard_map(
        per_device, mesh=mesh, in_specs=in_specs, out_specs=out_specs, check_vma=False
    )
```
